32 devices in a mesh: bx: 8 (over z, x), by: 4 (over y, core).
Axes of the slice: x: 2, y: 2, z: 4, core: 2. Of those that a mesh axis runs over, the one named last changes fastest.
Arguments:
- scalar_field: float32 [64, 256, 512], P(None, 'bx', 'by'), may hold values from -8 to 8
- transfer_in: bfloat16 [16, 8], replicated, may hold values from -2 to 2
- transfer_out: bfloat16 [16, 16], replicated, may hold values from -1.5 to 1.5
Outputs:
- view_x: float32 [2, 8, 64, 512], P(None, None, 'bx', 'by')
- view_y: float32 [2, 8, 64, 256], P(None, None, 'by', 'bx')
The draws below stay inside these ranges and needn't reach their ends.
All inputs are finite; a program needn't handle non-finite values.
Results may differ from the reference program's by a relative error of at most 0.00035.
Values sent between devices are 32-bit elements; how exact they have to be, the bound alone decides.
No kernel may reach another device: no remote copies, remote signals or barrier semaphores. Data moves between devices by JAX's collectives and lax.ppermute only.
A program may use at most 64 MiB of HBM per device.

```python
import jax
import jax.numpy as jnp
from jax import lax

BANDS = 8
HID = 16
FEAT = 8
NZ = 64
NX = 256
NY = 512


def draw_scalar_field(key, part):
    key_cells, key_stripes, key_columns = jax.random.split(key, 3)
    grains = jnp.clip(jax.random.normal(key_cells, (NZ, NX, NY), jnp.float32), -2.5, 2.5)
    stripes = jnp.clip(jax.random.normal(key_stripes, (NZ, 1, NY), jnp.float32), -2.5, 2.5)
    columns = jnp.clip(jax.random.normal(key_columns, (NZ, NX, 1), jnp.float32), -2.5, 2.5)
    return 0.6 * grains + stripes + columns


def centred(key, shape, width, reach, held_as=jnp.bfloat16):
    return jnp.clip(width * jax.random.normal(key, shape, jnp.float32), -reach, reach).astype(held_as)


def setup_inputs(seed: int = 0) -> dict:
    streams_of = jax.random.split(jax.random.key(seed), 4)
    return {
        "scalar_field": draw_scalar_field(jax.random.fold_in(streams_of[3], 71), 0),
        "transfer_in": centred(streams_of[1], (HID, FEAT), FEAT ** -0.5, 2.0),
        "transfer_out": centred(streams_of[2], (2 * BANDS, HID), HID ** -0.5, 1.5),
    }


def smooth(values):
    padded = jnp.pad(values, 1)
    nearby = padded[2:, 1:-1, 1:-1] + padded[:-2, 1:-1, 1:-1]
    nearby = nearby + padded[1:-1, 2:, 1:-1] + padded[1:-1, :-2, 1:-1]
    nearby = nearby + padded[1:-1, 1:-1, 2:] + padded[1:-1, 1:-1, :-2]
    return 0.4 * values + 0.1 * nearby

def gradients(padded):
    diff_x = padded[:, 2:, :] - padded[:, :-2, :]
    grad_x = (2.0 * diff_x[1:-1, :, 1:-1] + diff_x[:-2, :, 1:-1] + diff_x[2:, :, 1:-1] + diff_x[1:-1, :, :-2] + diff_x[1:-1, :, 2:]) / 12.0
    diff_y = padded[:, :, 2:] - padded[:, :, :-2]
    grad_y = (2.0 * diff_y[1:-1, 1:-1] + diff_y[:-2, 1:-1] + diff_y[2:, 1:-1] + diff_y[1:-1, :-2] + diff_y[1:-1, 2:]) / 12.0
    diff_z = padded[2:] - padded[:-2]
    grad_z = (2.0 * diff_z[:, 1:-1, 1:-1] + diff_z[:, :-2, 1:-1] + diff_z[:, 2:, 1:-1] + diff_z[:, 1:-1, :-2] + diff_z[:, 1:-1, 2:]) / 12.0
    return (padded[1:-1, 1:-1, 1:-1], grad_x, grad_y, grad_z)

def transfer(padded, transfer_in, transfer_out):
    centre, grad_x, grad_y, grad_z = gradients(padded)
    scaled_x = 4.0 * grad_x
    scaled_y = 4.0 * grad_y
    scaled_z = 4.0 * grad_z
    magnitude = jnp.sqrt(1.0 + scaled_x * scaled_x + scaled_y * scaled_y + scaled_z * scaled_z)
    features = jnp.stack([centre, scaled_x, scaled_y, scaled_z, magnitude, centre * magnitude, centre * centre, jnp.ones_like(centre)]).astype(jnp.bfloat16)
    hidden = jax.nn.silu(jnp.einsum('hf,fzxy->hzxy', transfer_in.astype(jnp.float32), features.astype(jnp.float32))).astype(jnp.bfloat16)
    channels = jnp.einsum('ch,hzxy->czxy', transfer_out.astype(jnp.float32), hidden.astype(jnp.float32))
    return (jax.nn.softplus(channels[:BANDS]), jax.nn.softplus(channels[BANDS:]))

def reference(scalar_field, transfer_in, transfer_out):
    smoothed = smooth(smooth(scalar_field))
    padded = jnp.pad(smoothed, 1)
    planes = 8
    step_x = 2.0 / NX
    step_y = 2.0 / NY

    def advance(carried, index):
        colour, optical = carried
        window = lax.dynamic_slice_in_dim(padded, (index * planes).astype(jnp.int32), planes + 2, 1)
        emission, absorption = transfer(window, transfer_in, transfer_out)
        thickness = absorption * step_x
        running = jnp.cumsum(thickness, axis=2)
        visible = jnp.exp(-(optical[:, :, None, :] + running - thickness))
        colour = colour + lax.optimization_barrier(jnp.sum(visible * -jnp.expm1(-thickness) * emission, axis=2))
        optical = optical + running[:, :, -1, :]
        thickness_y = absorption * step_y
        running_y = jnp.cumsum(thickness_y, axis=3)
        colour_y = lax.optimization_barrier(jnp.sum(jnp.exp(-(running_y - thickness_y)) * -jnp.expm1(-thickness_y) * emission, axis=3))
        clear_y = jnp.exp(-running_y[..., -1])
        return ((colour, optical), jnp.stack([colour_y, clear_y]))
    blank = jnp.zeros((BANDS, NZ, NY), jnp.float32)
    (colour, optical), images = lax.scan(advance, (blank, blank), jnp.arange(NX // planes, dtype=jnp.int32))
    view_x = jnp.stack([colour, jnp.exp(-optical)])
    view_y = jnp.transpose(images, (1, 2, 3, 0, 4)).reshape(2, BANDS, NZ, NX)
    return (view_x, view_y)
```

```python
import functools

import jax
import jax.numpy as jnp
from jax import lax
from jax.experimental import pallas as pl
from jax.experimental.pallas import tpu as pltpu
from jax.sharding import PartitionSpec as P

F32 = jnp.float32
LOG2E = 1.4426950408889634
SUB = 8
LANES = 128
REACH = 3
VMEM = pl.BlockSpec(memory_space=pltpu.VMEM)
PARAMS = pltpu.CompilerParams(vmem_limit_bytes=48 * 1024 * 1024)


def strips_kernel(field_ref, low_ref, high_ref):
    length = field_ref.shape[1]
    for k in range(REACH):
        low_ref[k] = field_ref[:, k, :]
        high_ref[k] = field_ref[:, length - REACH + k, :]


def turn_kernel(field_ref, before_ref, after_ref, out_ref, first_ref, last_ref):
    layers, length, width = field_ref.shape
    half = length // 2

    def row(x):
        if x < 0:
            return before_ref[x + REACH]
        if x >= length:
            return after_ref[x - length]
        return field_ref[:, x, :]

    for k in range(half + 2 * REACH):
        x = k - REACH
        turned = jnp.concatenate([row(x), row(x + half)], axis=0).T
        out_ref[k] = turned
        for j in range(REACH):
            first_ref[j, k : k + 1] = turned[j : j + 1]
            last_ref[j, k : k + 1] = turned[width - REACH + j : width - REACH + j + 1]


def over_sublanes(colour, clear):
    for shift in (1, 2, 4):
        rolled_c = pltpu.roll(colour, SUB - shift, axis=0)
        rolled_q = pltpu.roll(clear, SUB - shift, axis=0)
        colour = colour + clear * rolled_c
        clear = clear * rolled_q
    return colour, clear


def march_kernel(
    spans,
    flags,
    steps,
    bands,
    turned_ref,
    before_ref,
    after_ref,
    win_ref,
    wout_ref,
    image_x_ref,
    image_y_ref,
    raw_ref,
    once_ref,
    twice_ref,
    ridge_ref,
    tx_ref,
    cx_ref,
    ty_ref,
    cy_ref,
    rows_ref,
    rows_y_ref,
):
    wide_x, width, _ = turned_ref.shape
    half = wide_x - 2 * REACH
    run = width // SUB
    hidden_units = win_ref.shape[0] // 16
    layers = LANES // 2
    lane = lax.broadcasted_iota(jnp.int32, (SUB, LANES), 1)
    chunk = lax.broadcasted_iota(jnp.int32, (SUB, LANES), 0)
    z = lane % layers
    near = (z > 0).astype(F32)
    far = (z < layers - 1).astype(F32)
    at_x, at_y = lax.axis_index("bx"), lax.axis_index("by")
    count_x, count_y = flags
    mask_x_low = jnp.where((lane < layers) & (at_x == 0), 0.0, 1.0)
    mask_x_high = jnp.where((lane >= layers) & (at_x == count_x - 1), 0.0, 1.0)
    mask_y_low = jnp.where((chunk == 0) & (at_y == 0), 0.0, 1.0)
    mask_y_high = jnp.where((chunk == SUB - 1) & (at_y == count_y - 1), 0.0, 1.0)

    def z_sum(value):
        return pltpu.roll(value, 1, axis=1) * near + pltpu.roll(value, LANES - 1, axis=1) * far

    def fill(k, _):
        raw_ref[k, REACH : REACH + width] = turned_ref[k]
        for j in range(REACH):
            raw_ref[k, j : j + 1] = before_ref[j, pl.ds(k, 1)]
            raw_ref[k, REACH + width + j : REACH + width + j + 1] = after_ref[j, pl.ds(k, 1)]
        return 0

    lax.fori_loop(0, wide_x, fill, 0)

    def raw(k, y):
        return raw_ref[k, pl.ds(y + REACH, SUB, stride=run), :]

    def masked(value, y):
        if y < 0:
            value = value * mask_y_low
        if y >= run:
            value = value * mask_y_high
        return value

    low, high = spans[0][0], spans[-1][1]

    def smooth(centre, others):
        total = z_sum(centre)
        for other in others:
            total = total + other
        return 0.4 * centre + 0.1 * total

    def smooth_once(k, _):
        column = [raw(k + 1, y) for y in range(low - 3, high + 3)]
        for i in range(1, len(column) - 1):
            y = low - 3 + i
            value = smooth(column[i], [column[i - 1], column[i + 1], raw(k, y), raw(k + 2, y)])
            once_ref[k, y + 2] = masked(value, y)
        return 0

    lax.fori_loop(0, half + 4, smooth_once, 0)
    for ref, margin, ys in ((once_ref, 2, range(low - 2, high + 2)),):
        for y in ys:
            for k in (0, 1):
                ref[k, y + margin] = ref[k, y + margin] * mask_x_low
                ref[half + 2 + k, y + margin] = ref[half + 2 + k, y + margin] * mask_x_high

    def smooth_twice(k, _):
        at_low = jnp.where(k == 0, mask_x_low, 1.0)
        at_high = jnp.where(k == half + 1, mask_x_high, 1.0)
        edge = at_low * at_high
        column = [once_ref[k + 1, y + 2] for y in range(low - 2, high + 2)]
        for i in range(1, len(column) - 1):
            y = low - 2 + i
            value = smooth(
                column[i], [column[i - 1], column[i + 1], once_ref[k, y + 2], once_ref[k + 2, y + 2]]
            )
            value = masked(value * edge, y)
            twice_ref[k, y + 1] = value
            ridge_ref[k, y + 1] = 2.0 * value + z_sum(value)
        return 0

    lax.fori_loop(0, half + 2, smooth_twice, 0)

    ones = jnp.ones((16, 2 * LANES), jnp.bfloat16)

    def features(k, y):
        p = lambda a, b: twice_ref[k + 1 + a, y + 1 + b]
        r = lambda a, b: ridge_ref[k + 1 + a, y + 1 + b]
        centre = p(0, 0)
        pp, pm, mp, mm = p(1, 1), p(1, -1), p(-1, 1), p(-1, -1)
        main, cross = pp - mm, pm - mp
        third = 1.0 / 3.0
        gx = (main + cross + (r(1, 0) - r(-1, 0))) * third
        gy = (main - cross + (r(0, 1) - r(0, -1))) * third
        around = 2.0 * centre + ((p(1, 0) + p(-1, 0)) + (p(0, 1) + p(0, -1)))
        gz = (pltpu.roll(around, LANES - 1, axis=1) * far - pltpu.roll(around, 1, axis=1) * near) * third
        m = jnp.sqrt(1.0 + gx * gx + gy * gy + gz * gz)
        return [centre, gx, gy, gz, m, centre * m, centre * centre]

    def square(parts):
        return jnp.concatenate(
            [
                jnp.concatenate([parts[0], parts[1]], axis=1),
                jnp.concatenate([parts[2], parts[3]], axis=1),
            ],
            axis=0,
        )

    def network(x0, y):
        cells = [features(x0 + i, y) for i in range(4)]
        rows = [square([cell[f] for cell in cells]).astype(jnp.bfloat16) for f in range(7)] + [ones]
        packed = jnp.concatenate(rows, axis=0)
        half_v = jnp.dot(win_ref[...], packed, preferred_element_type=F32)
        hidden = (half_v + half_v * jnp.tanh(half_v)).astype(jnp.bfloat16)
        v = jnp.dot(wout_ref[...], hidden, preferred_element_type=F32)
        soft = jnp.maximum(v, jnp.log(1.0 + jnp.exp2(jnp.minimum(v * LOG2E, 126.0))))
        split = bands * 16
        emission = soft[:split]
        clear_y = jnp.exp2(soft[split:] * (-LOG2E * steps[1]))
        return emission, clear_y

    ratio = steps[0] / steps[1]

    def clear_of_x(q):
        if ratio == 1.0:
            return q
        if ratio == 2.0:
            return q * q
        return jnp.exp2(jnp.log(q) * (LOG2E * ratio))

    def cell_of(values, band, i):
        j, h = divmod(i, 2)
        return values[band * 16 + j * 8 : band * 16 + j * 8 + 8, h * LANES : (h + 1) * LANES]

    nys = sum(b - a for a, b in spans)
    zeros = jnp.zeros((SUB, LANES), F32)
    unit = jnp.ones((SUB, LANES), F32)

    def reset(k, _):
        for band in range(bands):
            ty_ref[k, band] = unit
            cy_ref[k, band] = zeros
        return 0

    lax.fori_loop(0, half, reset, 0)
    for k in range(nys):
        for band in range(bands):
            tx_ref[k, band] = unit
            cx_ref[k, band] = zeros

    slot0 = 0
    for first, last in spans:
        for y0 in range(first, last, 4):
            count = min(4, last - y0)

            def block(xb, _, y0=y0, count=count, slot=slot0 + y0 - first):
                x0 = xb * 4
                results = [network(x0, y0 + j) for j in range(count)]
                for band in range(bands):
                    ty = [ty_ref[x0 + i, band] for i in range(4)]
                    cy = [cy_ref[x0 + i, band] for i in range(4)]
                    for j, (emission, clear) in enumerate(results):
                        tx = tx_ref[slot + j, band]
                        cx = cx_ref[slot + j, band]
                        for i in range(4):
                            e = cell_of(emission, band, i)
                            q = cell_of(clear, band, i)
                            later = ty[i] * q
                            cy[i] = cy[i] + (ty[i] - later) * e
                            ty[i] = later
                            later = tx * clear_of_x(q)
                            cx = cx + (tx - later) * e
                            tx = later
                        tx_ref[slot + j, band] = tx
                        cx_ref[slot + j, band] = cx
                    for i in range(4):
                        ty_ref[x0 + i, band] = ty[i]
                        cy_ref[x0 + i, band] = cy[i]
                return 0

            lax.fori_loop(0, half // 4, block, 0)
        slot0 += last - first

    front = lane < layers
    for band in range(bands):
        for k in range(nys):
            colour, clear = cx_ref[k, band], tx_ref[k, band]
            colour = colour + clear * pltpu.roll(colour, layers, axis=1)
            clear = clear * pltpu.roll(clear, layers, axis=1)
            rows_ref[pl.ds(k, SUB, stride=nys), :] = jnp.where(
                front, colour, pltpu.roll(clear, layers, axis=1)
            )
        turned = rows_ref[...].T
        for kind in range(2):
            for d in range(layers // SUB):
                start = kind * layers + d * SUB
                image_x_ref[d, kind, band] = turned[start : start + SUB]

    def fold_y(k, _):
        for band in range(bands):
            colour, clear = over_sublanes(cy_ref[k, band], ty_ref[k, band])
            rows_y_ref[pl.ds(band * half + k, 1), :] = colour[:1]
            rows_y_ref[pl.ds((bands + band) * half + k, 1), :] = clear[:1]
        return 0

    lax.fori_loop(0, half, fold_y, 0)
    for kind in range(2):
        turned = rows_y_ref[kind * LANES : (kind + 1) * LANES].T
        image_y_ref[kind] = turned


def fold_kernel(pieces_ref, out_ref):
    colour, clear = pieces_ref[0, 0], pieces_ref[0, 1]
    for k in range(1, pieces_ref.shape[0]):
        colour = colour + clear * pieces_ref[k, 0]
        clear = clear * pieces_ref[k, 1]
    out_ref[0] = colour
    out_ref[1] = clear


def fold(pieces):
    return pl.pallas_call(
        fold_kernel,
        out_shape=jax.ShapeDtypeStruct(pieces.shape[1:], F32),
        in_specs=[VMEM],
        out_specs=VMEM,
        name="fold",
    )(pieces)


def exchange(last, first, axis):
    peers = lax.axis_size(axis)
    up = [(i, i + 1) for i in range(peers - 1)]
    down = [(j, i) for i, j in up]
    return lax.ppermute(last, axis, up), lax.ppermute(first, axis, down)


def body(scalar_field, transfer_in, transfer_out):
    layers, local_x, local_y = scalar_field.shape
    bands = transfer_out.shape[0] // 2
    count_x = lax.axis_size("bx")
    count_y = lax.axis_size("by")
    steps = (2.0 / (local_x * count_x), 2.0 / (local_y * count_y))
    half = local_x // 2
    wide = half + 2 * REACH
    run = local_y // SUB
    sds = jax.ShapeDtypeStruct
    eye = jnp.eye(16, dtype=jnp.bfloat16)
    win = jnp.kron(transfer_in * jnp.bfloat16(0.5), eye)
    wout = jnp.kron(transfer_out, eye)

    strip = sds((REACH, layers, local_y), F32)
    first, last = pl.pallas_call(
        strips_kernel,
        out_shape=[strip, strip],
        in_specs=[VMEM],
        out_specs=[VMEM, VMEM],
        compiler_params=PARAMS,
        name="strips",
    )(scalar_field)
    before, after = exchange(last, first, "bx")
    edge = sds((REACH, wide, LANES), F32)
    turned, first, last = pl.pallas_call(
        turn_kernel,
        out_shape=[sds((wide, local_y, LANES), F32), edge, edge],
        in_specs=[VMEM] * 3,
        out_specs=[VMEM] * 3,
        compiler_params=PARAMS,
        name="turn",
    )(scalar_field, before, after)
    before, after = exchange(last, first, "by")
    spans = ((0, run),)
    scratch = [
        pltpu.VMEM((wide, local_y + 2 * SUB, LANES), F32),
        pltpu.VMEM((half + 4, run + 4, SUB, LANES), F32),
        pltpu.VMEM((half + 2, run + 2, SUB, LANES), F32),
        pltpu.VMEM((half + 2, run + 2, SUB, LANES), F32),
        pltpu.VMEM((run, bands, SUB, LANES), F32),
        pltpu.VMEM((run, bands, SUB, LANES), F32),
        pltpu.VMEM((half, bands, SUB, LANES), F32),
        pltpu.VMEM((half, bands, SUB, LANES), F32),
        pltpu.VMEM((local_y, LANES), F32),
        pltpu.VMEM((2 * bands * half, LANES), F32),
    ]
    image_x, image_y = pl.pallas_call(
        functools.partial(march_kernel, spans, (count_x, count_y), steps, bands),
        out_shape=[
            sds((layers // SUB, 2, bands, SUB, local_y), F32),
            sds((2, LANES, bands * half), F32),
        ],
        in_specs=[VMEM] * 5,
        out_specs=[VMEM] * 2,
        scratch_shapes=scratch,
        compiler_params=PARAMS,
        name="march",
    )(turned, before, after, win, wout)
    share = layers // count_y
    pieces = image_y.reshape(2, 2, count_y, share, bands * half)
    pieces = jnp.transpose(pieces, (2, 0, 1, 3, 4)).reshape(count_y, 2, 2 * share, bands * half)
    pieces = lax.all_to_all(pieces, "by", split_axis=0, concat_axis=0, tiled=True)
    view_y = fold(pieces)
    view_y = jnp.transpose(
        view_y.reshape(2, 2, share, bands, half), (0, 3, 2, 1, 4)
    ).reshape(2, bands, share, local_x)
    share_x = layers // count_x
    image_x = image_x.reshape(layers // SUB, 2, bands, SUB, local_y)
    if share_x != SUB:
        image_x = jnp.transpose(image_x, (1, 2, 0, 3, 4)).reshape(2, bands, count_x, share_x, local_y)
        image_x = jnp.transpose(image_x, (2, 0, 1, 3, 4))
    pieces = lax.all_to_all(image_x, "bx", split_axis=0, concat_axis=0, tiled=True)
    view_x = fold(pieces)
    return (view_x, view_y)


def solution(mesh):
    return jax.shard_map(
        body,
        mesh=mesh,
        in_specs=(P(None, "bx", "by"), P(), P()),
        out_specs=(P(None, None, "bx", "by"), P(None, None, "by", "bx")),
        check_vma=False,
    )
```

```python
import functools

import jax
import jax.numpy as jnp
from jax import lax
from jax.experimental import pallas as pl
from jax.experimental.pallas import tpu as pltpu
from jax.sharding import PartitionSpec as P

F32 = jnp.float32
BF16 = jnp.bfloat16
LOG2E = 1.4426950408889634
SUB = 8
LANES = 128
CHUNKS = 16
REACH = 3
VMEM = pl.BlockSpec(memory_space=pltpu.VMEM)
PARAMS = pltpu.CompilerParams(vmem_limit_bytes=48 * 1024 * 1024)


def call(kernel, name, outs, count, scratch=()):
    return pl.pallas_call(
        kernel,
        out_shape=outs,
        in_specs=[VMEM] * count,
        out_specs=jax.tree.map(lambda _: VMEM, outs),
        scratch_shapes=scratch,
        compiler_params=PARAMS,
        name=name,
    )


def rows_of(width):
    return -(-(width + 2 * REACH) // 16) * 16


def iota(shape, dim):
    return lax.broadcasted_iota(jnp.int32, shape, dim)


def one_hot(mask):
    return jnp.where(mask, 1.0, 0.0).astype(BF16)


def spread(weights, left, right, mask):
    inner = lax.dot_general(
        left, weights, (((1,), (1,)), ((), ())), preferred_element_type=F32
    ).astype(BF16)
    return jnp.where(mask, jnp.dot(inner, right, preferred_element_type=F32), 0.0)


def turn_kernel(field_ref, in_ref, out_ref, turned_ref, first_ref, last_ref, win_ref, wout_ref):
    layers, length, width = field_ref.shape
    half = length // 2
    for k in range(half):
        turned = jnp.concatenate([field_ref[:, k, :], field_ref[:, k + half, :]], axis=0).T
        turned_ref[k, REACH : REACH + width] = turned
        for j in range(REACH):
            first_ref[j, k : k + 1] = turned[j : j + 1]
            last_ref[j, k : k + 1] = turned[width - REACH + j : width - REACH + j + 1]
    units, feats = in_ref.shape
    channels = out_ref.shape[0]
    bands = channels // 2
    rows, cols = feats * CHUNKS, units * CHUNKS
    left = one_hot(iota((rows, feats), 0) // CHUNKS == iota((rows, feats), 1))
    right = one_hot(iota((units, cols), 1) // CHUNKS == iota((units, cols), 0))
    mask = iota((rows, cols), 0) % CHUNKS == iota((rows, cols), 1) % CHUNKS
    win_ref[...] = (0.5 * spread(in_ref[...], left, right, mask)).astype(BF16)
    rows, cols = cols, channels * CHUNKS
    left = one_hot(iota((rows, units), 0) // CHUNKS == iota((rows, units), 1))
    at = iota((channels, cols), 1)
    right = one_hot((at // LANES) * bands + at % bands == iota((channels, cols), 0))
    mask = iota((rows, cols), 0) % CHUNKS == (iota((rows, cols), 1) % LANES) // bands
    wout_ref[...] = spread(out_ref[...], left, right, mask).astype(BF16)


def sides_kernel(rows_in, turned_ref, before_ref, after_ref, wide_ref, first_ref, last_ref):
    half, rows, _ = turned_ref.shape
    width = rows_in
    layers = LANES // 2
    part = rows // 2
    front = iota((part, LANES), 1) < layers
    for k in range(half):
        wide_ref[k, REACH : REACH + width] = turned_ref[k, REACH : REACH + width]
        for j in range(REACH):
            wide_ref[k, j : j + 1] = before_ref[j, k : k + 1]
            wide_ref[k, REACH + width + j : REACH + width + j + 1] = after_ref[j, k : k + 1]
        wide_ref[k, 2 * REACH + width :] = jnp.zeros((rows - 2 * REACH - width, LANES), F32)
    for j in range(REACH):
        top, low = wide_ref[j, :part], wide_ref[j, part:]
        first_ref[j] = jnp.where(front, top, pltpu.roll(low, layers, axis=1))
        k = half - REACH + j
        top, low = wide_ref[k, :part], wide_ref[k, part:]
        last_ref[j] = jnp.where(front, pltpu.roll(top, layers, axis=1), low)


def march_kernel(
    spans,
    block_y,
    counts,
    steps,
    *refs,
):
    (wide_ref, before_ref, after_ref, win_ref, wout_ref, image_x_ref, ty_ref, cy_ref) = refs[:8]
    (raw_ref, once_ref, twice_ref, ridge_ref, tx_ref, cx_ref) = refs[8:]
    half, rows, _ = wide_ref.shape
    run = tx_ref.shape[0]
    layers = LANES // 2
    shape = (CHUNKS, LANES)
    lane, chunk = iota(shape, 1), iota(shape, 0)
    z = lane % layers
    near = (z > 0).astype(F32)
    far = (z < layers - 1).astype(F32)
    at_x, at_y = lax.axis_index("bx"), lax.axis_index("by")
    count_x, count_y = counts
    mask_x_low = jnp.where((lane < layers) & (at_x == 0), 0.0, 1.0)
    mask_x_high = jnp.where((lane >= layers) & (at_x == count_x - 1), 0.0, 1.0)
    mask_y_low = jnp.where((chunk == 0) & (at_y == 0), 0.0, 1.0)
    mask_y_high = jnp.where((chunk == CHUNKS - 1) & (at_y == count_y - 1), 0.0, 1.0)

    def roll(value, shift):
        return pltpu.roll(value, shift % LANES, axis=1)

    def z_sum(value):
        return roll(value, 1) * near + roll(value, -1) * far

    part = rows // 2
    front = iota((part, LANES), 1) < layers
    for j in range(REACH):
        halo, own = before_ref[j], wide_ref[half - REACH + j]
        raw_ref[j, :part] = jnp.where(front, halo, roll(own[:part], layers))
        raw_ref[j, part:] = jnp.where(front, roll(halo, layers), roll(own[part:], layers))
        halo, own = after_ref[j], wide_ref[j]
        k = half + REACH + j
        raw_ref[k, :part] = jnp.where(front, roll(own[:part], layers), roll(halo, layers))
        raw_ref[k, part:] = jnp.where(front, roll(own[part:], layers), halo)

    def copy_in(k, _):
        raw_ref[k + REACH] = wide_ref[k]
        return 0

    lax.fori_loop(0, half, copy_in, 0)

    def raw(k, y):
        return raw_ref[k, pl.ds(y + REACH, CHUNKS, stride=run), :]

    def masked(value, y):
        if y < 0:
            value = value * mask_y_low
        if y >= run:
            value = value * mask_y_high
        return value

    def smooth(centre, others):
        total = z_sum(centre)
        for other in others:
            total = total + other
        return 0.4 * centre + 0.1 * total

    def smooth_once(k, _):
        column = [raw(k + 1, y) for y in range(-3, run + 3)]
        for i in range(1, len(column) - 1):
            y = i - 3
            value = smooth(column[i], [column[i - 1], column[i + 1], raw(k, y), raw(k + 2, y)])
            once_ref[k, y + 2] = masked(value, y)
        return 0

    lax.fori_loop(0, half + 4, smooth_once, 0)
    for y in range(run + 4):
        for k in (0, 1):
            once_ref[k, y] = once_ref[k, y] * mask_x_low
            once_ref[half + 2 + k, y] = once_ref[half + 2 + k, y] * mask_x_high

    def smooth_twice(k, _):
        edge = jnp.where(k == 0, mask_x_low, 1.0) * jnp.where(k == half + 1, mask_x_high, 1.0)
        column = [once_ref[k + 1, y] for y in range(run + 4)]
        for i in range(1, len(column) - 1):
            y = i - 2
            value = smooth(
                column[i], [column[i - 1], column[i + 1], once_ref[k, i], once_ref[k + 2, i]]
            )
            value = masked(value * edge, y)
            twice_ref[k, y + 1] = value
            ridge_ref[k, y + 1] = 2.0 * value + z_sum(value)
        return 0

    lax.fori_loop(0, half + 2, smooth_twice, 0)

    ones = jnp.ones(shape, BF16)

    def features(k, y):
        p = lambda a, b: twice_ref[k + 1 + a, y + 1 + b]
        r = lambda a, b: ridge_ref[k + 1 + a, y + 1 + b]
        centre = p(0, 0)
        main, cross = p(1, 1) - p(-1, -1), p(1, -1) - p(-1, 1)
        third = 1.0 / 3.0
        gx = (main + cross + (r(1, 0) - r(-1, 0))) * third
        gy = (main - cross + (r(0, 1) - r(0, -1))) * third
        around = 2.0 * centre + ((p(1, 0) + p(-1, 0)) + (p(0, 1) + p(0, -1)))
        gz = (roll(around, -1) * far - roll(around, 1) * near) * third
        m = jnp.sqrt(1.0 + gx * gx + gy * gy + gz * gz)
        parts = [centre, gx, gy, gz, m, centre * m, centre * centre]
        packed = [part.astype(BF16) for part in parts] + [ones]
        return jnp.concatenate(packed, axis=0).T

    def network(tiles):
        half_v = jnp.dot(tiles, win_ref[...], preferred_element_type=F32)
        hidden = (half_v + half_v * jnp.tanh(half_v)).astype(BF16)
        v = jnp.dot(hidden, wout_ref[...], preferred_element_type=F32)
        soft = jnp.maximum(v, jnp.log(1.0 + jnp.exp2(jnp.minimum(v * LOG2E, 126.0))))
        return soft[:, :LANES], jnp.exp2(soft[:, LANES:] * (-LOG2E * steps[1]))

    ratio = steps[0] / steps[1]

    def clear_of_x(q):
        if ratio == 1.0:
            return q
        if ratio == 2.0:
            return q * q
        return jnp.exp2(jnp.log(q) * (LOG2E * ratio))

    groups = LANES // SUB

    def reset(k, _):
        ty_ref[k] = jnp.ones((LANES, LANES), F32)
        cy_ref[k] = jnp.zeros((LANES, LANES), F32)
        return 0

    lax.fori_loop(0, half, reset, 0)
    for k in range(run):
        tx_ref[k] = jnp.ones((LANES, LANES), F32)
        cx_ref[k] = jnp.zeros((LANES, LANES), F32)

    def block(x0, y0, many_x, many_y):
        tiles = [features(x0 + i, y0 + j) for j in range(many_y) for i in range(many_x)]
        emission, clear = network(jnp.concatenate(tiles, axis=0))
        for g in range(groups):
            at = pl.ds(g * SUB, SUB)
            ty = [ty_ref[x0 + i, at] for i in range(many_x)]
            cy = [cy_ref[x0 + i, at] for i in range(many_x)]
            for j in range(many_y):
                tx, cx = tx_ref[y0 + j, at], cx_ref[y0 + j, at]
                for i in range(many_x):
                    start = (j * many_x + i) * LANES + g * SUB
                    e, q = emission[start : start + SUB], clear[start : start + SUB]
                    later = ty[i] * q
                    cy[i] = cy[i] + (ty[i] - later) * e
                    ty[i] = later
                    later = tx * clear_of_x(q)
                    cx = cx + (tx - later) * e
                    tx = later
                tx_ref[y0 + j, at], cx_ref[y0 + j, at] = tx, cx
            for i in range(many_x):
                ty_ref[x0 + i, at], cy_ref[x0 + i, at] = ty[i], cy[i]

    for first, last, many_x in spans:

        def over_blocks(step, _, first=first, many_x=many_x):
            x0 = first + (step // (run // block_y)) * many_x
            y0 = (step % (run // block_y)) * block_y
            block(x0, y0, many_x, block_y)
            return 0

        lax.fori_loop(0, (last - first) // many_x * (run // block_y), over_blocks, 0)

    for y in range(run):
        q = tx_ref[y, :layers]
        colour = cx_ref[y, :layers] + q * cx_ref[y, layers:]
        q = q * tx_ref[y, layers:]
        for d in range(layers // SUB):
            image_x_ref[d, 0, y] = colour[d * SUB : (d + 1) * SUB]
            image_x_ref[d, 1, y] = q[d * SUB : (d + 1) * SUB]


def columns_kernel(share, peers, ty_ref, cy_ref, *refs):
    outs, (rows_ref, turned_ref) = refs[:peers], refs[peers:]
    half = ty_ref.shape[0]
    layers = LANES // 2
    for k in range(half):
        colours, clears = cy_ref[k].T, ty_ref[k].T
        colour, clear = colours[:SUB], clears[:SUB]
        for c in range(1, CHUNKS):
            at = slice(c * SUB, (c + 1) * SUB)
            colour = colour + clear * colours[at]
            clear = clear * clears[at]
        rows_ref[0, k * SUB : (k + 1) * SUB] = colour
        rows_ref[1, k * SUB : (k + 1) * SUB] = clear
    me = lax.axis_index("by")
    for kind in range(2):
        turned_ref[kind] = rows_ref[kind].T
        for s in range(peers):
            start = pl.multiple_of(lax.rem(me + s, peers) * share, share)
            for part in range(2):
                outs[s][kind, part] = turned_ref[kind, pl.ds(part * layers + start, share)]


def fold_y_kernel(*refs):
    pieces, out_ref = refs[:-1], refs[-1]
    peers = len(pieces)
    me = lax.axis_index("by")

    def piece(source):
        shift = lax.rem(me - source + peers, peers)
        value = pieces[0][...]
        for s in range(1, peers):
            value = jnp.where(shift == s, pieces[s][...], value)
        return value

    value = piece(0)
    colour, clear = value[0], value[1]
    for source in range(1, peers):
        value = piece(source)
        colour = colour + clear * value[0]
        clear = clear * value[1]
    out_ref[0] = colour
    out_ref[1] = clear


def fold_x_kernel(pieces_ref, out_ref):
    peers, _, run, share, _ = pieces_ref.shape
    lane = iota((share, LANES), 1)
    kinds = [[], []]
    for y in range(run):
        colour, clear = pieces_ref[0, 0, y], pieces_ref[0, 1, y]
        for k in range(1, peers):
            colour = colour + clear * pieces_ref[k, 0, y]
            clear = clear * pieces_ref[k, 1, y]
        kinds[0].append(colour)
        kinds[1].append(clear)
    for kind, values in enumerate(kinds):
        for s in (1, 2, 4):
            for i in range(run):
                if not i & s:
                    a, b = values[i], values[i | s]
                    odd = (lane & s) != 0
                    values[i] = jnp.where(odd, pltpu.roll(b, s, axis=1), a)
                    values[i | s] = jnp.where(odd, b, pltpu.roll(a, LANES - s, axis=1))
        for band, value in enumerate(values):
            out_ref[kind, band] = value


def exchange(last, first, axis):
    peers = lax.axis_size(axis)
    up = [(i, i + 1) for i in range(peers - 1)]
    down = [(j, i) for i, j in up]
    return lax.ppermute(last, axis, up), lax.ppermute(first, axis, down)


def body(scalar_field, transfer_in, transfer_out):
    layers, local_x, local_y = scalar_field.shape
    units, feats = transfer_in.shape
    channels = transfer_out.shape[0]
    bands = channels // 2
    count_x, count_y = lax.axis_size("bx"), lax.axis_size("by")
    steps = (2.0 / (local_x * count_x), 2.0 / (local_y * count_y))
    half, run, rows = local_x // 2, local_y // CHUNKS, rows_of(local_y)
    sds = lambda *shape: jax.ShapeDtypeStruct(shape, F32)
    weights = [
        jax.ShapeDtypeStruct((feats * CHUNKS, units * CHUNKS), BF16),
        jax.ShapeDtypeStruct((units * CHUNKS, channels * CHUNKS), BF16),
    ]

    edge = sds(REACH, half, LANES)
    turned, first, last, win, wout = call(
        turn_kernel, "turn", [sds(half, rows, LANES), edge, edge] + weights, 3
    )(scalar_field, transfer_in, transfer_out)
    before, after = exchange(last, first, "by")
    edge = sds(REACH, rows // 2, LANES)
    wide, first, last = call(functools.partial(sides_kernel, local_y), "sides", [sds(half, rows, LANES), edge, edge], 3)(
        turned, before, after
    )
    before, after = exchange(last, first, "bx")
    state = sds(half, LANES, LANES)
    scratch = [
        pltpu.VMEM((half + 2 * REACH, rows, LANES), F32),
        pltpu.VMEM((half + 4, run + 4, CHUNKS, LANES), F32),
        pltpu.VMEM((half + 2, run + 2, CHUNKS, LANES), F32),
        pltpu.VMEM((half + 2, run + 2, CHUNKS, LANES), F32),
        pltpu.VMEM((run, LANES, LANES), F32),
        pltpu.VMEM((run, LANES, LANES), F32),
    ]
    image_x, clear_y, colour_y = call(
        functools.partial(march_kernel, ((0, half, 4),), 2, (count_x, count_y), steps),
        "march",
        [sds(layers // SUB, 2, run, SUB, LANES), state, state],
        5,
        scratch,
    )(wide, before, after, win, wout)

    share_x = layers // count_x
    if share_x != SUB:
        image_x = jnp.transpose(image_x, (1, 2, 0, 3, 4)).reshape(2, run, count_x, share_x, LANES)
        image_x = jnp.transpose(image_x, (2, 0, 1, 3, 4))
    pieces = lax.all_to_all(image_x, "bx", split_axis=0, concat_axis=0, tiled=True)
    view_x = call(fold_x_kernel, "fold_x", sds(2, bands, share_x, local_y), 1)(pieces)

    share = layers // count_y
    piece = sds(2, 2, share, LANES)
    scratch = [pltpu.VMEM((2, LANES, LANES), F32), pltpu.VMEM((2, LANES, LANES), F32)]
    pieces = call(
        functools.partial(columns_kernel, share, count_y), "columns", [piece] * count_y, 2, scratch
    )(clear_y, colour_y)
    pieces = list(pieces)
    for s in range(1, count_y):
        pairs = [(i, (i + s) % count_y) for i in range(count_y)]
        pieces[s] = lax.ppermute(pieces[s], "by", pairs)
    view_y = call(fold_y_kernel, "fold_y", piece, count_y)(*pieces)
    view_y = view_y.reshape(2, 2, share, half, bands)
    view_y = jnp.transpose(view_y, (0, 4, 2, 1, 3)).reshape(2, bands, share, local_x)
    return (view_x, view_y)


def solution(mesh):
    return jax.shard_map(
        body,
        mesh=mesh,
        in_specs=(P(None, "bx", "by"), P(), P()),
        out_specs=(P(None, None, "bx", "by"), P(None, None, "by", "bx")),
        check_vma=False,
    )
```

```python
import functools

import jax
import jax.numpy as jnp
from jax import lax
from jax.experimental import pallas as pl
from jax.experimental.pallas import tpu as pltpu
from jax.sharding import PartitionSpec as P

F32 = jnp.float32
BF16 = jnp.bfloat16
LOG2E = 1.4426950408889634
SUB = 8
LANES = 128
CHUNKS = 16
REACH = 3
VMEM = pl.BlockSpec(memory_space=pltpu.VMEM)
PARAMS = pltpu.CompilerParams(vmem_limit_bytes=48 * 1024 * 1024)


def call(kernel, name, outs, count, scratch=()):
    return pl.pallas_call(
        kernel,
        out_shape=outs,
        in_specs=[VMEM] * count,
        out_specs=jax.tree.map(lambda _: VMEM, outs),
        scratch_shapes=scratch,
        compiler_params=PARAMS,
        name=name,
    )


def rows_of(width):
    return -(-(width + 2 * REACH) // 16) * 16


def iota(shape, dim):
    return lax.broadcasted_iota(jnp.int32, shape, dim)


def one_hot(mask):
    return jnp.where(mask, 1.0, 0.0).astype(BF16)


def spread(weights, left, right, mask):
    inner = lax.dot_general(
        left, weights, (((1,), (1,)), ((), ())), preferred_element_type=F32
    ).astype(BF16)
    return jnp.where(mask, jnp.dot(inner, right, preferred_element_type=F32), 0.0)


def turn_kernel(field_ref, turned_ref, first_ref, last_ref):
    layers, length, width = field_ref.shape
    half = length // 2
    for k in range(half):
        turned = jnp.concatenate([field_ref[:, k, :], field_ref[:, k + half, :]], axis=0).T
        turned_ref[k, REACH : REACH + width] = turned
        for j in range(REACH):
            first_ref[j, k : k + 1] = turned[j : j + 1]
            last_ref[j, k : k + 1] = turned[width - REACH + j : width - REACH + j + 1]


def weights_kernel(in_ref, out_ref, after_ref, win_ref, wout_ref):
    del after_ref
    units, feats = in_ref.shape
    channels = out_ref.shape[0]
    bands = channels // 2
    rows, cols = feats * CHUNKS, units * CHUNKS
    left = one_hot(iota((rows, feats), 0) // CHUNKS == iota((rows, feats), 1))
    right = one_hot(iota((units, cols), 1) // CHUNKS == iota((units, cols), 0))
    mask = iota((rows, cols), 0) % CHUNKS == iota((rows, cols), 1) % CHUNKS
    win_ref[...] = (0.5 * spread(in_ref[...], left, right, mask)).astype(BF16)
    rows, cols = cols, channels * CHUNKS
    left = one_hot(iota((rows, units), 0) // CHUNKS == iota((rows, units), 1))
    at = iota((channels, cols), 1)
    right = one_hot((at // LANES) * bands + at % bands == iota((channels, cols), 0))
    mask = iota((rows, cols), 0) % CHUNKS == (iota((rows, cols), 1) % LANES) // bands
    wout_ref[...] = spread(out_ref[...], left, right, mask).astype(BF16)


def sides_kernel(rows_in, turned_ref, before_ref, after_ref, wide_ref, first_ref, last_ref):
    half, rows, _ = turned_ref.shape
    width = rows_in
    layers = LANES // 2
    part = rows // 2
    front = iota((part, LANES), 1) < layers
    for k in range(half):
        wide_ref[k, REACH : REACH + width] = turned_ref[k, REACH : REACH + width]
        for j in range(REACH):
            wide_ref[k, j : j + 1] = before_ref[j, k : k + 1]
            wide_ref[k, REACH + width + j : REACH + width + j + 1] = after_ref[j, k : k + 1]
        wide_ref[k, 2 * REACH + width :] = jnp.zeros((rows - 2 * REACH - width, LANES), F32)
    for j in range(REACH):
        top, low = wide_ref[j, :part], wide_ref[j, part:]
        first_ref[j] = jnp.where(front, top, pltpu.roll(low, layers, axis=1))
        k = half - REACH + j
        top, low = wide_ref[k, :part], wide_ref[k, part:]
        last_ref[j] = jnp.where(front, pltpu.roll(top, layers, axis=1), low)


class Stencil:
    def __init__(self, run, counts):
        self.run = run
        self.layers = layers = LANES // 2
        self.shape = (CHUNKS, LANES)
        lane, chunk = iota(self.shape, 1), iota(self.shape, 0)
        z = lane % layers
        self.near = (z > 0).astype(F32)
        self.far = (z < layers - 1).astype(F32)
        at_x, at_y = lax.axis_index("bx"), lax.axis_index("by")
        count_x, count_y = counts
        self.x_low = jnp.where((lane < layers) & (at_x == 0), 0.0, 1.0)
        self.x_high = jnp.where((lane >= layers) & (at_x == count_x - 1), 0.0, 1.0)
        self.y_low = jnp.where((chunk == 0) & (at_y == 0), 0.0, 1.0)
        self.y_high = jnp.where((chunk == CHUNKS - 1) & (at_y == count_y - 1), 0.0, 1.0)

    def z_sum(self, value):
        return roll(value, 1) * self.near + roll(value, -1) * self.far

    def inside(self, value, y, edge):
        if edge is not None:
            value = value * edge
        if y < 0:
            value = value * self.y_low
        if y >= self.run:
            value = value * self.y_high
        return value

    def smooth(self, centre, others):
        total = self.z_sum(centre)
        for other in others:
            total = total + other
        return 0.4 * centre + 0.1 * total

    def raw(self, ref, k, y):
        return ref[k, pl.ds(y + REACH, CHUNKS, stride=self.run), :]

    def once(self, raw, k, out, at, edge=None):
        column = [self.raw(raw, k, y) for y in range(-3, self.run + 3)]
        for i in range(1, len(column) - 1):
            y = i - 3
            sides = [self.raw(raw, k - 1, y), self.raw(raw, k + 1, y)]
            value = self.smooth(column[i], [column[i - 1], column[i + 1]] + sides)
            out[at, i - 1] = self.inside(value, y, edge)

    def twice(self, once, k, out, ridge, at, edge=None):
        column = [once[k, i] for i in range(self.run + 4)]
        for i in range(1, len(column) - 1):
            sides = [once[k - 1, i], once[k + 1, i]]
            value = self.smooth(column[i], [column[i - 1], column[i + 1]] + sides)
            value = self.inside(value, i - 2, edge)
            out[at, i - 1] = value
            ridge[at, i - 1] = 2.0 * value + self.z_sum(value)

    def features(self, twice, ridge, k, y):
        p = lambda a, b: twice[k + a, y + 1 + b]
        r = lambda a, b: ridge[k + a, y + 1 + b]
        centre = p(0, 0)
        main, cross = p(1, 1) - p(-1, -1), p(1, -1) - p(-1, 1)
        third = 1.0 / 3.0
        gx = (main + cross + (r(1, 0) - r(-1, 0))) * third
        gy = (main - cross + (r(0, 1) - r(0, -1))) * third
        around = 2.0 * centre + ((p(1, 0) + p(-1, 0)) + (p(0, 1) + p(0, -1)))
        gz = (roll(around, -1) * self.far - roll(around, 1) * self.near) * third
        m = jnp.sqrt(1.0 + gx * gx + gy * gy + gz * gz)
        parts = [centre, gx, gy, gz, m, centre * m, centre * centre]
        packed = [part.astype(BF16) for part in parts] + [jnp.ones(self.shape, BF16)]
        return jnp.concatenate(packed, axis=0).T


def roll(value, shift):
    return pltpu.roll(value, shift % LANES, axis=1)


def network(tiles, win_ref, wout_ref, step):
    cells = jnp.concatenate(tiles, axis=0)
    half_v = jnp.dot(cells, win_ref[...], preferred_element_type=F32)
    hidden = (half_v + half_v * jnp.tanh(half_v)).astype(BF16)
    v = jnp.dot(hidden, wout_ref[...], preferred_element_type=F32)
    soft = jnp.maximum(v, jnp.log(1.0 + jnp.exp2(jnp.minimum(v * LOG2E, 126.0))))
    return soft[:, :LANES], jnp.exp2(soft[:, LANES:] * (-LOG2E * step))


def clear_of_x(q, ratio):
    if ratio == 1.0:
        return q
    if ratio == 2.0:
        return q * q
    return jnp.exp2(jnp.log(q) * (LOG2E * ratio))


def step_ray(ray, clear, emission):
    colour, light = ray
    later = light * clear
    return colour + (light - later) * emission, later


def middle_kernel(
    spans,
    counts,
    steps,
    wide_ref,
    win_ref,
    wout_ref,
    once_out_ref,
    twice_out_ref,
    ridge_out_ref,
    cx_ref,
    tx_ref,
    cy_ref,
    ty_ref,
    once_ref,
    twice_ref,
    ridge_ref,
):
    half = wide_ref.shape[0]
    run = cx_ref.shape[0]
    stencil = Stencil(run, counts)
    many_x, many_y = spans
    inner = half - 2 * REACH

    def once(k, _):
        stencil.once(wide_ref, k + 1, once_ref, k)
        return 0

    lax.fori_loop(0, inner + 4, once, 0, unroll=2)

    def twice(k, _):
        stencil.twice(once_ref, k + 1, twice_ref, ridge_ref, k)
        return 0

    lax.fori_loop(0, inner + 2, twice, 0, unroll=2)
    for k in range(4):
        once_out_ref[0, k] = once_ref[k]
        once_out_ref[1, k] = once_ref[inner + k]
    for k in range(2):
        twice_out_ref[0, k] = twice_ref[k]
        twice_out_ref[1, k] = twice_ref[inner + k]
        ridge_out_ref[0, k] = ridge_ref[k]
        ridge_out_ref[1, k] = ridge_ref[inner + k]

    for k in range(run):
        tx_ref[k] = jnp.ones((LANES, LANES), F32)
        cx_ref[k] = jnp.zeros((LANES, LANES), F32)
    for k in range(inner):
        ty_ref[k] = jnp.ones((LANES, LANES), F32)
        cy_ref[k] = jnp.zeros((LANES, LANES), F32)
    ratio = steps[0] / steps[1]
    down = run // many_y

    def block(step, _):
        x0, y0 = (step // down) * many_x, (step % down) * many_y
        tiles = [
            stencil.features(twice_ref, ridge_ref, x0 + i + 1, y0 + j)
            for j in range(many_y)
            for i in range(many_x)
        ]
        emission, clear = network(tiles, win_ref, wout_ref, steps[1])
        for g in range(LANES // SUB):
            at = pl.ds(g * SUB, SUB)
            rays_y = [(cy_ref[x0 + i, at], ty_ref[x0 + i, at]) for i in range(many_x)]
            for j in range(many_y):
                ray_x = cx_ref[y0 + j, at], tx_ref[y0 + j, at]
                for i in range(many_x):
                    start = (j * many_x + i) * LANES + g * SUB
                    e, q = emission[start : start + SUB], clear[start : start + SUB]
                    rays_y[i] = step_ray(rays_y[i], q, e)
                    ray_x = step_ray(ray_x, clear_of_x(q, ratio), e)
                cx_ref[y0 + j, at], tx_ref[y0 + j, at] = ray_x
            for i in range(many_x):
                cy_ref[x0 + i, at], ty_ref[x0 + i, at] = rays_y[i]
        return 0

    lax.fori_loop(0, inner // many_x * down, block, 0)


def ends_kernel(
    many_y,
    counts,
    steps,
    wide_ref,
    before_ref,
    after_ref,
    win_ref,
    wout_ref,
    once_in_ref,
    twice_in_ref,
    ridge_in_ref,
    cx_ref,
    tx_ref,
    image_x_ref,
    cy_ref,
    ty_ref,
    raw_ref,
    once_ref,
    twice_ref,
    ridge_ref,
):
    half, rows, _ = wide_ref.shape
    run = cx_ref.shape[0]
    layers = LANES // 2
    stencil = Stencil(run, counts)
    part = rows // 2
    front = iota((part, LANES), 1) < layers
    for j in range(REACH):
        halo, own = before_ref[j], wide_ref[half - REACH + j]
        raw_ref[0, j, :part] = jnp.where(front, halo, roll(own[:part], layers))
        raw_ref[0, j, part:] = jnp.where(front, roll(halo, layers), roll(own[part:], layers))
        halo, own = after_ref[j], wide_ref[j]
        raw_ref[1, 2 + j, :part] = jnp.where(front, roll(own[:part], layers), roll(halo, layers))
        raw_ref[1, 2 + j, part:] = jnp.where(front, roll(own[part:], layers), halo)
    for j in range(2):
        raw_ref[0, REACH + j] = wide_ref[j]
        raw_ref[1, j] = wide_ref[half - 2 + j]
    for k in range(4):
        once_ref[0, 3 + k] = once_in_ref[0, k]
        once_ref[1, k] = once_in_ref[1, k]
    for k in range(2):
        twice_ref[0, 3 + k] = twice_in_ref[0, k]
        twice_ref[1, k] = twice_in_ref[1, k]
        ridge_ref[0, 3 + k] = ridge_in_ref[0, k]
        ridge_ref[1, k] = ridge_in_ref[1, k]
    for side, edge in enumerate((stencil.x_low, stencil.x_high)):
        outside = (0, 1) if side == 0 else (1, 2)
        for k in range(3):
            kept = edge if k in outside else None
            stencil.once(raw_ref.at[side], k + 1, once_ref.at[side], k + 4 * side, kept)
    for side, edge in enumerate((stencil.x_low, stencil.x_high)):
        for k in range(3):
            kept = edge if k == 2 * side else None
            at = k + 2 * side
            stencil.twice(once_ref.at[side], at + 1, twice_ref.at[side], ridge_ref.at[side], at, kept)

    ratio = steps[0] / steps[1]
    planes = [(0, 1), (0, 2), (0, 3), (1, 1), (1, 2), (1, 3)]
    for k in range(len(planes)):
        ty_ref[k] = jnp.ones((LANES, LANES), F32)
        cy_ref[k] = jnp.zeros((LANES, LANES), F32)

    def block(step, _):
        y0 = step * many_y
        tiles = [
            stencil.features(twice_ref.at[side], ridge_ref.at[side], k, y0 + j)
            for j in range(many_y)
            for side, k in planes
        ]
        emission, clear = network(tiles, win_ref, wout_ref, steps[1])
        images = [[], []]
        for g in range(LANES // SUB):
            at = pl.ds(g * SUB, SUB)
            rays_y = [(cy_ref[i, at], ty_ref[i, at]) for i in range(len(planes))]
            for j in range(many_y):
                ray_x = jnp.zeros((SUB, LANES), F32), jnp.ones((SUB, LANES), F32)
                for i in range(len(planes)):
                    if i == REACH:
                        colour, light = ray_x
                        colour = colour + light * cx_ref[y0 + j, at]
                        ray_x = colour, light * tx_ref[y0 + j, at]
                    start = (j * len(planes) + i) * LANES + g * SUB
                    e, q = emission[start : start + SUB], clear[start : start + SUB]
                    rays_y[i] = step_ray(rays_y[i], q, e)
                    ray_x = step_ray(ray_x, clear_of_x(q, ratio), e)
                images[0].append(ray_x[0])
                images[1].append(ray_x[1])
            for i in range(len(planes)):
                cy_ref[i, at], ty_ref[i, at] = rays_y[i]
        for d in range(layers // SUB):
            for j in range(many_y):
                near, far = d * many_y + j, (d + layers // SUB) * many_y + j
                q = images[1][near]
                image_x_ref[d, 0, y0 + j] = images[0][near] + q * images[0][far]
                image_x_ref[d, 1, y0 + j] = q * images[1][far]
        return 0

    lax.fori_loop(0, run // many_y, block, 0)


def columns_kernel(share, peers, cy_ref, ty_ref, cy_ends_ref, ty_ends_ref, *refs):
    outs, (rows_ref, turned_ref) = refs[:peers], refs[peers:]
    inner = ty_ref.shape[0]
    half = inner + 2 * REACH
    layers = LANES // 2
    for k in range(half):
        if k < REACH:
            colours, clears = cy_ends_ref[k].T, ty_ends_ref[k].T
        elif k < REACH + inner:
            colours, clears = cy_ref[k - REACH].T, ty_ref[k - REACH].T
        else:
            colours, clears = cy_ends_ref[k - inner].T, ty_ends_ref[k - inner].T
        colour, clear = colours[:SUB], clears[:SUB]
        for c in range(1, CHUNKS):
            at = slice(c * SUB, (c + 1) * SUB)
            colour = colour + clear * colours[at]
            clear = clear * clears[at]
        rows_ref[0, k * SUB : (k + 1) * SUB] = colour
        rows_ref[1, k * SUB : (k + 1) * SUB] = clear
    me = lax.axis_index("by")
    for kind in range(2):
        turned_ref[kind] = rows_ref[kind].T
        for s in range(peers):
            start = pl.multiple_of(lax.rem(me + s, peers) * share, share)
            for part in range(2):
                outs[s][kind, part] = turned_ref[kind, pl.ds(part * layers + start, share)]


def fold_y_kernel(*refs):
    pieces, out_ref = refs[:-1], refs[-1]
    peers = len(pieces)
    me = lax.axis_index("by")

    def piece(source):
        shift = lax.rem(me - source + peers, peers)
        value = pieces[0][...]
        for s in range(1, peers):
            value = jnp.where(shift == s, pieces[s][...], value)
        return value

    value = piece(0)
    colour, clear = value[0], value[1]
    for source in range(1, peers):
        value = piece(source)
        colour = colour + clear * value[0]
        clear = clear * value[1]
    out_ref[0] = colour
    out_ref[1] = clear


def fold_x_kernel(pieces_ref, out_ref):
    peers, _, run, share, _ = pieces_ref.shape
    lane = iota((share, LANES), 1)
    kinds = [[], []]
    for y in range(run):
        colour, clear = pieces_ref[0, 0, y], pieces_ref[0, 1, y]
        for k in range(1, peers):
            colour = colour + clear * pieces_ref[k, 0, y]
            clear = clear * pieces_ref[k, 1, y]
        kinds[0].append(colour)
        kinds[1].append(clear)
    for kind, values in enumerate(kinds):
        for s in (1, 2, 4):
            for i in range(run):
                if not i & s:
                    a, b = values[i], values[i | s]
                    odd = (lane & s) != 0
                    values[i] = jnp.where(odd, pltpu.roll(b, s, axis=1), a)
                    values[i | s] = jnp.where(odd, b, pltpu.roll(a, LANES - s, axis=1))
        for band, value in enumerate(values):
            out_ref[kind, band] = value


def exchange(last, first, axis):
    peers = lax.axis_size(axis)
    up = [(i, i + 1) for i in range(peers - 1)]
    down = [(j, i) for i, j in up]
    return lax.ppermute(last, axis, up), lax.ppermute(first, axis, down)


def body(scalar_field, transfer_in, transfer_out):
    layers, local_x, local_y = scalar_field.shape
    units, feats = transfer_in.shape
    channels = transfer_out.shape[0]
    bands = channels // 2
    count_x, count_y = lax.axis_size("bx"), lax.axis_size("by")
    steps = (2.0 / (local_x * count_x), 2.0 / (local_y * count_y))
    half, run, rows = local_x // 2, local_y // CHUNKS, rows_of(local_y)
    sds = lambda *shape: jax.ShapeDtypeStruct(shape, F32)
    weights = [
        jax.ShapeDtypeStruct((feats * CHUNKS, units * CHUNKS), BF16),
        jax.ShapeDtypeStruct((units * CHUNKS, channels * CHUNKS), BF16),
    ]

    edge = sds(REACH, half, LANES)
    turned, first, last = call(turn_kernel, "turn", [sds(half, rows, LANES), edge, edge], 1)(
        scalar_field
    )
    win, wout = call(weights_kernel, "weights", weights, 3)(transfer_in, transfer_out, first)
    before, after = exchange(last, first, "by")
    edge = sds(REACH, rows // 2, LANES)
    wide, first, last = call(
        functools.partial(sides_kernel, local_y), "sides", [sds(half, rows, LANES), edge, edge], 3
    )(turned, before, after)
    before, after = exchange(last, first, "bx")
    inner = half - 2 * REACH
    counts = (count_x, count_y)
    plane = lambda *lead: sds(*lead, CHUNKS, LANES)
    many_x = 5 if inner % 5 == 0 else 1
    many_y = 4 if run % 4 == 0 else 1
    once, twice, ridge, colour_x, clear_x, colour_y, clear_y = call(
        functools.partial(middle_kernel, (many_x, many_y), counts, steps),
        "middle",
        [plane(2, 4, run + 4), plane(2, 2, run + 2), plane(2, 2, run + 2)]
        + [sds(run, LANES, LANES)] * 2
        + [sds(inner, LANES, LANES)] * 2,
        3,
        [
            pltpu.VMEM((inner + 4, run + 4, CHUNKS, LANES), F32),
            pltpu.VMEM((inner + 2, run + 2, CHUNKS, LANES), F32),
            pltpu.VMEM((inner + 2, run + 2, CHUNKS, LANES), F32),
        ],
    )(wide, win, wout)
    image_x, colour_ends, clear_ends = call(
        functools.partial(ends_kernel, many_y, counts, steps),
        "ends",
        [sds(layers // SUB, 2, run, SUB, LANES)] + [sds(2 * REACH, LANES, LANES)] * 2,
        10,
        [
            pltpu.VMEM((2, 5, rows, LANES), F32),
            pltpu.VMEM((2, 7, run + 4, CHUNKS, LANES), F32),
            pltpu.VMEM((2, 5, run + 2, CHUNKS, LANES), F32),
            pltpu.VMEM((2, 5, run + 2, CHUNKS, LANES), F32),
        ],
    )(wide, before, after, win, wout, once, twice, ridge, colour_x, clear_x)

    share_x = layers // count_x
    if share_x != SUB:
        image_x = jnp.transpose(image_x, (1, 2, 0, 3, 4)).reshape(2, run, count_x, share_x, LANES)
        image_x = jnp.transpose(image_x, (2, 0, 1, 3, 4))
    pieces = lax.all_to_all(image_x, "bx", split_axis=0, concat_axis=0, tiled=True)
    view_x = call(fold_x_kernel, "fold_x", sds(2, bands, share_x, local_y), 1)(pieces)

    share = layers // count_y
    piece = sds(2, 2, share, LANES)
    scratch = [pltpu.VMEM((2, LANES, LANES), F32), pltpu.VMEM((2, LANES, LANES), F32)]
    pieces = call(
        functools.partial(columns_kernel, share, count_y), "columns", [piece] * count_y, 4, scratch
    )(colour_y, clear_y, colour_ends, clear_ends)
    pieces = list(pieces)
    for s in range(1, count_y):
        pairs = [(i, (i + s) % count_y) for i in range(count_y)]
        pieces[s] = lax.ppermute(pieces[s], "by", pairs)
    view_y = call(fold_y_kernel, "fold_y", piece, count_y)(*pieces)
    view_y = view_y.reshape(2, 2, share, half, bands)
    view_y = jnp.transpose(view_y, (0, 4, 2, 1, 3)).reshape(2, bands, share, local_x)
    return (view_x, view_y)


def solution(mesh):
    return jax.shard_map(
        body,
        mesh=mesh,
        in_specs=(P(None, "bx", "by"), P(), P()),
        out_specs=(P(None, None, "bx", "by"), P(None, None, "by", "bx")),
        check_vma=False,
    )
```

```python
import functools

import jax
import jax.numpy as jnp
from jax import lax
from jax.experimental import pallas as pl
from jax.experimental.pallas import tpu as pltpu
from jax.sharding import PartitionSpec as P

F32 = jnp.float32
BF16 = jnp.bfloat16
LOG2E = 1.4426950408889634
SUB = 8
LANES = 128
CHUNKS = 16
REACH = 3
VMEM = pl.BlockSpec(memory_space=pltpu.VMEM)
PARAMS = pltpu.CompilerParams(vmem_limit_bytes=48 * 1024 * 1024)


def call(kernel, name, outs, count, scratch=()):
    return pl.pallas_call(
        kernel,
        out_shape=outs,
        in_specs=[VMEM] * count,
        out_specs=jax.tree.map(lambda _: VMEM, outs),
        scratch_shapes=scratch,
        compiler_params=PARAMS,
        name=name,
    )


def rows_of(width):
    return -(-(width + 2 * REACH) // 16) * 16


def iota(shape, dim):
    return lax.broadcasted_iota(jnp.int32, shape, dim)


def one_hot(mask):
    return jnp.where(mask, 1.0, 0.0).astype(BF16)


def spread(weights, left, right, mask):
    inner = lax.dot_general(
        left, weights, (((1,), (1,)), ((), ())), preferred_element_type=F32
    ).astype(BF16)
    return jnp.where(mask, jnp.dot(inner, right, preferred_element_type=F32), 0.0)


def turn_kernel(field_ref, turned_ref, first_ref, last_ref):
    layers, length, width = field_ref.shape
    half = length // 2
    for k in range(half):
        turned = jnp.concatenate([field_ref[:, k, :], field_ref[:, k + half, :]], axis=0).T
        turned_ref[k, REACH : REACH + width] = turned
        for j in range(REACH):
            first_ref[j, k : k + 1] = turned[j : j + 1]
            last_ref[j, k : k + 1] = turned[width - REACH + j : width - REACH + j + 1]


def weights_kernel(in_ref, out_ref, after_ref, win_ref, wout_ref):
    del after_ref
    units, feats = in_ref.shape
    channels = out_ref.shape[0]
    bands = channels // 2
    rows, cols = feats * CHUNKS, units * CHUNKS
    left = one_hot(iota((rows, feats), 0) // CHUNKS == iota((rows, feats), 1))
    right = one_hot(iota((units, cols), 1) // CHUNKS == iota((units, cols), 0))
    mask = iota((rows, cols), 0) % CHUNKS == iota((rows, cols), 1) % CHUNKS
    win_ref[...] = (0.5 * spread(in_ref[...], left, right, mask)).astype(BF16)
    rows, cols = cols, channels * CHUNKS
    left = one_hot(iota((rows, units), 0) // CHUNKS == iota((rows, units), 1))
    at = iota((channels, cols), 1)
    right = one_hot((at // LANES) * bands + at % bands == iota((channels, cols), 0))
    mask = iota((rows, cols), 0) % CHUNKS == (iota((rows, cols), 1) % LANES) // bands
    wout_ref[...] = spread(out_ref[...], left, right, mask).astype(BF16)


def sides_kernel(rows_in, turned_ref, before_ref, after_ref, wide_ref, first_ref, last_ref):
    half, rows, _ = turned_ref.shape
    width = rows_in
    layers = LANES // 2
    part = rows // 2
    front = iota((part, LANES), 1) < layers
    for k in range(half):
        wide_ref[k, REACH : REACH + width] = turned_ref[k, REACH : REACH + width]
        for j in range(REACH):
            wide_ref[k, j : j + 1] = before_ref[j, k : k + 1]
            wide_ref[k, REACH + width + j : REACH + width + j + 1] = after_ref[j, k : k + 1]
        wide_ref[k, 2 * REACH + width :] = jnp.zeros((rows - 2 * REACH - width, LANES), F32)
    for j in range(REACH):
        top, low = wide_ref[j, :part], wide_ref[j, part:]
        first_ref[j] = jnp.where(front, top, pltpu.roll(low, layers, axis=1))
        k = half - REACH + j
        top, low = wide_ref[k, :part], wide_ref[k, part:]
        last_ref[j] = jnp.where(front, pltpu.roll(top, layers, axis=1), low)


class Stencil:
    def __init__(self, run, counts):
        self.run = run
        self.layers = layers = LANES // 2
        self.shape = (CHUNKS, LANES)
        lane, chunk = iota(self.shape, 1), iota(self.shape, 0)
        z = lane % layers
        self.near = (z > 0).astype(F32)
        self.far = (z < layers - 1).astype(F32)
        at_x, at_y = lax.axis_index("bx"), lax.axis_index("by")
        count_x, count_y = counts
        self.x_low = jnp.where((lane < layers) & (at_x == 0), 0.0, 1.0)
        self.x_high = jnp.where((lane >= layers) & (at_x == count_x - 1), 0.0, 1.0)
        self.y_low = jnp.where((chunk == 0) & (at_y == 0), 0.0, 1.0)
        self.y_high = jnp.where((chunk == CHUNKS - 1) & (at_y == count_y - 1), 0.0, 1.0)

    def z_sum(self, value):
        return roll(value, 1) * self.near + roll(value, -1) * self.far

    def inside(self, value, y, edge):
        if edge is not None:
            value = value * edge
        if y < 0:
            value = value * self.y_low
        if y >= self.run:
            value = value * self.y_high
        return value

    def smooth(self, centre, others):
        total = self.z_sum(centre)
        for other in others:
            total = total + other
        return 0.4 * centre + 0.1 * total

    def raw(self, ref, k, y):
        return ref[k, pl.ds(y + REACH, CHUNKS, stride=self.run), :]

    def once(self, raw, k, out, at, edge=None):
        column = [self.raw(raw, k, y) for y in range(-3, self.run + 3)]
        for i in range(1, len(column) - 1):
            y = i - 3
            sides = [self.raw(raw, k - 1, y), self.raw(raw, k + 1, y)]
            value = self.smooth(column[i], [column[i - 1], column[i + 1]] + sides)
            out[at, i - 1] = self.inside(value, y, edge)

    def twice(self, once, k, out, ridge, at, edge=None):
        column = [once[k, i] for i in range(self.run + 4)]
        for i in range(1, len(column) - 1):
            sides = [once[k - 1, i], once[k + 1, i]]
            value = self.smooth(column[i], [column[i - 1], column[i + 1]] + sides)
            value = self.inside(value, i - 2, edge)
            out[at, i - 1] = value
            ridge[at, i - 1] = 2.0 * value + self.z_sum(value)

    def features(self, twice, ridge, k, y):
        p = lambda a, b: twice[k + a, y + 1 + b]
        r = lambda a, b: ridge[k + a, y + 1 + b]
        centre = p(0, 0)
        main, cross = p(1, 1) - p(-1, -1), p(1, -1) - p(-1, 1)
        third = 1.0 / 3.0
        gx = (main + cross + (r(1, 0) - r(-1, 0))) * third
        gy = (main - cross + (r(0, 1) - r(0, -1))) * third
        around = 2.0 * centre + ((p(1, 0) + p(-1, 0)) + (p(0, 1) + p(0, -1)))
        gz = (roll(around, -1) * self.far - roll(around, 1) * self.near) * third
        m = jnp.sqrt(1.0 + gx * gx + gy * gy + gz * gz)
        parts = [centre, gx, gy, gz, m, centre * m, centre * centre]
        packed = [part.astype(BF16) for part in parts] + [jnp.ones(self.shape, BF16)]
        return jnp.concatenate(packed, axis=0).T


def roll(value, shift):
    return pltpu.roll(value, shift % LANES, axis=1)


def network(tiles, win_ref, wout_ref, step):
    cells = jnp.concatenate(tiles, axis=0)
    half_v = jnp.dot(cells, win_ref[...], preferred_element_type=F32)
    hidden = (half_v + half_v * jnp.tanh(half_v)).astype(BF16)
    v = jnp.dot(hidden, wout_ref[...], preferred_element_type=F32)
    soft = jnp.maximum(v, jnp.log(1.0 + jnp.exp2(jnp.minimum(v * LOG2E, 126.0))))
    return soft[:, :LANES], jnp.exp2(soft[:, LANES:] * (-LOG2E * step))


def clear_of_x(q, ratio):
    if ratio == 1.0:
        return q
    if ratio == 2.0:
        return q * q
    return jnp.exp2(jnp.log(q) * (LOG2E * ratio))


def step_ray(ray, clear, emission):
    colour, light = ray
    later = light * clear
    return colour + (light - later) * emission, later


def middle_kernel(
    spans,
    counts,
    steps,
    wide_ref,
    win_ref,
    wout_ref,
    once_out_ref,
    twice_out_ref,
    ridge_out_ref,
    cx_ref,
    tx_ref,
    cy_ref,
    ty_ref,
    once_ref,
    twice_ref,
    ridge_ref,
):
    half = wide_ref.shape[0]
    run = cx_ref.shape[0]
    stencil = Stencil(run, counts)
    many_x, many_y = spans
    inner = half - 2 * REACH

    for k in range(inner + 4):
        stencil.once(wide_ref, k + 1, once_ref, k)
    for k in range(inner + 2):
        stencil.twice(once_ref, k + 1, twice_ref, ridge_ref, k)
    for k in range(4):
        once_out_ref[0, k] = once_ref[k]
        once_out_ref[1, k] = once_ref[inner + k]
    for k in range(2):
        twice_out_ref[0, k] = twice_ref[k]
        twice_out_ref[1, k] = twice_ref[inner + k]
        ridge_out_ref[0, k] = ridge_ref[k]
        ridge_out_ref[1, k] = ridge_ref[inner + k]

    for k in range(run):
        tx_ref[k] = jnp.ones((LANES, LANES), F32)
        cx_ref[k] = jnp.zeros((LANES, LANES), F32)
    for k in range(inner):
        ty_ref[k] = jnp.ones((LANES, LANES), F32)
        cy_ref[k] = jnp.zeros((LANES, LANES), F32)
    ratio = steps[0] / steps[1]
    down = run // many_y

    def block(step):
        x0, y0 = (step // down) * many_x, (step % down) * many_y
        tiles = [
            stencil.features(twice_ref, ridge_ref, x0 + i + 1, y0 + j)
            for j in range(many_y)
            for i in range(many_x)
        ]
        emission, clear = network(tiles, win_ref, wout_ref, steps[1])
        for g in range(LANES // SUB):
            at = pl.ds(g * SUB, SUB)
            rays_y = [(cy_ref[x0 + i, at], ty_ref[x0 + i, at]) for i in range(many_x)]
            for j in range(many_y):
                ray_x = cx_ref[y0 + j, at], tx_ref[y0 + j, at]
                for i in range(many_x):
                    start = (j * many_x + i) * LANES + g * SUB
                    e, q = emission[start : start + SUB], clear[start : start + SUB]
                    rays_y[i] = step_ray(rays_y[i], q, e)
                    ray_x = step_ray(ray_x, clear_of_x(q, ratio), e)
                cx_ref[y0 + j, at], tx_ref[y0 + j, at] = ray_x
            for i in range(many_x):
                cy_ref[x0 + i, at], ty_ref[x0 + i, at] = rays_y[i]

    for step in range(inner // many_x * down):
        block(step)


def ends_kernel(
    many_y,
    counts,
    steps,
    wide_ref,
    before_ref,
    after_ref,
    win_ref,
    wout_ref,
    once_in_ref,
    twice_in_ref,
    ridge_in_ref,
    cx_ref,
    tx_ref,
    image_x_ref,
    cy_ref,
    ty_ref,
    raw_ref,
    once_ref,
    twice_ref,
    ridge_ref,
):
    half, rows, _ = wide_ref.shape
    run = cx_ref.shape[0]
    layers = LANES // 2
    stencil = Stencil(run, counts)
    part = rows // 2
    front = iota((part, LANES), 1) < layers
    for j in range(REACH):
        halo, own = before_ref[j], wide_ref[half - REACH + j]
        raw_ref[0, j, :part] = jnp.where(front, halo, roll(own[:part], layers))
        raw_ref[0, j, part:] = jnp.where(front, roll(halo, layers), roll(own[part:], layers))
        halo, own = after_ref[j], wide_ref[j]
        raw_ref[1, 2 + j, :part] = jnp.where(front, roll(own[:part], layers), roll(halo, layers))
        raw_ref[1, 2 + j, part:] = jnp.where(front, roll(own[part:], layers), halo)
    for j in range(2):
        raw_ref[0, REACH + j] = wide_ref[j]
        raw_ref[1, j] = wide_ref[half - 2 + j]
    for k in range(4):
        once_ref[0, 3 + k] = once_in_ref[0, k]
        once_ref[1, k] = once_in_ref[1, k]
    for k in range(2):
        twice_ref[0, 3 + k] = twice_in_ref[0, k]
        twice_ref[1, k] = twice_in_ref[1, k]
        ridge_ref[0, 3 + k] = ridge_in_ref[0, k]
        ridge_ref[1, k] = ridge_in_ref[1, k]
    for side, edge in enumerate((stencil.x_low, stencil.x_high)):
        outside = (0, 1) if side == 0 else (1, 2)
        for k in range(3):
            kept = edge if k in outside else None
            stencil.once(raw_ref.at[side], k + 1, once_ref.at[side], k + 4 * side, kept)
    for side, edge in enumerate((stencil.x_low, stencil.x_high)):
        for k in range(3):
            kept = edge if k == 2 * side else None
            at = k + 2 * side
            stencil.twice(once_ref.at[side], at + 1, twice_ref.at[side], ridge_ref.at[side], at, kept)

    ratio = steps[0] / steps[1]
    planes = [(0, 1), (0, 2), (0, 3), (1, 1), (1, 2), (1, 3)]
    for k in range(len(planes)):
        ty_ref[k] = jnp.ones((LANES, LANES), F32)
        cy_ref[k] = jnp.zeros((LANES, LANES), F32)

    def block(step):
        y0 = step * many_y
        tiles = [
            stencil.features(twice_ref.at[side], ridge_ref.at[side], k, y0 + j)
            for j in range(many_y)
            for side, k in planes
        ]
        emission, clear = network(tiles, win_ref, wout_ref, steps[1])
        images = [[], []]
        for g in range(LANES // SUB):
            at = pl.ds(g * SUB, SUB)
            rays_y = [(cy_ref[i, at], ty_ref[i, at]) for i in range(len(planes))]
            for j in range(many_y):
                ray_x = jnp.zeros((SUB, LANES), F32), jnp.ones((SUB, LANES), F32)
                for i in range(len(planes)):
                    if i == REACH:
                        colour, light = ray_x
                        colour = colour + light * cx_ref[y0 + j, at]
                        ray_x = colour, light * tx_ref[y0 + j, at]
                    start = (j * len(planes) + i) * LANES + g * SUB
                    e, q = emission[start : start + SUB], clear[start : start + SUB]
                    rays_y[i] = step_ray(rays_y[i], q, e)
                    ray_x = step_ray(ray_x, clear_of_x(q, ratio), e)
                images[0].append(ray_x[0])
                images[1].append(ray_x[1])
            for i in range(len(planes)):
                cy_ref[i, at], ty_ref[i, at] = rays_y[i]
        for d in range(layers // SUB):
            for j in range(many_y):
                near, far = d * many_y + j, (d + layers // SUB) * many_y + j
                q = images[1][near]
                image_x_ref[d, 0, y0 + j] = images[0][near] + q * images[0][far]
                image_x_ref[d, 1, y0 + j] = q * images[1][far]

    for step in range(run // many_y):
        block(step)


def columns_kernel(share, peers, cy_ref, ty_ref, cy_ends_ref, ty_ends_ref, *refs):
    outs, (rows_ref, turned_ref) = refs[:peers], refs[peers:]
    inner = ty_ref.shape[0]
    half = inner + 2 * REACH
    layers = LANES // 2
    for k in range(half):
        if k < REACH:
            colours, clears = cy_ends_ref[k].T, ty_ends_ref[k].T
        elif k < REACH + inner:
            colours, clears = cy_ref[k - REACH].T, ty_ref[k - REACH].T
        else:
            colours, clears = cy_ends_ref[k - inner].T, ty_ends_ref[k - inner].T
        colour, clear = colours[:SUB], clears[:SUB]
        for c in range(1, CHUNKS):
            at = slice(c * SUB, (c + 1) * SUB)
            colour = colour + clear * colours[at]
            clear = clear * clears[at]
        rows_ref[0, k * SUB : (k + 1) * SUB] = colour
        rows_ref[1, k * SUB : (k + 1) * SUB] = clear
    me = lax.axis_index("by")
    for kind in range(2):
        turned_ref[kind] = rows_ref[kind].T
        for s in range(peers):
            start = pl.multiple_of(lax.rem(me + s, peers) * share, share)
            for part in range(2):
                outs[s][kind, part] = turned_ref[kind, pl.ds(part * layers + start, share)]


def fold_y_kernel(*refs):
    pieces, out_ref = refs[:-1], refs[-1]
    peers = len(pieces)
    me = lax.axis_index("by")

    def piece(source):
        shift = lax.rem(me - source + peers, peers)
        value = pieces[0][...]
        for s in range(1, peers):
            value = jnp.where(shift == s, pieces[s][...], value)
        return value

    value = piece(0)
    colour, clear = value[0], value[1]
    for source in range(1, peers):
        value = piece(source)
        colour = colour + clear * value[0]
        clear = clear * value[1]
    out_ref[0] = colour
    out_ref[1] = clear


def fold_x_kernel(pieces_ref, out_ref):
    peers, _, run, share, _ = pieces_ref.shape
    lane = iota((share, LANES), 1)
    kinds = [[], []]
    for y in range(run):
        colour, clear = pieces_ref[0, 0, y], pieces_ref[0, 1, y]
        for k in range(1, peers):
            colour = colour + clear * pieces_ref[k, 0, y]
            clear = clear * pieces_ref[k, 1, y]
        kinds[0].append(colour)
        kinds[1].append(clear)
    for kind, values in enumerate(kinds):
        for s in (1, 2, 4):
            for i in range(run):
                if not i & s:
                    a, b = values[i], values[i | s]
                    odd = (lane & s) != 0
                    values[i] = jnp.where(odd, pltpu.roll(b, s, axis=1), a)
                    values[i | s] = jnp.where(odd, b, pltpu.roll(a, LANES - s, axis=1))
        for band, value in enumerate(values):
            out_ref[kind, band] = value


def exchange(last, first, axis):
    peers = lax.axis_size(axis)
    up = [(i, i + 1) for i in range(peers - 1)]
    down = [(j, i) for i, j in up]
    return lax.ppermute(last, axis, up), lax.ppermute(first, axis, down)


def body(scalar_field, transfer_in, transfer_out):
    layers, local_x, local_y = scalar_field.shape
    units, feats = transfer_in.shape
    channels = transfer_out.shape[0]
    bands = channels // 2
    count_x, count_y = lax.axis_size("bx"), lax.axis_size("by")
    steps = (2.0 / (local_x * count_x), 2.0 / (local_y * count_y))
    half, run, rows = local_x // 2, local_y // CHUNKS, rows_of(local_y)
    sds = lambda *shape: jax.ShapeDtypeStruct(shape, F32)
    weights = [
        jax.ShapeDtypeStruct((feats * CHUNKS, units * CHUNKS), BF16),
        jax.ShapeDtypeStruct((units * CHUNKS, channels * CHUNKS), BF16),
    ]

    edge = sds(REACH, half, LANES)
    turned, first, last = call(turn_kernel, "turn", [sds(half, rows, LANES), edge, edge], 1)(
        scalar_field
    )
    win, wout = call(weights_kernel, "weights", weights, 3)(transfer_in, transfer_out, first)
    before, after = exchange(last, first, "by")
    edge = sds(REACH, rows // 2, LANES)
    wide, first, last = call(
        functools.partial(sides_kernel, local_y), "sides", [sds(half, rows, LANES), edge, edge], 3
    )(turned, before, after)
    before, after = exchange(last, first, "bx")
    inner = half - 2 * REACH
    counts = (count_x, count_y)
    plane = lambda *lead: sds(*lead, CHUNKS, LANES)
    many_x, many_y = inner, 2
    once, twice, ridge, colour_x, clear_x, colour_y, clear_y = call(
        functools.partial(middle_kernel, (many_x, many_y), counts, steps),
        "middle",
        [plane(2, 4, run + 4), plane(2, 2, run + 2), plane(2, 2, run + 2)]
        + [sds(run, LANES, LANES)] * 2
        + [sds(inner, LANES, LANES)] * 2,
        3,
        [
            pltpu.VMEM((inner + 4, run + 4, CHUNKS, LANES), F32),
            pltpu.VMEM((inner + 2, run + 2, CHUNKS, LANES), F32),
            pltpu.VMEM((inner + 2, run + 2, CHUNKS, LANES), F32),
        ],
    )(wide, win, wout)
    image_x, colour_ends, clear_ends = call(
        functools.partial(ends_kernel, many_y, counts, steps),
        "ends",
        [sds(layers // SUB, 2, run, SUB, LANES)] + [sds(2 * REACH, LANES, LANES)] * 2,
        10,
        [
            pltpu.VMEM((2, 5, rows, LANES), F32),
            pltpu.VMEM((2, 7, run + 4, CHUNKS, LANES), F32),
            pltpu.VMEM((2, 5, run + 2, CHUNKS, LANES), F32),
            pltpu.VMEM((2, 5, run + 2, CHUNKS, LANES), F32),
        ],
    )(wide, before, after, win, wout, once, twice, ridge, colour_x, clear_x)

    share_x = layers // count_x
    if share_x != SUB:
        image_x = jnp.transpose(image_x, (1, 2, 0, 3, 4)).reshape(2, run, count_x, share_x, LANES)
        image_x = jnp.transpose(image_x, (2, 0, 1, 3, 4))
    pieces = lax.all_to_all(image_x, "bx", split_axis=0, concat_axis=0, tiled=True)
    view_x = call(fold_x_kernel, "fold_x", sds(2, bands, share_x, local_y), 1)(pieces)

    share = layers // count_y
    piece = sds(2, 2, share, LANES)
    scratch = [pltpu.VMEM((2, LANES, LANES), F32), pltpu.VMEM((2, LANES, LANES), F32)]
    pieces = call(
        functools.partial(columns_kernel, share, count_y), "columns", [piece] * count_y, 4, scratch
    )(colour_y, clear_y, colour_ends, clear_ends)
    pieces = list(pieces)
    for s in range(1, count_y):
        pairs = [(i, (i + s) % count_y) for i in range(count_y)]
        pieces[s] = lax.ppermute(pieces[s], "by", pairs)
    view_y = call(fold_y_kernel, "fold_y", piece, count_y)(*pieces)
    view_y = view_y.reshape(2, 2, share, half, bands)
    view_y = jnp.transpose(view_y, (0, 4, 2, 1, 3)).reshape(2, bands, share, local_x)
    return (view_x, view_y)


def solution(mesh):
    return jax.shard_map(
        body,
        mesh=mesh,
        in_specs=(P(None, "bx", "by"), P(), P()),
        out_specs=(P(None, None, "bx", "by"), P(None, None, "by", "bx")),
        check_vma=False,
    )
```

```python
import functools

import jax
import jax.numpy as jnp
from jax import lax
from jax.experimental import pallas as pl
from jax.experimental.pallas import tpu as pltpu
from jax.sharding import PartitionSpec as P

F32 = jnp.float32
BF16 = jnp.bfloat16
LOG2E = 1.4426950408889634
SUB = 8
LANES = 128
CHUNKS = 16
REACH = 3
VMEM = pl.BlockSpec(memory_space=pltpu.VMEM)
PARAMS = pltpu.CompilerParams(vmem_limit_bytes=48 * 1024 * 1024)


def call(kernel, name, outs, count, scratch=()):
    return pl.pallas_call(
        kernel,
        out_shape=outs,
        in_specs=[VMEM] * count,
        out_specs=jax.tree.map(lambda _: VMEM, outs),
        scratch_shapes=scratch,
        compiler_params=PARAMS,
        name=name,
    )


def rows_of(width):
    return -(-(width + 2 * REACH) // 16) * 16


def iota(shape, dim):
    return lax.broadcasted_iota(jnp.int32, shape, dim)


def one_hot(mask):
    return jnp.where(mask, 1.0, 0.0).astype(BF16)


def spread(weights, left, right, mask):
    inner = lax.dot_general(
        left, weights, (((1,), (1,)), ((), ())), preferred_element_type=F32
    ).astype(BF16)
    return jnp.where(mask, jnp.dot(inner, right, preferred_element_type=F32), 0.0)


def turn_kernel(field_hbm, turned_ref, first_ref, last_ref, field_ref, arrived):
    layers, length, width = field_ref.shape
    half = length // 2
    copies = []
    for i in range(length // SUB):
        part = (slice(None), pl.ds(i * SUB, SUB))
        copies.append(
            pltpu.make_async_copy(field_hbm.at[part], field_ref.at[part], arrived.at[i])
        )
    order = [i for k in range(half // SUB) for i in (k, k + half // SUB)]
    for i in order:
        copies[i].start()
    for k in range(half):
        if k % SUB == 0:
            copies[k // SUB].wait()
            copies[(k + half) // SUB].wait()
        turned = jnp.concatenate([field_ref[:, k, :], field_ref[:, k + half, :]], axis=0).T
        turned_ref[k, REACH : REACH + width] = turned
        for j in range(REACH):
            first_ref[j, k : k + 1] = turned[j : j + 1]
            last_ref[j, k : k + 1] = turned[width - REACH + j : width - REACH + j + 1]


def spread_weights(in_ref, out_ref, win_ref, wout_ref):
    units, feats = in_ref.shape
    channels = out_ref.shape[0]
    bands = channels // 2
    rows, cols = feats * CHUNKS, units * CHUNKS
    left = one_hot(iota((rows, feats), 0) // CHUNKS == iota((rows, feats), 1))
    right = one_hot(iota((units, cols), 1) // CHUNKS == iota((units, cols), 0))
    mask = iota((rows, cols), 0) % CHUNKS == iota((rows, cols), 1) % CHUNKS
    win_ref[...] = (0.5 * spread(in_ref[...], left, right, mask)).astype(BF16)
    rows, cols = cols, channels * CHUNKS
    left = one_hot(iota((rows, units), 0) // CHUNKS == iota((rows, units), 1))
    at = iota((channels, cols), 1)
    right = one_hot((at // LANES) * bands + at % bands == iota((channels, cols), 0))
    mask = iota((rows, cols), 0) % CHUNKS == (iota((rows, cols), 1) % LANES) // bands
    wout_ref[...] = spread(out_ref[...], left, right, mask).astype(BF16)


def sides_kernel(width, count_y, turned_ref, before_ref, after_ref, wide_ref, first_ref, last_ref):
    half, rows, _ = turned_ref.shape
    layers = LANES // 2
    part = rows // 2
    front = iota((part, LANES), 1) < layers
    at_y = lax.axis_index("by")
    keep_low = jnp.where(at_y == 0, 0.0, 1.0)
    keep_high = jnp.where(at_y == count_y - 1, 0.0, 1.0)
    for k in range(half):
        wide_ref[k, REACH : REACH + width] = turned_ref[k, REACH : REACH + width]
        for j in range(REACH):
            at = REACH + width + j
            wide_ref[k, j : j + 1] = before_ref[j, k : k + 1] * keep_low
            wide_ref[k, at : at + 1] = after_ref[j, k : k + 1] * keep_high
        wide_ref[k, 2 * REACH + width :] = jnp.zeros((rows - 2 * REACH - width, LANES), F32)
    for j in range(REACH):
        top, low = wide_ref[j, :part], wide_ref[j, part:]
        first_ref[j] = jnp.where(front, top, pltpu.roll(low, layers, axis=1))
        k = half - REACH + j
        top, low = wide_ref[k, :part], wide_ref[k, part:]
        last_ref[j] = jnp.where(front, pltpu.roll(top, layers, axis=1), low)


class Stencil:
    def __init__(self, run, counts):
        self.run = run
        self.layers = layers = LANES // 2
        self.shape = (CHUNKS, LANES)
        lane, chunk = iota(self.shape, 1), iota(self.shape, 0)
        z = lane % layers
        self.near = (z > 0).astype(F32)
        self.far = (z < layers - 1).astype(F32)
        at_x, at_y = lax.axis_index("bx"), lax.axis_index("by")
        count_x, count_y = counts
        self.x_low = jnp.where((lane < layers) & (at_x == 0), 0.0, 1.0)
        self.x_high = jnp.where((lane >= layers) & (at_x == count_x - 1), 0.0, 1.0)
        self.y_low = jnp.where((chunk == 0) & (at_y == 0), 0.0, 1.0)
        self.y_high = jnp.where((chunk == CHUNKS - 1) & (at_y == count_y - 1), 0.0, 1.0)

    def z_sum(self, value):
        return roll(value, 1) * self.near + roll(value, -1) * self.far

    def inside(self, value, y, edge):
        if edge is not None:
            value = value * edge
        if y < 0:
            value = value * self.y_low
        if y >= self.run:
            value = value * self.y_high
        return value

    def smooth(self, centre, others):
        total = self.z_sum(centre)
        for other in others:
            total = total + other
        return 0.4 * centre + 0.1 * total

    def raw(self, ref, k, y):
        return ref[k, pl.ds(y + REACH, CHUNKS, stride=self.run), :]

    def once(self, raw, k, out, at, edge=None):
        column = [self.raw(raw, k, y) for y in range(-3, self.run + 3)]
        for i in range(1, len(column) - 1):
            y = i - 3
            sides = [self.raw(raw, k - 1, y), self.raw(raw, k + 1, y)]
            value = self.smooth(column[i], [column[i - 1], column[i + 1]] + sides)
            out[at, i - 1] = self.inside(value, y, edge)

    def twice(self, once, k, out, ridge, at, edge=None):
        column = [once[k, i] for i in range(self.run + 4)]
        for i in range(1, len(column) - 1):
            sides = [once[k - 1, i], once[k + 1, i]]
            value = self.smooth(column[i], [column[i - 1], column[i + 1]] + sides)
            value = self.inside(value, i - 2, edge)
            out[at, i - 1] = value
            ridge[at, i - 1] = 2.0 * value + self.z_sum(value)

    def features(self, twice, ridge, k, y):
        p = lambda a, b: twice[k + a, y + 1 + b]
        r = lambda a, b: ridge[k + a, y + 1 + b]
        centre = p(0, 0)
        main, cross = p(1, 1) - p(-1, -1), p(1, -1) - p(-1, 1)
        third = 1.0 / 3.0
        gx = (main + cross + (r(1, 0) - r(-1, 0))) * third
        gy = (main - cross + (r(0, 1) - r(0, -1))) * third
        around = 2.0 * centre + ((p(1, 0) + p(-1, 0)) + (p(0, 1) + p(0, -1)))
        gz = (roll(around, -1) * self.far - roll(around, 1) * self.near) * third
        m = jnp.sqrt(1.0 + gx * gx + gy * gy + gz * gz)
        parts = [centre, gx, gy, gz, m, centre * m, centre * centre]
        packed = [part.astype(BF16) for part in parts] + [jnp.ones(self.shape, BF16)]
        return jnp.concatenate(packed, axis=0).T


def roll(value, shift):
    return pltpu.roll(value, shift % LANES, axis=1)


def network(tiles, win_ref, wout_ref, step):
    cells = jnp.concatenate(tiles, axis=0)
    half_v = jnp.dot(cells, win_ref[...], preferred_element_type=F32)
    hidden = (half_v + half_v * jnp.tanh(half_v)).astype(BF16)
    v = jnp.dot(hidden, wout_ref[...], preferred_element_type=F32)
    soft = jnp.maximum(v, jnp.log(1.0 + jnp.exp2(jnp.minimum(v * LOG2E, 126.0))))
    return soft[:, :LANES], jnp.exp2(soft[:, LANES:] * (-LOG2E * step))


def clear_of_x(q, ratio):
    if ratio == 1.0:
        return q
    if ratio == 2.0:
        return q * q
    return jnp.exp2(jnp.log(q) * (LOG2E * ratio))


def step_ray(ray, clear, emission):
    colour, light = ray
    later = light * clear
    return colour + (light - later) * emission, later


def middle_kernel(
    spans,
    counts,
    steps,
    wide_ref,
    in_ref,
    out_ref,
    win_ref,
    wout_ref,
    once_out_ref,
    twice_out_ref,
    ridge_out_ref,
    cx_ref,
    tx_ref,
    cy_ref,
    ty_ref,
    once_ref,
    twice_ref,
    ridge_ref,
):
    half = wide_ref.shape[0]
    run = cx_ref.shape[0]
    stencil = Stencil(run, counts)
    many_x, many_y = spans
    inner = half - 2 * REACH
    spread_weights(in_ref, out_ref, win_ref, wout_ref)
    for k in range(inner + 4):
        stencil.once(wide_ref, k + 1, once_ref, k)
    for k in range(inner + 2):
        stencil.twice(once_ref, k + 1, twice_ref, ridge_ref, k)
    for k in range(4):
        once_out_ref[0, k] = once_ref[k]
        once_out_ref[1, k] = once_ref[inner + k]
    for k in range(2):
        twice_out_ref[0, k] = twice_ref[k]
        twice_out_ref[1, k] = twice_ref[inner + k]
        ridge_out_ref[0, k] = ridge_ref[k]
        ridge_out_ref[1, k] = ridge_ref[inner + k]

    for k in range(run):
        tx_ref[k] = jnp.ones((LANES, LANES), F32)
        cx_ref[k] = jnp.zeros((LANES, LANES), F32)
    for k in range(inner):
        ty_ref[k] = jnp.ones((LANES, LANES), F32)
        cy_ref[k] = jnp.zeros((LANES, LANES), F32)
    ratio = steps[0] / steps[1]
    down = run // many_y

    def block(step):
        x0, y0 = (step // down) * many_x, (step % down) * many_y
        tiles = [
            stencil.features(twice_ref, ridge_ref, x0 + i + 1, y0 + j)
            for j in range(many_y)
            for i in range(many_x)
        ]
        emission, clear = network(tiles, win_ref, wout_ref, steps[1])
        for g in range(LANES // SUB):
            at = pl.ds(g * SUB, SUB)
            rays_y = [(cy_ref[x0 + i, at], ty_ref[x0 + i, at]) for i in range(many_x)]
            for j in range(many_y):
                ray_x = cx_ref[y0 + j, at], tx_ref[y0 + j, at]
                for i in range(many_x):
                    start = (j * many_x + i) * LANES + g * SUB
                    e, q = emission[start : start + SUB], clear[start : start + SUB]
                    rays_y[i] = step_ray(rays_y[i], q, e)
                    ray_x = step_ray(ray_x, clear_of_x(q, ratio), e)
                cx_ref[y0 + j, at], tx_ref[y0 + j, at] = ray_x
            for i in range(many_x):
                cy_ref[x0 + i, at], ty_ref[x0 + i, at] = rays_y[i]

    for step in range(inner // many_x * down):
        block(step)


def ends_kernel(
    many_y,
    counts,
    steps,
    wide_ref,
    before_ref,
    after_ref,
    win_ref,
    wout_ref,
    once_in_ref,
    twice_in_ref,
    ridge_in_ref,
    cx_ref,
    tx_ref,
    cy_ref,
    ty_ref,
    *refs,
):
    outs, (image_ref, raw_ref, once_ref, twice_ref, ridge_ref) = refs[: counts[0]], refs[counts[0] :]
    half, rows, _ = wide_ref.shape
    run = cx_ref.shape[0]
    layers = LANES // 2
    stencil = Stencil(run, counts)
    part = rows // 2
    front = iota((part, LANES), 1) < layers
    at_x = lax.axis_index("bx")
    keep_low = jnp.where(at_x == 0, 0.0, 1.0)
    keep_high = jnp.where(at_x == counts[0] - 1, 0.0, 1.0)
    for j in range(REACH):
        halo, own = before_ref[j] * keep_low, wide_ref[half - REACH + j]
        raw_ref[0, j, :part] = jnp.where(front, halo, roll(own[:part], layers))
        raw_ref[0, j, part:] = jnp.where(front, roll(halo, layers), roll(own[part:], layers))
        halo, own = after_ref[j] * keep_high, wide_ref[j]
        raw_ref[1, 2 + j, :part] = jnp.where(front, roll(own[:part], layers), roll(halo, layers))
        raw_ref[1, 2 + j, part:] = jnp.where(front, roll(own[part:], layers), halo)
    for j in range(2):
        raw_ref[0, REACH + j] = wide_ref[j]
        raw_ref[1, j] = wide_ref[half - 2 + j]
    for k in range(4):
        once_ref[0, 3 + k] = once_in_ref[0, k]
        once_ref[1, k] = once_in_ref[1, k]
    for k in range(2):
        twice_ref[0, 3 + k] = twice_in_ref[0, k]
        twice_ref[1, k] = twice_in_ref[1, k]
        ridge_ref[0, 3 + k] = ridge_in_ref[0, k]
        ridge_ref[1, k] = ridge_in_ref[1, k]
    for side, edge in enumerate((stencil.x_low, stencil.x_high)):
        outside = (0, 1) if side == 0 else (1, 2)
        for k in range(3):
            kept = edge if k in outside else None
            stencil.once(raw_ref.at[side], k + 1, once_ref.at[side], k + 4 * side, kept)
    for side, edge in enumerate((stencil.x_low, stencil.x_high)):
        for k in range(3):
            kept = edge if k == 2 * side else None
            at = k + 2 * side
            stencil.twice(once_ref.at[side], at + 1, twice_ref.at[side], ridge_ref.at[side], at, kept)

    ratio = steps[0] / steps[1]
    planes = [(0, 1), (0, 2), (0, 3), (1, 1), (1, 2), (1, 3)]
    for k in range(len(planes)):
        ty_ref[k] = jnp.ones((LANES, LANES), F32)
        cy_ref[k] = jnp.zeros((LANES, LANES), F32)

    def block(step):
        y0 = step * many_y
        tiles = [
            stencil.features(twice_ref.at[side], ridge_ref.at[side], k, y0 + j)
            for j in range(many_y)
            for side, k in planes
        ]
        emission, clear = network(tiles, win_ref, wout_ref, steps[1])
        images = [[], []]
        for g in range(LANES // SUB):
            at = pl.ds(g * SUB, SUB)
            rays_y = [(cy_ref[i, at], ty_ref[i, at]) for i in range(len(planes))]
            for j in range(many_y):
                ray_x = jnp.zeros((SUB, LANES), F32), jnp.ones((SUB, LANES), F32)
                for i in range(len(planes)):
                    if i == REACH:
                        colour, light = ray_x
                        colour = colour + light * cx_ref[y0 + j, at]
                        ray_x = colour, light * tx_ref[y0 + j, at]
                    start = (j * len(planes) + i) * LANES + g * SUB
                    e, q = emission[start : start + SUB], clear[start : start + SUB]
                    rays_y[i] = step_ray(rays_y[i], q, e)
                    ray_x = step_ray(ray_x, clear_of_x(q, ratio), e)
                images[0].append(ray_x[0])
                images[1].append(ray_x[1])
            for i in range(len(planes)):
                cy_ref[i, at], ty_ref[i, at] = rays_y[i]
        for d in range(layers // SUB):
            for j in range(many_y):
                near, far = d * many_y + j, (d + layers // SUB) * many_y + j
                q = images[1][near]
                at = pl.ds(d * SUB, SUB)
                image_ref[0, y0 + j, at] = images[0][near] + q * images[0][far]
                image_ref[1, y0 + j, at] = q * images[1][far]

    for step in range(run // many_y):
        block(step)
    share = layers // counts[0]
    for s, out_ref in enumerate(outs):
        start = pl.multiple_of(lax.rem(at_x + s, counts[0]) * share, share)
        out_ref[...] = image_ref[:, :, pl.ds(start, share), :]


def columns_kernel(share, peers, cy_ref, ty_ref, cy_ends_ref, ty_ends_ref, *refs):
    outs, (rows_ref, turned_ref) = refs[:peers], refs[peers:]
    inner = ty_ref.shape[0]
    half = inner + 2 * REACH
    layers = LANES // 2
    for k in range(half):
        if k < REACH:
            colours, clears = cy_ends_ref[k].T, ty_ends_ref[k].T
        elif k < REACH + inner:
            colours, clears = cy_ref[k - REACH].T, ty_ref[k - REACH].T
        else:
            colours, clears = cy_ends_ref[k - inner].T, ty_ends_ref[k - inner].T
        colour, clear = colours[:SUB], clears[:SUB]
        for c in range(1, CHUNKS):
            at = slice(c * SUB, (c + 1) * SUB)
            colour = colour + clear * colours[at]
            clear = clear * clears[at]
        rows_ref[0, k * SUB : (k + 1) * SUB] = colour
        rows_ref[1, k * SUB : (k + 1) * SUB] = clear
    me = lax.axis_index("by")
    for kind in range(2):
        turned_ref[kind] = rows_ref[kind].T
        for s in range(peers):
            start = pl.multiple_of(lax.rem(me + s, peers) * share, share)
            for part in range(2):
                outs[s][kind, part] = turned_ref[kind, pl.ds(part * layers + start, share)]


def fold_y_kernel(*refs):
    pieces, out_ref = refs[:-1], refs[-1]
    peers = len(pieces)
    me = lax.axis_index("by")

    def piece(source):
        shift = lax.rem(me - source + peers, peers)
        value = pieces[0][...]
        for s in range(1, peers):
            value = jnp.where(shift == s, pieces[s][...], value)
        return value

    value = piece(0)
    colour, clear = value[0], value[1]
    for source in range(1, peers):
        value = piece(source)
        colour = colour + clear * value[0]
        clear = clear * value[1]
    out_ref[0] = colour
    out_ref[1] = clear


def fold_x_kernel(*refs):
    pieces, out_ref = refs[:-1], refs[-1]
    _, run, share, _ = pieces[0].shape
    lane = iota((share, LANES), 1)
    me = lax.axis_index("bx")
    kinds = [[], []]
    for y in range(run):
        behind = colour, clear = jnp.zeros((share, LANES), F32), jnp.ones((share, LANES), F32)
        for s in reversed(range(len(pieces))):
            start = me == s
            behind = jnp.where(start, colour, behind[0]), jnp.where(start, clear, behind[1])
            colour, clear = jnp.where(start, 0.0, colour), jnp.where(start, 1.0, clear)
            colour = colour + clear * pieces[s][0, y]
            clear = clear * pieces[s][1, y]
        kinds[0].append(colour + clear * behind[0])
        kinds[1].append(clear * behind[1])
    for kind, values in enumerate(kinds):
        for s in (1, 2, 4):
            for i in range(run):
                if not i & s:
                    a, b = values[i], values[i | s]
                    odd = (lane & s) != 0
                    values[i] = jnp.where(odd, pltpu.roll(b, s, axis=1), a)
                    values[i | s] = jnp.where(odd, b, pltpu.roll(a, LANES - s, axis=1))
        for band, value in enumerate(values):
            out_ref[kind, band] = value


def exchange(last, first, axis):
    peers = lax.axis_size(axis)
    up = [(i, (i + 1) % peers) for i in range(peers)]
    down = [(j, i) for i, j in up]
    return lax.ppermute(last, axis, up), lax.ppermute(first, axis, down)


def shifted(pieces, axis):
    peers = lax.axis_size(axis)
    return [pieces[0]] + [
        lax.ppermute(pieces[s], axis, [(i, (i + s) % peers) for i in range(peers)])
        for s in range(1, peers)
    ]


def body(scalar_field, transfer_in, transfer_out):
    layers, local_x, local_y = scalar_field.shape
    units, feats = transfer_in.shape
    channels = transfer_out.shape[0]
    bands = channels // 2
    count_x, count_y = lax.axis_size("bx"), lax.axis_size("by")
    steps = (2.0 / (local_x * count_x), 2.0 / (local_y * count_y))
    half, run, rows = local_x // 2, local_y // CHUNKS, rows_of(local_y)
    sds = lambda *shape: jax.ShapeDtypeStruct(shape, F32)
    weights = [
        jax.ShapeDtypeStruct((feats * CHUNKS, units * CHUNKS), BF16),
        jax.ShapeDtypeStruct((units * CHUNKS, channels * CHUNKS), BF16),
    ]

    edge = sds(REACH, half, LANES)
    turned, first, last = pl.pallas_call(
        turn_kernel,
        out_shape=[sds(half, rows, LANES), edge, edge],
        in_specs=[pl.BlockSpec(memory_space=pltpu.HBM)],
        out_specs=[VMEM] * 3,
        scratch_shapes=[
            pltpu.VMEM(scalar_field.shape, F32),
            pltpu.SemaphoreType.DMA((local_x // SUB,)),
        ],
        compiler_params=PARAMS,
        name="turn",
    )(scalar_field)
    before, after = exchange(last, first, "by")
    edge = sds(REACH, rows // 2, LANES)
    wide, first, last = call(
        functools.partial(sides_kernel, local_y, count_y), "sides", [sds(half, rows, LANES), edge, edge], 3
    )(turned, before, after)
    before, after = exchange(last, first, "bx")
    inner = half - 2 * REACH
    counts = (count_x, count_y)
    plane = lambda *lead: sds(*lead, CHUNKS, LANES)
    many_x, many_y = inner, 2
    win, wout, once, twice, ridge, colour_x, clear_x, colour_y, clear_y = call(
        functools.partial(middle_kernel, (many_x, many_y), counts, steps),
        "middle",
        weights + [plane(2, 4, run + 4), plane(2, 2, run + 2), plane(2, 2, run + 2)]
        + [sds(run, LANES, LANES)] * 2
        + [sds(inner, LANES, LANES)] * 2,
        3,
        [
            pltpu.VMEM((inner + 4, run + 4, CHUNKS, LANES), F32),
            pltpu.VMEM((inner + 2, run + 2, CHUNKS, LANES), F32),
            pltpu.VMEM((inner + 2, run + 2, CHUNKS, LANES), F32),
        ],
    )(wide, transfer_in, transfer_out)
    share = layers // count_x
    piece = sds(2, run, share, LANES)
    colour_ends, clear_ends, *pieces = call(
        functools.partial(ends_kernel, many_y, counts, steps),
        "ends",
        [sds(2 * REACH, LANES, LANES)] * 2 + [piece] * count_x,
        10,
        [
            pltpu.VMEM((2, run, layers, LANES), F32),
            pltpu.VMEM((2, 5, rows, LANES), F32),
            pltpu.VMEM((2, 7, run + 4, CHUNKS, LANES), F32),
            pltpu.VMEM((2, 5, run + 2, CHUNKS, LANES), F32),
            pltpu.VMEM((2, 5, run + 2, CHUNKS, LANES), F32),
        ],
    )(wide, before, after, win, wout, once, twice, ridge, colour_x, clear_x)
    pieces = shifted(pieces, "bx")
    view_x = call(fold_x_kernel, "fold_x", sds(2, bands, share, local_y), count_x)(*pieces)

    share = layers // count_y
    piece = sds(2, 2, share, LANES)
    scratch = [pltpu.VMEM((2, LANES, LANES), F32), pltpu.VMEM((2, LANES, LANES), F32)]
    pieces = call(
        functools.partial(columns_kernel, share, count_y), "columns", [piece] * count_y, 4, scratch
    )(colour_y, clear_y, colour_ends, clear_ends)
    pieces = shifted(pieces, "by")
    view_y = call(fold_y_kernel, "fold_y", piece, count_y)(*pieces)
    view_y = view_y.reshape(2, 2, share, half, bands)
    view_y = jnp.transpose(view_y, (0, 4, 2, 1, 3)).reshape(2, bands, share, local_x)
    return (view_x, view_y)


def solution(mesh):
    return jax.shard_map(
        body,
        mesh=mesh,
        in_specs=(P(None, "bx", "by"), P(), P()),
        out_specs=(P(None, None, "bx", "by"), P(None, None, "by", "bx")),
        check_vma=False,
    )
```

```python
import functools

import jax
import jax.numpy as jnp
from jax import lax
from jax.experimental import pallas as pl
from jax.experimental.pallas import tpu as pltpu
from jax.sharding import PartitionSpec as P

F32 = jnp.float32
BF16 = jnp.bfloat16
LOG2E = 1.4426950408889634
SUB = 8
LANES = 128
CHUNKS = 16
REACH = 3
VMEM = pl.BlockSpec(memory_space=pltpu.VMEM)
PARAMS = pltpu.CompilerParams(vmem_limit_bytes=48 * 1024 * 1024)


def call(kernel, name, outs, count, scratch=()):
    return pl.pallas_call(
        kernel,
        out_shape=outs,
        in_specs=[VMEM] * count,
        out_specs=jax.tree.map(lambda _: VMEM, outs),
        scratch_shapes=scratch,
        compiler_params=PARAMS,
        name=name,
    )


def rows_of(width):
    return -(-(width + 2 * REACH) // 16) * 16


def iota(shape, dim):
    return lax.broadcasted_iota(jnp.int32, shape, dim)


def one_hot(mask):
    return jnp.where(mask, 1.0, 0.0).astype(BF16)


def spread(weights, left, right, mask):
    inner = lax.dot_general(
        left, weights, (((1,), (1,)), ((), ())), preferred_element_type=F32
    ).astype(BF16)
    return jnp.where(mask, jnp.dot(inner, right, preferred_element_type=F32), 0.0)


def turn_kernel(field_hbm, turned_ref, first_ref, last_ref, field_ref, arrived):
    layers, length, width = field_ref.shape
    half = length // 2
    copies = []
    for i in range(length // SUB):
        part = (slice(None), pl.ds(i * SUB, SUB))
        copies.append(
            pltpu.make_async_copy(field_hbm.at[part], field_ref.at[part], arrived.at[i])
        )
    order = [i for k in range(half // SUB) for i in (k, k + half // SUB)]
    for i in order:
        copies[i].start()
    for k in range(half):
        if k % SUB == 0:
            copies[k // SUB].wait()
            copies[(k + half) // SUB].wait()
        turned = jnp.concatenate([field_ref[:, k, :], field_ref[:, k + half, :]], axis=0).T
        turned_ref[k, REACH : REACH + width] = turned
        for j in range(REACH):
            first_ref[j, k : k + 1] = turned[j : j + 1]
            last_ref[j, k : k + 1] = turned[width - REACH + j : width - REACH + j + 1]


def spread_weights(in_ref, out_ref, win_ref, wout_ref):
    units, feats = in_ref.shape
    channels = out_ref.shape[0]
    bands = channels // 2
    rows, cols = feats * CHUNKS, units * CHUNKS
    left = one_hot(iota((rows, feats), 0) // CHUNKS == iota((rows, feats), 1))
    right = one_hot(iota((units, cols), 1) // CHUNKS == iota((units, cols), 0))
    mask = iota((rows, cols), 0) % CHUNKS == iota((rows, cols), 1) % CHUNKS
    win_ref[...] = (0.5 * spread(in_ref[...], left, right, mask)).astype(BF16)
    rows, cols = cols, channels * CHUNKS
    left = one_hot(iota((rows, units), 0) // CHUNKS == iota((rows, units), 1))
    at = iota((channels, cols), 1)
    right = one_hot((at // LANES) * bands + at % bands == iota((channels, cols), 0))
    mask = iota((rows, cols), 0) % CHUNKS == (iota((rows, cols), 1) % LANES) // bands
    wout_ref[...] = spread(out_ref[...], left, right, mask).astype(BF16)


def sides_kernel(width, count_y, turned_ref, before_ref, after_ref, wide_ref, first_ref, last_ref):
    half, rows, _ = turned_ref.shape
    layers = LANES // 2
    part = rows // 2
    front = iota((part, LANES), 1) < layers
    at_y = lax.axis_index("by")
    keep_low = jnp.where(at_y == 0, 0.0, 1.0)
    keep_high = jnp.where(at_y == count_y - 1, 0.0, 1.0)
    for k in range(half):
        wide_ref[k, REACH : REACH + width] = turned_ref[k, REACH : REACH + width]
        for j in range(REACH):
            at = REACH + width + j
            wide_ref[k, j : j + 1] = before_ref[j, k : k + 1] * keep_low
            wide_ref[k, at : at + 1] = after_ref[j, k : k + 1] * keep_high
        wide_ref[k, 2 * REACH + width :] = jnp.zeros((rows - 2 * REACH - width, LANES), F32)
    for j in range(REACH):
        top, low = wide_ref[j, :part], wide_ref[j, part:]
        first_ref[j] = jnp.where(front, top, pltpu.roll(low, layers, axis=1))
        k = half - REACH + j
        top, low = wide_ref[k, :part], wide_ref[k, part:]
        last_ref[j] = jnp.where(front, pltpu.roll(top, layers, axis=1), low)


class Stencil:
    def __init__(self, run, counts):
        self.run = run
        self.layers = layers = LANES // 2
        self.shape = (CHUNKS, LANES)
        lane, chunk = iota(self.shape, 1), iota(self.shape, 0)
        z = lane % layers
        self.near = (z > 0).astype(F32)
        self.far = (z < layers - 1).astype(F32)
        at_x, at_y = lax.axis_index("bx"), lax.axis_index("by")
        count_x, count_y = counts
        self.x_low = jnp.where((lane < layers) & (at_x == 0), 0.0, 1.0)
        self.x_high = jnp.where((lane >= layers) & (at_x == count_x - 1), 0.0, 1.0)
        self.y_low = jnp.where((chunk == 0) & (at_y == 0), 0.0, 1.0)
        self.y_high = jnp.where((chunk == CHUNKS - 1) & (at_y == count_y - 1), 0.0, 1.0)

    def z_sum(self, value):
        return roll(value, 1) * self.near + roll(value, -1) * self.far

    def inside(self, value, y, edge):
        if edge is not None:
            value = value * edge
        if y < 0:
            value = value * self.y_low
        if y >= self.run:
            value = value * self.y_high
        return value

    def smooth(self, centre, others):
        total = self.z_sum(centre)
        for other in others:
            total = total + other
        return 0.4 * centre + 0.1 * total

    def raw(self, ref, k, y):
        return ref[k, pl.ds(y + REACH, CHUNKS, stride=self.run), :]

    def once(self, raw, k, out, at, edge=None):
        column = [self.raw(raw, k, y) for y in range(-3, self.run + 3)]
        for i in range(1, len(column) - 1):
            y = i - 3
            sides = [self.raw(raw, k - 1, y), self.raw(raw, k + 1, y)]
            value = self.smooth(column[i], [column[i - 1], column[i + 1]] + sides)
            out[at, i - 1] = self.inside(value, y, edge)

    def twice(self, once, k, out, ridge, at, edge=None):
        column = [once[k, i] for i in range(self.run + 4)]
        for i in range(1, len(column) - 1):
            sides = [once[k - 1, i], once[k + 1, i]]
            value = self.smooth(column[i], [column[i - 1], column[i + 1]] + sides)
            value = self.inside(value, i - 2, edge)
            out[at, i - 1] = value
            ridge[at, i - 1] = 2.0 * value + self.z_sum(value)

    def features(self, twice, ridge, k, y):
        p = lambda a, b: twice[k + a, y + 1 + b]
        r = lambda a, b: ridge[k + a, y + 1 + b]
        centre = p(0, 0)
        main, cross = p(1, 1) - p(-1, -1), p(1, -1) - p(-1, 1)
        third = 1.0 / 3.0
        gx = (main + cross + (r(1, 0) - r(-1, 0))) * third
        gy = (main - cross + (r(0, 1) - r(0, -1))) * third
        around = 2.0 * centre + ((p(1, 0) + p(-1, 0)) + (p(0, 1) + p(0, -1)))
        gz = (roll(around, -1) * self.far - roll(around, 1) * self.near) * third
        m = jnp.sqrt(1.0 + gx * gx + gy * gy + gz * gz)
        parts = [centre, gx, gy, gz, m, centre * m, centre * centre]
        packed = [part.astype(BF16) for part in parts] + [jnp.ones(self.shape, BF16)]
        return jnp.concatenate(packed, axis=0).T


def roll(value, shift):
    return pltpu.roll(value, shift % LANES, axis=1)


def network(tiles, win_ref, wout_ref, step):
    cells = jnp.concatenate(tiles, axis=0)
    half_v = jnp.dot(cells, win_ref[...], preferred_element_type=F32)
    hidden = (half_v + half_v * jnp.tanh(half_v)).astype(BF16)
    v = jnp.dot(hidden, wout_ref[...], preferred_element_type=F32)
    soft = jnp.maximum(v, jnp.log(1.0 + jnp.exp2(jnp.minimum(v * LOG2E, 126.0))))
    return soft[:, :LANES], jnp.exp2(soft[:, LANES:] * (-LOG2E * step))


def clear_of_x(q, ratio):
    if ratio == 1.0:
        return q
    if ratio == 2.0:
        return q * q
    return jnp.exp2(jnp.log(q) * (LOG2E * ratio))


def step_ray(ray, clear, emission):
    colour, light = ray
    later = light * clear
    return colour + (light - later) * emission, later


def middle_kernel(
    spans,
    counts,
    steps,
    wide_ref,
    in_ref,
    out_ref,
    win_ref,
    wout_ref,
    once_out_ref,
    twice_out_ref,
    ridge_out_ref,
    cx_ref,
    tx_ref,
    cy_ref,
    ty_ref,
    once_ref,
    twice_ref,
    ridge_ref,
):
    half = wide_ref.shape[0]
    run = cx_ref.shape[0]
    stencil = Stencil(run, counts)
    many_x, many_y = spans
    inner = half - 2 * REACH
    spread_weights(in_ref, out_ref, win_ref, wout_ref)
    for k in range(inner + 4):
        stencil.once(wide_ref, k + 1, once_ref, k)
    for k in range(inner + 2):
        stencil.twice(once_ref, k + 1, twice_ref, ridge_ref, k)
    for k in range(4):
        once_out_ref[0, k] = once_ref[k]
        once_out_ref[1, k] = once_ref[inner + k]
    for k in range(2):
        twice_out_ref[0, k] = twice_ref[k]
        twice_out_ref[1, k] = twice_ref[inner + k]
        ridge_out_ref[0, k] = ridge_ref[k]
        ridge_out_ref[1, k] = ridge_ref[inner + k]

    for k in range(run):
        tx_ref[k] = jnp.ones((LANES, LANES), F32)
        cx_ref[k] = jnp.zeros((LANES, LANES), F32)
    for k in range(inner):
        ty_ref[k] = jnp.ones((LANES, LANES), F32)
        cy_ref[k] = jnp.zeros((LANES, LANES), F32)
    ratio = steps[0] / steps[1]
    down = run // many_y

    def block(step):
        x0, y0 = (step // down) * many_x, (step % down) * many_y
        tiles = [
            stencil.features(twice_ref, ridge_ref, x0 + i + 1, y0 + j)
            for j in range(many_y)
            for i in range(many_x)
        ]
        emission, clear = network(tiles, win_ref, wout_ref, steps[1])
        for g in range(LANES // SUB):
            at = pl.ds(g * SUB, SUB)
            rays_y = [(cy_ref[x0 + i, at], ty_ref[x0 + i, at]) for i in range(many_x)]
            for j in range(many_y):
                ray_x = cx_ref[y0 + j, at], tx_ref[y0 + j, at]
                for i in range(many_x):
                    start = (j * many_x + i) * LANES + g * SUB
                    e, q = emission[start : start + SUB], clear[start : start + SUB]
                    rays_y[i] = step_ray(rays_y[i], q, e)
                    ray_x = step_ray(ray_x, clear_of_x(q, ratio), e)
                cx_ref[y0 + j, at], tx_ref[y0 + j, at] = ray_x
            for i in range(many_x):
                cy_ref[x0 + i, at], ty_ref[x0 + i, at] = rays_y[i]

    for step in range(inner // many_x * down):
        block(step)


def ends_kernel(
    many_y,
    counts,
    steps,
    wide_ref,
    before_ref,
    after_ref,
    win_ref,
    wout_ref,
    once_in_ref,
    twice_in_ref,
    ridge_in_ref,
    cx_ref,
    tx_ref,
    cy_middle_ref,
    ty_middle_ref,
    kept_ref,
    sent_ref,
    *refs,
):
    outs, refs = refs[: counts[0]], refs[counts[0] :]
    image_ref, raw_ref, once_ref, twice_ref, ridge_ref, cy_ref, ty_ref, rows_ref, columns_ref = refs
    half, rows, _ = wide_ref.shape
    run = cx_ref.shape[0]
    layers = LANES // 2
    stencil = Stencil(run, counts)
    part = rows // 2
    front = iota((part, LANES), 1) < layers
    at_x = lax.axis_index("bx")
    keep_low = jnp.where(at_x == 0, 0.0, 1.0)
    keep_high = jnp.where(at_x == counts[0] - 1, 0.0, 1.0)
    for j in range(REACH):
        halo, own = before_ref[j] * keep_low, wide_ref[half - REACH + j]
        raw_ref[0, j, :part] = jnp.where(front, halo, roll(own[:part], layers))
        raw_ref[0, j, part:] = jnp.where(front, roll(halo, layers), roll(own[part:], layers))
        halo, own = after_ref[j] * keep_high, wide_ref[j]
        raw_ref[1, 2 + j, :part] = jnp.where(front, roll(own[:part], layers), roll(halo, layers))
        raw_ref[1, 2 + j, part:] = jnp.where(front, roll(own[part:], layers), halo)
    for j in range(2):
        raw_ref[0, REACH + j] = wide_ref[j]
        raw_ref[1, j] = wide_ref[half - 2 + j]
    for k in range(4):
        once_ref[0, 3 + k] = once_in_ref[0, k]
        once_ref[1, k] = once_in_ref[1, k]
    for k in range(2):
        twice_ref[0, 3 + k] = twice_in_ref[0, k]
        twice_ref[1, k] = twice_in_ref[1, k]
        ridge_ref[0, 3 + k] = ridge_in_ref[0, k]
        ridge_ref[1, k] = ridge_in_ref[1, k]
    for side, edge in enumerate((stencil.x_low, stencil.x_high)):
        outside = (0, 1) if side == 0 else (1, 2)
        for k in range(3):
            kept = edge if k in outside else None
            stencil.once(raw_ref.at[side], k + 1, once_ref.at[side], k + 4 * side, kept)
    for side, edge in enumerate((stencil.x_low, stencil.x_high)):
        for k in range(3):
            kept = edge if k == 2 * side else None
            at = k + 2 * side
            stencil.twice(once_ref.at[side], at + 1, twice_ref.at[side], ridge_ref.at[side], at, kept)

    ratio = steps[0] / steps[1]
    planes = [(0, 1), (0, 2), (0, 3), (1, 1), (1, 2), (1, 3)]
    for k in range(len(planes)):
        ty_ref[k] = jnp.ones((LANES, LANES), F32)
        cy_ref[k] = jnp.zeros((LANES, LANES), F32)

    def block(step):
        y0 = step * many_y
        tiles = [
            stencil.features(twice_ref.at[side], ridge_ref.at[side], k, y0 + j)
            for j in range(many_y)
            for side, k in planes
        ]
        emission, clear = network(tiles, win_ref, wout_ref, steps[1])
        images = [[], []]
        for g in range(LANES // SUB):
            at = pl.ds(g * SUB, SUB)
            rays_y = [(cy_ref[i, at], ty_ref[i, at]) for i in range(len(planes))]
            for j in range(many_y):
                ray_x = jnp.zeros((SUB, LANES), F32), jnp.ones((SUB, LANES), F32)
                for i in range(len(planes)):
                    if i == REACH:
                        colour, light = ray_x
                        colour = colour + light * cx_ref[y0 + j, at]
                        ray_x = colour, light * tx_ref[y0 + j, at]
                    start = (j * len(planes) + i) * LANES + g * SUB
                    e, q = emission[start : start + SUB], clear[start : start + SUB]
                    rays_y[i] = step_ray(rays_y[i], q, e)
                    ray_x = step_ray(ray_x, clear_of_x(q, ratio), e)
                images[0].append(ray_x[0])
                images[1].append(ray_x[1])
            for i in range(len(planes)):
                cy_ref[i, at], ty_ref[i, at] = rays_y[i]
        for d in range(layers // SUB):
            for j in range(many_y):
                near, far = d * many_y + j, (d + layers // SUB) * many_y + j
                q = images[1][near]
                at = pl.ds(d * SUB, SUB)
                image_ref[0, y0 + j, at] = images[0][near] + q * images[0][far]
                image_ref[1, y0 + j, at] = q * images[1][far]

    for step in range(run // many_y):
        block(step)
    share = layers // counts[0]
    for s, out_ref in enumerate(outs):
        start = pl.multiple_of(lax.rem(at_x + s, counts[0]) * share, share)
        out_ref[...] = image_ref[:, :, pl.ds(start, share), :]

    inner = half - 2 * REACH
    for k in range(half):
        if REACH <= k < REACH + inner:
            image = column_image(cy_middle_ref[k - REACH], ty_middle_ref[k - REACH])
        else:
            i = k if k < REACH else k - inner
            image = column_image(cy_ref[i], ty_ref[i])
        for kind in range(2):
            rows_ref[kind, k * SUB : (k + 1) * SUB] = image[kind]
    share = layers // counts[1]
    mine = lax.axis_index("by") & 1
    for kind in range(2):
        columns_ref[kind] = rows_ref[kind].T
        for r in range(counts[1] // 2):
            for out_ref, bit in ((kept_ref, mine), (sent_ref, 1 - mine)):
                for part in range(2):
                    start = pl.multiple_of((2 * r + bit) * share + part * layers, share)
                    out_ref[r, kind, part] = columns_ref[kind, pl.ds(start, share)]


def column_image(colours, clears):
    colours, clears = colours.T, clears.T
    colour, clear = colours[:SUB], clears[:SUB]
    for c in range(1, CHUNKS):
        at = slice(c * SUB, (c + 1) * SUB)
        colour = colour + clear * colours[at]
        clear = clear * clears[at]
    return colour, clear


def merge_kernel(level, peers, kept_ref, received_ref, *refs):
    me = lax.axis_index("by") >> (level - 1)
    later = (me & 1) == 1
    kept, received = kept_ref[...], received_ref[...]
    front = jnp.where(later, received, kept)
    back = jnp.where(later, kept, received)
    many = kept.shape[0]
    colour = front[:, 0] + front[:, 1] * back[:, 0]
    clear = front[:, 1] * back[:, 1]
    if many == 1:
        refs[0][0] = colour[0]
        refs[0][1] = clear[0]
        return
    out_kept_ref, out_sent_ref = refs
    bit = ((me >> 1) & 1) == 1
    for r in range(many // 2):
        for kind, value in enumerate((colour, clear)):
            even, odd = value[2 * r], value[2 * r + 1]
            out_kept_ref[r, kind] = jnp.where(bit, odd, even)
            out_sent_ref[r, kind] = jnp.where(bit, even, odd)


def fold_x_kernel(*refs):
    pieces, out_ref = refs[:-1], refs[-1]
    _, run, share, _ = pieces[0].shape
    lane = iota((share, LANES), 1)
    me = lax.axis_index("bx")
    kinds = [[], []]
    for y in range(run):
        behind = colour, clear = jnp.zeros((share, LANES), F32), jnp.ones((share, LANES), F32)
        for s in reversed(range(len(pieces))):
            start = me == s
            behind = jnp.where(start, colour, behind[0]), jnp.where(start, clear, behind[1])
            colour, clear = jnp.where(start, 0.0, colour), jnp.where(start, 1.0, clear)
            colour = colour + clear * pieces[s][0, y]
            clear = clear * pieces[s][1, y]
        kinds[0].append(colour + clear * behind[0])
        kinds[1].append(clear * behind[1])
    for kind, values in enumerate(kinds):
        for s in (1, 2, 4):
            for i in range(run):
                if not i & s:
                    a, b = values[i], values[i | s]
                    odd = (lane & s) != 0
                    values[i] = jnp.where(odd, pltpu.roll(b, s, axis=1), a)
                    values[i | s] = jnp.where(odd, b, pltpu.roll(a, LANES - s, axis=1))
        for band, value in enumerate(values):
            out_ref[kind, band] = value


def exchange(last, first, axis):
    peers = lax.axis_size(axis)
    up = [(i, (i + 1) % peers) for i in range(peers)]
    down = [(j, i) for i, j in up]
    return lax.ppermute(last, axis, up), lax.ppermute(first, axis, down)


def shifted(pieces, axis):
    peers = lax.axis_size(axis)
    return [pieces[0]] + [
        lax.ppermute(pieces[s], axis, [(i, (i + s) % peers) for i in range(peers)])
        for s in range(1, peers)
    ]


def body(scalar_field, transfer_in, transfer_out):
    layers, local_x, local_y = scalar_field.shape
    units, feats = transfer_in.shape
    channels = transfer_out.shape[0]
    bands = channels // 2
    count_x, count_y = lax.axis_size("bx"), lax.axis_size("by")
    steps = (2.0 / (local_x * count_x), 2.0 / (local_y * count_y))
    half, run, rows = local_x // 2, local_y // CHUNKS, rows_of(local_y)
    sds = lambda *shape: jax.ShapeDtypeStruct(shape, F32)
    weights = [
        jax.ShapeDtypeStruct((feats * CHUNKS, units * CHUNKS), BF16),
        jax.ShapeDtypeStruct((units * CHUNKS, channels * CHUNKS), BF16),
    ]

    edge = sds(REACH, half, LANES)
    turned, first, last = pl.pallas_call(
        turn_kernel,
        out_shape=[sds(half, rows, LANES), edge, edge],
        in_specs=[pl.BlockSpec(memory_space=pltpu.HBM)],
        out_specs=[VMEM] * 3,
        scratch_shapes=[
            pltpu.VMEM(scalar_field.shape, F32),
            pltpu.SemaphoreType.DMA((local_x // SUB,)),
        ],
        compiler_params=pltpu.CompilerParams(vmem_limit_bytes=52 * 1024 * 1024),
        name="turn",
    )(scalar_field)
    before, after = exchange(last, first, "by")
    edge = sds(REACH, rows // 2, LANES)
    wide, first, last = call(
        functools.partial(sides_kernel, local_y, count_y), "sides", [sds(half, rows, LANES), edge, edge], 3
    )(turned, before, after)
    before, after = exchange(last, first, "bx")
    inner = half - 2 * REACH
    counts = (count_x, count_y)
    plane = lambda *lead: sds(*lead, CHUNKS, LANES)
    many_x, many_y = inner, 2
    win, wout, once, twice, ridge, colour_x, clear_x, colour_y, clear_y = call(
        functools.partial(middle_kernel, (many_x, many_y), counts, steps),
        "middle",
        weights + [plane(2, 4, run + 4), plane(2, 2, run + 2), plane(2, 2, run + 2)]
        + [sds(run, LANES, LANES)] * 2
        + [sds(inner, LANES, LANES)] * 2,
        3,
        [
            pltpu.VMEM((inner + 4, run + 4, CHUNKS, LANES), F32),
            pltpu.VMEM((inner + 2, run + 2, CHUNKS, LANES), F32),
            pltpu.VMEM((inner + 2, run + 2, CHUNKS, LANES), F32),
        ],
    )(wide, transfer_in, transfer_out)
    share = layers // count_x
    share_y = layers // count_y
    piece = sds(2, run, share, LANES)
    parts = sds(count_y // 2, 2, 2, share_y, LANES)
    kept, sent, *pieces = call(
        functools.partial(ends_kernel, many_y, counts, steps),
        "ends",
        [parts] * 2 + [piece] * count_x,
        12,
        [
            pltpu.VMEM((2, run, layers, LANES), F32),
            pltpu.VMEM((2, 5, rows, LANES), F32),
            pltpu.VMEM((2, 7, run + 4, CHUNKS, LANES), F32),
            pltpu.VMEM((2, 5, run + 2, CHUNKS, LANES), F32),
            pltpu.VMEM((2, 5, run + 2, CHUNKS, LANES), F32),
            pltpu.VMEM((2 * REACH, LANES, LANES), F32),
            pltpu.VMEM((2 * REACH, LANES, LANES), F32),
            pltpu.VMEM((2, LANES, LANES), F32),
            pltpu.VMEM((2, LANES, LANES), F32),
        ],
    )(wide, before, after, win, wout, once, twice, ridge, colour_x, clear_x, colour_y, clear_y)

    level, many = 1, count_y // 2
    while many:
        pairs = [(i, i ^ level) for i in range(count_y)]
        received = lax.ppermute(sent, "by", pairs)
        merge = functools.partial(merge_kernel, level.bit_length(), count_y)
        if many > 1:
            half_parts = sds(many // 2, 2, 2, share_y, LANES)
            kept, sent = call(merge, "merge", [half_parts] * 2, 2)(kept, received)
        else:
            view_y = call(merge, "merge", sds(2, 2, share_y, LANES), 2)(kept, received)
        level, many = 2 * level, many // 2
    pieces = shifted(pieces, "bx")
    view_x = call(fold_x_kernel, "fold_x", sds(2, bands, share, local_y), count_x)(*pieces)
    view_y = view_y.reshape(2, 2, share_y, half, bands)
    view_y = jnp.transpose(view_y, (0, 4, 2, 1, 3)).reshape(2, bands, share_y, local_x)
    return (view_x, view_y)


def solution(mesh):
    return jax.shard_map(
        body,
        mesh=mesh,
        in_specs=(P(None, "bx", "by"), P(), P()),
        out_specs=(P(None, None, "bx", "by"), P(None, None, "by", "bx")),
        check_vma=False,
    )
```

```python
import functools

import jax
import jax.numpy as jnp
from jax import lax
from jax.experimental import pallas as pl
from jax.experimental.pallas import tpu as pltpu
from jax.sharding import PartitionSpec as P

F32 = jnp.float32
BF16 = jnp.bfloat16
LOG2E = 1.4426950408889634
SUB = 8
LANES = 128
CHUNKS = 16
REACH = 3
VMEM = pl.BlockSpec(memory_space=pltpu.VMEM)
PARAMS = pltpu.CompilerParams(vmem_limit_bytes=36 * 1024 * 1024)


def call(kernel, name, outs, count, scratch=()):
    return pl.pallas_call(
        kernel,
        out_shape=outs,
        in_specs=[VMEM] * count,
        out_specs=jax.tree.map(lambda _: VMEM, outs),
        scratch_shapes=scratch,
        compiler_params=PARAMS,
        name=name,
    )


def rows_of(width):
    return -(-(width + 2 * REACH) // 16) * 16


def iota(shape, dim):
    return lax.broadcasted_iota(jnp.int32, shape, dim)


def one_hot(mask):
    return jnp.where(mask, 1.0, 0.0).astype(BF16)


def spread(weights, left, right, mask):
    inner = lax.dot_general(
        left, weights, (((1,), (1,)), ((), ())), preferred_element_type=F32
    ).astype(BF16)
    return jnp.where(mask, jnp.dot(inner, right, preferred_element_type=F32), 0.0)


def turn_kernel(field_ref, turned_ref, first_ref, last_ref):
    layers, length, width = field_ref.shape
    half = length // 2
    for k in range(half):
        turned = jnp.concatenate([field_ref[:, k, :], field_ref[:, k + half, :]], axis=0).T
        turned_ref[k, REACH : REACH + width] = turned
        for j in range(REACH):
            first_ref[j, k : k + 1] = turned[j : j + 1]
            last_ref[j, k : k + 1] = turned[width - REACH + j : width - REACH + j + 1]


def spread_weights(in_ref, out_ref, win_ref, wout_ref):
    units, feats = in_ref.shape
    channels = out_ref.shape[0]
    bands = channels // 2
    rows, cols = feats * CHUNKS, units * CHUNKS
    left = one_hot(iota((rows, feats), 0) // CHUNKS == iota((rows, feats), 1))
    right = one_hot(iota((units, cols), 1) // CHUNKS == iota((units, cols), 0))
    mask = iota((rows, cols), 0) % CHUNKS == iota((rows, cols), 1) % CHUNKS
    win_ref[...] = (0.5 * spread(in_ref[...], left, right, mask)).astype(BF16)
    rows, cols = cols, channels * CHUNKS
    left = one_hot(iota((rows, units), 0) // CHUNKS == iota((rows, units), 1))
    at = iota((channels, cols), 1)
    right = one_hot((at // LANES) * bands + at % bands == iota((channels, cols), 0))
    mask = iota((rows, cols), 0) % CHUNKS == (iota((rows, cols), 1) % LANES) // bands
    wout_ref[...] = spread(out_ref[...], left, right, mask).astype(BF16)


def sides_kernel(width, count_y, turned_ref, before_ref, after_ref, wide_ref, first_ref, last_ref):
    half, rows, _ = turned_ref.shape
    layers = LANES // 2
    part = rows // 2
    front = iota((part, LANES), 1) < layers
    at_y = lax.axis_index("by")
    keep_low = jnp.where(at_y == 0, 0.0, 1.0)
    keep_high = jnp.where(at_y == count_y - 1, 0.0, 1.0)
    for k in range(half):
        wide_ref[k, REACH : REACH + width] = turned_ref[k, REACH : REACH + width]
        for j in range(REACH):
            at = REACH + width + j
            wide_ref[k, j : j + 1] = before_ref[j, k : k + 1] * keep_low
            wide_ref[k, at : at + 1] = after_ref[j, k : k + 1] * keep_high
        wide_ref[k, 2 * REACH + width :] = jnp.zeros((rows - 2 * REACH - width, LANES), F32)
    for j in range(REACH):
        top, low = wide_ref[j, :part], wide_ref[j, part:]
        first_ref[j] = jnp.where(front, top, pltpu.roll(low, layers, axis=1))
        k = half - REACH + j
        top, low = wide_ref[k, :part], wide_ref[k, part:]
        last_ref[j] = jnp.where(front, pltpu.roll(top, layers, axis=1), low)


class Stencil:
    def __init__(self, run, counts):
        self.run = run
        self.layers = layers = LANES // 2
        self.shape = (CHUNKS, LANES)
        lane, chunk = iota(self.shape, 1), iota(self.shape, 0)
        z = lane % layers
        self.near = (z > 0).astype(F32)
        self.far = (z < layers - 1).astype(F32)
        at_x, at_y = lax.axis_index("bx"), lax.axis_index("by")
        count_x, count_y = counts
        self.x_low = jnp.where((lane < layers) & (at_x == 0), 0.0, 1.0)
        self.x_high = jnp.where((lane >= layers) & (at_x == count_x - 1), 0.0, 1.0)
        self.y_low = jnp.where((chunk == 0) & (at_y == 0), 0.0, 1.0)
        self.y_high = jnp.where((chunk == CHUNKS - 1) & (at_y == count_y - 1), 0.0, 1.0)

    def z_sum(self, value):
        return roll(value, 1) * self.near + roll(value, -1) * self.far

    def inside(self, value, y, edge):
        if edge is not None:
            value = value * edge
        if y < 0:
            value = value * self.y_low
        if y >= self.run:
            value = value * self.y_high
        return value

    def smooth(self, centre, others):
        total = self.z_sum(centre)
        for other in others:
            total = total + other
        return 0.4 * centre + 0.1 * total

    def raw(self, ref, k, y):
        return ref[k, pl.ds(y + REACH, CHUNKS, stride=self.run), :]

    def once(self, raw, k, out, at, edge=None):
        column = [self.raw(raw, k, y) for y in range(-3, self.run + 3)]
        for i in range(1, len(column) - 1):
            y = i - 3
            sides = [self.raw(raw, k - 1, y), self.raw(raw, k + 1, y)]
            value = self.smooth(column[i], [column[i - 1], column[i + 1]] + sides)
            out[at, i - 1] = self.inside(value, y, edge)

    def twice(self, once, k, out, ridge, at, edge=None):
        column = [once[k, i] for i in range(self.run + 4)]
        for i in range(1, len(column) - 1):
            sides = [once[k - 1, i], once[k + 1, i]]
            value = self.smooth(column[i], [column[i - 1], column[i + 1]] + sides)
            value = self.inside(value, i - 2, edge)
            out[at, i - 1] = value
            ridge[at, i - 1] = 2.0 * value + self.z_sum(value)

    def features(self, twice, ridge, k, y):
        p = lambda a, b: twice[k + a, y + 1 + b]
        r = lambda a, b: ridge[k + a, y + 1 + b]
        centre = p(0, 0)
        main, cross = p(1, 1) - p(-1, -1), p(1, -1) - p(-1, 1)
        third = 1.0 / 3.0
        gx = (main + cross + (r(1, 0) - r(-1, 0))) * third
        gy = (main - cross + (r(0, 1) - r(0, -1))) * third
        around = 2.0 * centre + ((p(1, 0) + p(-1, 0)) + (p(0, 1) + p(0, -1)))
        gz = (roll(around, -1) * self.far - roll(around, 1) * self.near) * third
        m = jnp.sqrt(1.0 + gx * gx + gy * gy + gz * gz)
        parts = [centre, gx, gy, gz, m, centre * m, centre * centre]
        packed = [part.astype(BF16) for part in parts] + [jnp.ones(self.shape, BF16)]
        return jnp.concatenate(packed, axis=0).T


def roll(value, shift):
    return pltpu.roll(value, shift % LANES, axis=1)


def network(tiles, win_ref, wout_ref, step):
    cells = jnp.concatenate(tiles, axis=0)
    half_v = jnp.dot(cells, win_ref[...], preferred_element_type=F32)
    hidden = (half_v + half_v * jnp.tanh(half_v)).astype(BF16)
    v = jnp.dot(hidden, wout_ref[...], preferred_element_type=F32)
    soft = jnp.maximum(v, jnp.log(1.0 + jnp.exp2(jnp.minimum(v * LOG2E, 126.0))))
    return soft[:, :LANES], jnp.exp2(soft[:, LANES:] * (-LOG2E * step))


def clear_of_x(q, ratio):
    if ratio == 1.0:
        return q
    if ratio == 2.0:
        return q * q
    return jnp.exp2(jnp.log(q) * (LOG2E * ratio))


def step_ray(ray, clear, emission):
    colour, light = ray
    later = light * clear
    return colour + (light - later) * emission, later


def middle_kernel(
    spans,
    counts,
    steps,
    wide_ref,
    in_ref,
    out_ref,
    win_ref,
    wout_ref,
    once_out_ref,
    twice_out_ref,
    ridge_out_ref,
    cx_ref,
    tx_ref,
    cy_ref,
    ty_ref,
    once_ref,
    twice_ref,
    ridge_ref,
):
    half = wide_ref.shape[0]
    run = cx_ref.shape[0]
    stencil = Stencil(run, counts)
    many_x, many_y = spans
    inner = half - 2 * REACH
    spread_weights(in_ref, out_ref, win_ref, wout_ref)
    for k in range(inner + 4):
        stencil.once(wide_ref, k + 1, once_ref, k)
    for k in range(inner + 2):
        stencil.twice(once_ref, k + 1, twice_ref, ridge_ref, k)
    for k in range(4):
        once_out_ref[0, k] = once_ref[k]
        once_out_ref[1, k] = once_ref[inner + k]
    for k in range(2):
        twice_out_ref[0, k] = twice_ref[k]
        twice_out_ref[1, k] = twice_ref[inner + k]
        ridge_out_ref[0, k] = ridge_ref[k]
        ridge_out_ref[1, k] = ridge_ref[inner + k]

    for k in range(run):
        tx_ref[k] = jnp.ones((LANES, LANES), F32)
        cx_ref[k] = jnp.zeros((LANES, LANES), F32)
    for k in range(inner):
        ty_ref[k] = jnp.ones((LANES, LANES), F32)
        cy_ref[k] = jnp.zeros((LANES, LANES), F32)
    ratio = steps[0] / steps[1]
    down = run // many_y

    def block(step):
        x0, y0 = (step // down) * many_x, (step % down) * many_y
        tiles = [
            stencil.features(twice_ref, ridge_ref, x0 + i + 1, y0 + j)
            for j in range(many_y)
            for i in range(many_x)
        ]
        emission, clear = network(tiles, win_ref, wout_ref, steps[1])
        for g in range(LANES // SUB):
            at = pl.ds(g * SUB, SUB)
            rays_y = [(cy_ref[x0 + i, at], ty_ref[x0 + i, at]) for i in range(many_x)]
            for j in range(many_y):
                ray_x = cx_ref[y0 + j, at], tx_ref[y0 + j, at]
                for i in range(many_x):
                    start = (j * many_x + i) * LANES + g * SUB
                    e, q = emission[start : start + SUB], clear[start : start + SUB]
                    rays_y[i] = step_ray(rays_y[i], q, e)
                    ray_x = step_ray(ray_x, clear_of_x(q, ratio), e)
                cx_ref[y0 + j, at], tx_ref[y0 + j, at] = ray_x
            for i in range(many_x):
                cy_ref[x0 + i, at], ty_ref[x0 + i, at] = rays_y[i]

    for step in range(inner // many_x * down):
        block(step)


def parts_of(image_ref, kept_ref, sent_ref, mine):
    many, share = kept_ref.shape[0], kept_ref.shape[3]
    for r in range(many):
        for out_ref, bit in ((kept_ref, mine), (sent_ref, 1 - mine)):
            start = pl.multiple_of((2 * r + bit) * share, share)
            out_ref[r] = image_ref[:, :, pl.ds(start, share), :]


def march_ends(stencil, steps, first, weights, fields, middle, rays, image_ref):
    twice_ref, ridge_ref = fields
    cx_ref, tx_ref = middle
    cy_ref, ty_ref = rays
    layers = stencil.layers
    many_y = image_ref.shape[1]
    ratio = steps[0] / steps[1]
    planes = [(0, 1), (0, 2), (0, 3), (1, 1), (1, 2), (1, 3)]
    tiles = [
        stencil.features(twice_ref.at[side], ridge_ref.at[side], k, first + j)
        for j in range(many_y)
        for side, k in planes
    ]
    emission, clear = network(tiles, *weights, steps[1])
    images = [[], []]
    for g in range(LANES // SUB):
        at = pl.ds(g * SUB, SUB)
        rays_y = [(cy_ref[i, at], ty_ref[i, at]) for i in range(len(planes))]
        for j in range(many_y):
            ray_x = jnp.zeros((SUB, LANES), F32), jnp.ones((SUB, LANES), F32)
            for i in range(len(planes)):
                if i == REACH:
                    colour, light = ray_x
                    colour = colour + light * cx_ref[first + j, at]
                    ray_x = colour, light * tx_ref[first + j, at]
                start = (j * len(planes) + i) * LANES + g * SUB
                e, q = emission[start : start + SUB], clear[start : start + SUB]
                rays_y[i] = step_ray(rays_y[i], q, e)
                ray_x = step_ray(ray_x, clear_of_x(q, ratio), e)
            images[0].append(ray_x[0])
            images[1].append(ray_x[1])
        for i in range(len(planes)):
            cy_ref[i, at], ty_ref[i, at] = rays_y[i]
    for d in range(layers // SUB):
        for j in range(many_y):
            near, far = d * many_y + j, (d + layers // SUB) * many_y + j
            q = images[1][near]
            at = pl.ds(d * SUB, SUB)
            image_ref[0, j, at] = images[0][near] + q * images[0][far]
            image_ref[1, j, at] = q * images[1][far]


def ends_first_kernel(
    counts,
    steps,
    wide_ref,
    before_ref,
    after_ref,
    win_ref,
    wout_ref,
    once_in_ref,
    twice_in_ref,
    ridge_in_ref,
    cx_ref,
    tx_ref,
    twice_ref,
    ridge_ref,
    cy_ref,
    ty_ref,
    kept_ref,
    sent_ref,
    image_ref,
    raw_ref,
    once_ref,
):
    half, rows, _ = wide_ref.shape
    run = cx_ref.shape[0]
    layers = LANES // 2
    stencil = Stencil(run, counts)
    part = rows // 2
    front = iota((part, LANES), 1) < layers
    at_x = lax.axis_index("bx")
    keep_low = jnp.where(at_x == 0, 0.0, 1.0)
    keep_high = jnp.where(at_x == counts[0] - 1, 0.0, 1.0)
    for j in range(REACH):
        halo, own = before_ref[j] * keep_low, wide_ref[half - REACH + j]
        raw_ref[0, j, :part] = jnp.where(front, halo, roll(own[:part], layers))
        raw_ref[0, j, part:] = jnp.where(front, roll(halo, layers), roll(own[part:], layers))
        halo, own = after_ref[j] * keep_high, wide_ref[j]
        raw_ref[1, 2 + j, :part] = jnp.where(front, roll(own[:part], layers), roll(halo, layers))
        raw_ref[1, 2 + j, part:] = jnp.where(front, roll(own[part:], layers), halo)
    for j in range(2):
        raw_ref[0, REACH + j] = wide_ref[j]
        raw_ref[1, j] = wide_ref[half - 2 + j]
    for k in range(4):
        once_ref[0, 3 + k] = once_in_ref[0, k]
        once_ref[1, k] = once_in_ref[1, k]
    for k in range(2):
        twice_ref[0, 3 + k] = twice_in_ref[0, k]
        twice_ref[1, k] = twice_in_ref[1, k]
        ridge_ref[0, 3 + k] = ridge_in_ref[0, k]
        ridge_ref[1, k] = ridge_in_ref[1, k]
    for side, edge in enumerate((stencil.x_low, stencil.x_high)):
        outside = (0, 1) if side == 0 else (1, 2)
        for k in range(3):
            kept = edge if k in outside else None
            stencil.once(raw_ref.at[side], k + 1, once_ref.at[side], k + 4 * side, kept)
    for side, edge in enumerate((stencil.x_low, stencil.x_high)):
        for k in range(3):
            kept = edge if k == 2 * side else None
            at = k + 2 * side
            stencil.twice(once_ref.at[side], at + 1, twice_ref.at[side], ridge_ref.at[side], at, kept)
    for k in range(2 * REACH):
        ty_ref[k] = jnp.ones((LANES, LANES), F32)
        cy_ref[k] = jnp.zeros((LANES, LANES), F32)
    march_ends(
        stencil,
        steps,
        0,
        (win_ref, wout_ref),
        (twice_ref, ridge_ref),
        (cx_ref, tx_ref),
        (cy_ref, ty_ref),
        image_ref,
    )
    parts_of(image_ref, kept_ref, sent_ref, at_x & 1)


def ends_last_kernel(
    counts,
    steps,
    win_ref,
    wout_ref,
    twice_ref,
    ridge_ref,
    cx_ref,
    tx_ref,
    cy_in_ref,
    ty_in_ref,
    cy_middle_ref,
    ty_middle_ref,
    kept_ref,
    sent_ref,
    kept_y_ref,
    sent_y_ref,
    image_ref,
    cy_ref,
    ty_ref,
    rows_ref,
    columns_ref,
):
    run = cx_ref.shape[0]
    stencil = Stencil(run, counts)
    layers = stencil.layers
    cy_ref[...] = cy_in_ref[...]
    ty_ref[...] = ty_in_ref[...]
    march_ends(
        stencil,
        steps,
        run - image_ref.shape[1],
        (win_ref, wout_ref),
        (twice_ref, ridge_ref),
        (cx_ref, tx_ref),
        (cy_ref, ty_ref),
        image_ref,
    )
    parts_of(image_ref, kept_ref, sent_ref, lax.axis_index("bx") & 1)
    inner = cy_middle_ref.shape[0]
    half = inner + 2 * REACH
    for k in range(half):
        if REACH <= k < REACH + inner:
            image = column_image(cy_middle_ref[k - REACH], ty_middle_ref[k - REACH])
        else:
            i = k if k < REACH else k - inner
            image = column_image(cy_ref[i], ty_ref[i])
        for kind in range(2):
            rows_ref[kind, k * SUB : (k + 1) * SUB] = image[kind]
    for kind in range(2):
        turned = rows_ref[kind].T
        for part in range(2):
            columns_ref[kind, part] = turned[part * layers : (part + 1) * layers]
    parts_of(columns_ref, kept_y_ref, sent_y_ref, lax.axis_index("by") & 1)


def column_image(colours, clears):
    colours, clears = colours.T, clears.T
    colour, clear = colours[:SUB], clears[:SUB]
    for c in range(1, CHUNKS):
        at = slice(c * SUB, (c + 1) * SUB)
        colour = colour + clear * colours[at]
        clear = clear * clears[at]
    return colour, clear


def merge_kernel(level, kept_ref, received_ref, *refs):
    me = lax.axis_index("by") >> (level - 1)
    later = (me & 1) == 1
    kept, received = kept_ref[...], received_ref[...]
    front = jnp.where(later, received, kept)
    back = jnp.where(later, kept, received)
    many = kept.shape[0]
    colour = front[:, 0] + front[:, 1] * back[:, 0]
    clear = front[:, 1] * back[:, 1]
    if many == 1:
        refs[0][0] = colour[0]
        refs[0][1] = clear[0]
        return
    out_kept_ref, out_sent_ref = refs
    bit = ((me >> 1) & 1) == 1
    for r in range(many // 2):
        for kind, value in enumerate((colour, clear)):
            even, odd = value[2 * r], value[2 * r + 1]
            out_kept_ref[r, kind] = jnp.where(bit, odd, even)
            out_sent_ref[r, kind] = jnp.where(bit, even, odd)


def merge_x_kernel(*refs):
    ins, outs = refs[:4], refs[4:]
    many, _, some, _, _ = ins[0].shape
    at = lax.axis_index("bx")
    later = (at & 1) == 1
    for i in range(2):
        kept_ref, received_ref = ins[2 * i], ins[2 * i + 1]
        for t in range(many):
            r = lax.rem((at >> 1) + t, many)
            kept, received = kept_ref[r], received_ref[r]
            front = jnp.where(later, received, kept)
            back = jnp.where(later, kept, received)
            outs[t][0, i * some : (i + 1) * some] = front[0] + front[1] * back[0]
            outs[t][1, i * some : (i + 1) * some] = front[1] * back[1]


def fold_x_kernel(*refs):
    pieces, out_ref = refs[:-1], refs[-1]
    _, run, share, _ = pieces[0].shape
    lane = iota((share, LANES), 1)
    me = lax.axis_index("bx") >> 1
    kinds = [[], []]
    for y in range(run):
        behind = colour, clear = jnp.zeros((share, LANES), F32), jnp.ones((share, LANES), F32)
        for s in reversed(range(len(pieces))):
            start = me == s
            behind = jnp.where(start, colour, behind[0]), jnp.where(start, clear, behind[1])
            colour, clear = jnp.where(start, 0.0, colour), jnp.where(start, 1.0, clear)
            colour = colour + clear * pieces[s][0, y]
            clear = clear * pieces[s][1, y]
        kinds[0].append(colour + clear * behind[0])
        kinds[1].append(clear * behind[1])
    for kind, values in enumerate(kinds):
        for s in (1, 2, 4):
            for i in range(run):
                if not i & s:
                    a, b = values[i], values[i | s]
                    odd = (lane & s) != 0
                    values[i] = jnp.where(odd, pltpu.roll(b, s, axis=1), a)
                    values[i | s] = jnp.where(odd, b, pltpu.roll(a, LANES - s, axis=1))
        for band, value in enumerate(values):
            out_ref[kind, band] = value


def exchange(last, first, axis):
    peers = lax.axis_size(axis)
    up = [(i, (i + 1) % peers) for i in range(peers)]
    down = [(j, i) for i, j in up]
    return lax.ppermute(last, axis, up), lax.ppermute(first, axis, down)


def swap(value, axis, bit):
    return lax.ppermute(value, axis, [(i, i ^ bit) for i in range(lax.axis_size(axis))])


def body(scalar_field, transfer_in, transfer_out):
    layers, local_x, local_y = scalar_field.shape
    units, feats = transfer_in.shape
    channels = transfer_out.shape[0]
    bands = channels // 2
    count_x, count_y = lax.axis_size("bx"), lax.axis_size("by")
    steps = (2.0 / (local_x * count_x), 2.0 / (local_y * count_y))
    half, run, rows = local_x // 2, local_y // CHUNKS, rows_of(local_y)
    sds = lambda *shape: jax.ShapeDtypeStruct(shape, F32)
    weights = [
        jax.ShapeDtypeStruct((feats * CHUNKS, units * CHUNKS), BF16),
        jax.ShapeDtypeStruct((units * CHUNKS, channels * CHUNKS), BF16),
    ]

    edge = sds(REACH, half, LANES)
    turned, first, last = call(turn_kernel, "turn", [sds(half, rows, LANES), edge, edge], 1)(
        scalar_field
    )
    before, after = exchange(last, first, "by")
    edge = sds(REACH, rows // 2, LANES)
    wide, first, last = call(
        functools.partial(sides_kernel, local_y, count_y), "sides", [sds(half, rows, LANES), edge, edge], 3
    )(turned, before, after)
    before, after = exchange(last, first, "bx")
    inner = half - 2 * REACH
    counts = (count_x, count_y)
    plane = lambda *lead: sds(*lead, CHUNKS, LANES)
    many_x, many_y = inner, 2
    win, wout, once, twice, ridge, colour_x, clear_x, colour_y, clear_y = call(
        functools.partial(middle_kernel, (many_x, many_y), counts, steps),
        "middle",
        weights + [plane(2, 4, run + 4), plane(2, 2, run + 2), plane(2, 2, run + 2)]
        + [sds(run, LANES, LANES)] * 2
        + [sds(inner, LANES, LANES)] * 2,
        3,
        [
            pltpu.VMEM((inner + 4, run + 4, CHUNKS, LANES), F32),
            pltpu.VMEM((inner + 2, run + 2, CHUNKS, LANES), F32),
            pltpu.VMEM((inner + 2, run + 2, CHUNKS, LANES), F32),
        ],
    )(wide, transfer_in, transfer_out)
    share = layers // count_x
    share_y = layers // count_y
    parts = sds(count_x // 2, 2, run // 2, share, LANES)
    parts_y = sds(count_y // 2, 2, 2, share_y, LANES)
    image = pltpu.VMEM((2, run // 2, layers, LANES), F32)
    ray = pltpu.VMEM((2 * REACH, LANES, LANES), F32)
    field = plane(2, 5, run + 2)
    twice, ridge, colour_ends, clear_ends, kept, sent = call(
        functools.partial(ends_first_kernel, counts, steps),
        "ends_first",
        [field] * 2 + [sds(2 * REACH, LANES, LANES)] * 2 + [parts] * 2,
        10,
        [
            image,
            pltpu.VMEM((2, 5, rows, LANES), F32),
            pltpu.VMEM((2, 7, run + 4, CHUNKS, LANES), F32),
        ],
    )(wide, before, after, win, wout, once, twice, ridge, colour_x, clear_x)
    halves = [kept, swap(sent, "bx", 1)]
    kept, sent, kept_y, sent_y = call(
        functools.partial(ends_last_kernel, counts, steps),
        "ends_last",
        [parts] * 2 + [parts_y] * 2,
        10,
        [
            image,
            ray,
            ray,
            pltpu.VMEM((2, LANES, LANES), F32),
            pltpu.VMEM((2, 2, layers, LANES), F32),
        ],
    )(win, wout, twice, ridge, colour_x, clear_x, colour_ends, clear_ends, colour_y, clear_y)
    halves += [kept, swap(sent, "bx", 1)]

    level, many = 1, count_y // 2
    while many:
        received = swap(sent_y, "by", level)
        merge = functools.partial(merge_kernel, level.bit_length())
        if many > 1:
            half_parts = sds(many // 2, 2, 2, share_y, LANES)
            kept_y, sent_y = call(merge, "merge", [half_parts] * 2, 2)(kept_y, received)
        else:
            view_y = call(merge, "merge", sds(2, 2, share_y, LANES), 2)(kept_y, received)
        level, many = 2 * level, many // 2
    many = count_x // 2
    piece = sds(2, run, share, LANES)
    pieces = list(call(merge_x_kernel, "merge_x", [piece] * many, 4)(*halves))
    for t in range(1, many):
        pairs = [(i, (i + 2 * t) % count_x) for i in range(count_x)]
        pieces[t] = lax.ppermute(pieces[t], "bx", pairs)
    view_x = call(fold_x_kernel, "fold_x", sds(2, bands, share, local_y), many)(*pieces)
    view_y = view_y.reshape(2, 2, share_y, half, bands)
    view_y = jnp.transpose(view_y, (0, 4, 2, 1, 3)).reshape(2, bands, share_y, local_x)
    return (view_x, view_y)


def solution(mesh):
    return jax.shard_map(
        body,
        mesh=mesh,
        in_specs=(P(None, "bx", "by"), P(), P()),
        out_specs=(P(None, None, "bx", "by"), P(None, None, "by", "bx")),
        check_vma=False,
    )
```

```python
import functools

import jax
import jax.numpy as jnp
from jax import lax
from jax.experimental import pallas as pl
from jax.experimental.pallas import tpu as pltpu
from jax.sharding import PartitionSpec as P

F32 = jnp.float32
BF16 = jnp.bfloat16
LOG2E = 1.4426950408889634
SUB = 8
LANES = 128
CHUNKS = 16
REACH = 3
AHEAD = 2
VMEM = pl.BlockSpec(memory_space=pltpu.VMEM)
PARAMS = pltpu.CompilerParams(vmem_limit_bytes=36 * 1024 * 1024)


def call(kernel, name, outs, count, scratch=()):
    return pl.pallas_call(
        kernel,
        out_shape=outs,
        in_specs=[VMEM] * count,
        out_specs=jax.tree.map(lambda _: VMEM, outs),
        scratch_shapes=scratch,
        compiler_params=PARAMS,
        name=name,
    )


def rows_of(width):
    return -(-(width + 2 * REACH) // 16) * 16


def iota(shape, dim):
    return lax.broadcasted_iota(jnp.int32, shape, dim)


def one_hot(mask):
    return jnp.where(mask, 1.0, 0.0).astype(BF16)


def spread(weights, left, right, mask):
    inner = lax.dot_general(
        left, weights, (((1,), (1,)), ((), ())), preferred_element_type=F32
    ).astype(BF16)
    return jnp.where(mask, jnp.dot(inner, right, preferred_element_type=F32), 0.0)


def is_even(axis):
    return (lax.axis_index(axis) & 1) == 0


def to_partners(axis, first, last):
    even = is_even(axis)
    return jnp.where(even, last, first), jnp.where(even, first, last)


def from_partners(axis, peers, pair, other):
    at, even = lax.axis_index(axis), is_even(axis)
    before, after = jnp.where(even, other, pair), jnp.where(even, pair, other)
    return jnp.where(at == 0, 0.0, before), jnp.where(at == peers - 1, 0.0, after)


def turn_kernel(field_ref, pair_ref, other_ref, turned_ref):
    layers, length, width = field_ref.shape
    half = length // 2
    for k in range(half):
        turned = jnp.concatenate([field_ref[:, k, :], field_ref[:, k + half, :]], axis=0).T
        turned_ref[k, REACH : REACH + width] = turned
        first, last = turned[:REACH], turned[width - REACH :]
        pair, other = to_partners("by", first, last)
        for j in range(REACH):
            pair_ref[j, k : k + 1] = pair[j : j + 1]
            other_ref[j, k : k + 1] = other[j : j + 1]


def spread_weights(in_ref, out_ref, win_ref, wout_ref):
    units, feats = in_ref.shape
    channels = out_ref.shape[0]
    bands = channels // 2
    rows, cols = feats * CHUNKS, units * CHUNKS
    left = one_hot(iota((rows, feats), 0) // CHUNKS == iota((rows, feats), 1))
    right = one_hot(iota((units, cols), 1) // CHUNKS == iota((units, cols), 0))
    mask = iota((rows, cols), 0) % CHUNKS == iota((rows, cols), 1) % CHUNKS
    win_ref[...] = (0.5 * spread(in_ref[...], left, right, mask)).astype(BF16)
    rows, cols = cols, channels * CHUNKS
    left = one_hot(iota((rows, units), 0) // CHUNKS == iota((rows, units), 1))
    at = iota((channels, cols), 1)
    right = one_hot((at // LANES) * bands + at % bands == iota((channels, cols), 0))
    mask = iota((rows, cols), 0) % CHUNKS == (iota((rows, cols), 1) % LANES) // bands
    wout_ref[...] = spread(out_ref[...], left, right, mask).astype(BF16)


def sides_kernel(
    width, count_y, turned_ref, pair_in_ref, other_in_ref, wide_ref, pair_ref, other_ref
):
    half, rows, _ = turned_ref.shape
    layers = LANES // 2
    part = rows // 2
    front = iota((part, LANES), 1) < layers
    befores, afters = from_partners("by", count_y, pair_in_ref[...], other_in_ref[...])
    for k in range(half):
        wide_ref[k, REACH : REACH + width] = turned_ref[k, REACH : REACH + width]
        for j in range(REACH):
            at = REACH + width + j
            wide_ref[k, j : j + 1] = befores[j, k : k + 1]
            wide_ref[k, at : at + 1] = afters[j, k : k + 1]
        wide_ref[k, 2 * REACH + width :] = jnp.zeros((rows - 2 * REACH - width, LANES), F32)
    for j in range(REACH):
        top, low = wide_ref[j, :part], wide_ref[j, part:]
        first = jnp.where(front, top, pltpu.roll(low, layers, axis=1))
        k = half - REACH + j
        top, low = wide_ref[k, :part], wide_ref[k, part:]
        last = jnp.where(front, pltpu.roll(top, layers, axis=1), low)
        pair_ref[j], other_ref[j] = to_partners("bx", first, last)


class Stencil:
    def __init__(self, run, counts):
        self.run = run
        self.layers = layers = LANES // 2
        self.shape = (CHUNKS, LANES)
        lane, chunk = iota(self.shape, 1), iota(self.shape, 0)
        z = lane % layers
        self.near = (z > 0).astype(F32)
        self.far = (z < layers - 1).astype(F32)
        at_x, at_y = lax.axis_index("bx"), lax.axis_index("by")
        count_x, count_y = counts
        self.x_low = jnp.where((lane < layers) & (at_x == 0), 0.0, 1.0)
        self.x_high = jnp.where((lane >= layers) & (at_x == count_x - 1), 0.0, 1.0)
        self.y_low = jnp.where((chunk == 0) & (at_y == 0), 0.0, 1.0)
        self.y_high = jnp.where((chunk == CHUNKS - 1) & (at_y == count_y - 1), 0.0, 1.0)

    def z_sum(self, value):
        return roll(value, 1) * self.near + roll(value, -1) * self.far

    def inside(self, value, y, edge):
        if edge is not None:
            value = value * edge
        if y < 0:
            value = value * self.y_low
        if y >= self.run:
            value = value * self.y_high
        return value

    def smooth(self, centre, others):
        total = self.z_sum(centre)
        for other in others:
            total = total + other
        return 0.4 * centre + 0.1 * total

    def raw(self, ref, k, y):
        return ref[k, pl.ds(y + REACH, CHUNKS, stride=self.run), :]

    def once(self, raw, k, out, at, edge=None):
        column = [self.raw(raw, k, y) for y in range(-3, self.run + 3)]
        for i in range(1, len(column) - 1):
            y = i - 3
            sides = [self.raw(raw, k - 1, y), self.raw(raw, k + 1, y)]
            value = self.smooth(column[i], [column[i - 1], column[i + 1]] + sides)
            out[at, i - 1] = self.inside(value, y, edge)

    def twice(self, once, k, out, ridge, slope, at, edge=None):
        column = [once[k, i] for i in range(self.run + 4)]
        for i in range(1, len(column) - 1):
            sides = [once[k - 1, i], once[k + 1, i]]
            value = self.smooth(column[i], [column[i - 1], column[i + 1]] + sides)
            value = self.inside(value, i - 2, edge)
            out[at, i - 1] = value
            below, above = roll(value, 1) * self.near, roll(value, -1) * self.far
            ridge[at, i - 1] = 2.0 * value + (below + above)
            slope[at, i - 1] = above - below

    def features(self, twice, ridge, slope, k, y):
        p = lambda a, b: twice[k + a, y + 1 + b]
        r = lambda a, b: ridge[k + a, y + 1 + b]
        centre = p(0, 0)
        main, cross = p(1, 1) - p(-1, -1), p(1, -1) - p(-1, 1)
        third = 1.0 / 3.0
        gx = (main + cross + (r(1, 0) - r(-1, 0))) * third
        gy = (main - cross + (r(0, 1) - r(0, -1))) * third
        d = lambda a, b: slope[k + a, y + 1 + b]
        gz = (2.0 * d(0, 0) + ((d(1, 0) + d(-1, 0)) + (d(0, 1) + d(0, -1)))) * third
        m = jnp.sqrt(1.0 + gx * gx + gy * gy + gz * gz)
        parts = [centre, gx, gy, gz, m, centre * m, centre * centre]
        packed = [part.astype(BF16) for part in parts] + [jnp.ones(self.shape, BF16)]
        return jnp.concatenate(packed, axis=0).T


def roll(value, shift):
    return pltpu.roll(value, shift % LANES, axis=1)


def network(tiles, win_ref, wout_ref, step):
    cells = jnp.concatenate(tiles, axis=0)
    half_v = jnp.dot(cells, win_ref[...], preferred_element_type=F32)
    hidden = (half_v + half_v * jnp.tanh(half_v)).astype(BF16)
    v = jnp.dot(hidden, wout_ref[...], preferred_element_type=F32)
    soft = jnp.maximum(v, jnp.log(1.0 + jnp.exp2(jnp.minimum(v * LOG2E, 126.0))))
    return soft[:, :LANES], jnp.exp2(soft[:, LANES:] * (-LOG2E * step))


def clear_of_x(q, ratio):
    if ratio == 1.0:
        return q
    if ratio == 2.0:
        return q * q
    return jnp.exp2(jnp.log(q) * (LOG2E * ratio))


def step_ray(ray, clear, emission):
    colour, light = ray
    later = light * clear
    return colour + (light - later) * emission, later


def middle_kernel(
    spans,
    counts,
    steps,
    wide_ref,
    in_ref,
    out_ref,
    win_ref,
    wout_ref,
    once_out_ref,
    twice_out_ref,
    ridge_out_ref,
    slope_out_ref,
    cx_ref,
    tx_ref,
    cy_ref,
    ty_ref,
    once_ref,
    twice_ref,
    ridge_ref,
    slope_ref,
):
    half = wide_ref.shape[0]
    run = cx_ref.shape[0]
    stencil = Stencil(run, counts)
    inner = half - 2 * REACH
    spread_weights(in_ref, out_ref, win_ref, wout_ref)
    for k in range(run):
        tx_ref[k] = jnp.ones((LANES, LANES), F32)
        cx_ref[k] = jnp.zeros((LANES, LANES), F32)
    for k in range(inner):
        ty_ref[k] = jnp.ones((LANES, LANES), F32)
        cy_ref[k] = jnp.zeros((LANES, LANES), F32)
    ratio = steps[0] / steps[1]

    def prepare(first, last):
        start = 0 if first == 0 else first + 2
        for k in range(start, last + 2):
            stencil.once(wide_ref, k + 1, once_ref, k)
        for k in range(first, last):
            stencil.twice(once_ref, k + 1, twice_ref, ridge_ref, slope_ref, k)

    def block(x0, y0, many_x, many_y):
        tiles = [
            stencil.features(twice_ref, ridge_ref, slope_ref, x0 + i + 1, y0 + j)
            for j in range(many_y)
            for i in range(many_x)
        ]
        emission, clear = network(tiles, win_ref, wout_ref, steps[1])
        for g in range(LANES // SUB):
            at = pl.ds(g * SUB, SUB)
            rays_y = [(cy_ref[x0 + i, at], ty_ref[x0 + i, at]) for i in range(many_x)]
            for j in range(many_y):
                ray_x = cx_ref[y0 + j, at], tx_ref[y0 + j, at]
                for i in range(many_x):
                    start = (j * many_x + i) * LANES + g * SUB
                    e, q = emission[start : start + SUB], clear[start : start + SUB]
                    rays_y[i] = step_ray(rays_y[i], q, e)
                    ray_x = step_ray(ray_x, clear_of_x(q, ratio), e)
                cx_ref[y0 + j, at], tx_ref[y0 + j, at] = ray_x
            for i in range(many_x):
                cy_ref[x0 + i, at], ty_ref[x0 + i, at] = rays_y[i]

    many_x, many_y = spans
    ready = 0
    for x0 in range(0, inner, many_x):
        ahead = min(inner + 2, x0 + many_x + 2 + AHEAD)
        prepare(ready, ahead)
        ready = ahead
        for y0 in range(0, run, many_y):
            block(x0, y0, many_x, many_y)
    for k in range(4):
        once_out_ref[0, k] = once_ref[k]
        once_out_ref[1, k] = once_ref[inner + k]
    for k in range(2):
        for out_ref, ref in ((twice_out_ref, twice_ref), (ridge_out_ref, ridge_ref)):
            out_ref[0, k] = ref[k]
            out_ref[1, k] = ref[inner + k]
        slope_out_ref[0, k] = slope_ref[k]
        slope_out_ref[1, k] = slope_ref[inner + k]


def parts_of(image_ref, kept_ref, sent_ref, mine):
    many, share = kept_ref.shape[0], kept_ref.shape[3]
    for r in range(many):
        for out_ref, bit in ((kept_ref, mine), (sent_ref, 1 - mine)):
            start = pl.multiple_of((2 * r + bit) * share, share)
            out_ref[r] = image_ref[:, :, pl.ds(start, share), :]


def march_ends(stencil, steps, first, weights, fields, middle, rays, image_ref):
    cx_ref, tx_ref = middle
    cy_ref, ty_ref = rays
    layers = stencil.layers
    many_y = image_ref.shape[1]
    ratio = steps[0] / steps[1]
    planes = [(0, 1), (0, 2), (0, 3), (1, 1), (1, 2), (1, 3)]
    tiles = [
        stencil.features(*[ref.at[side] for ref in fields], k, first + j)
        for j in range(many_y)
        for side, k in planes
    ]
    emission, clear = network(tiles, *weights, steps[1])
    images = [[], []]
    for g in range(LANES // SUB):
        at = pl.ds(g * SUB, SUB)
        rays_y = [(cy_ref[i, at], ty_ref[i, at]) for i in range(len(planes))]
        for j in range(many_y):
            ray_x = jnp.zeros((SUB, LANES), F32), jnp.ones((SUB, LANES), F32)
            for i in range(len(planes)):
                if i == REACH:
                    colour, light = ray_x
                    colour = colour + light * cx_ref[first + j, at]
                    ray_x = colour, light * tx_ref[first + j, at]
                start = (j * len(planes) + i) * LANES + g * SUB
                e, q = emission[start : start + SUB], clear[start : start + SUB]
                rays_y[i] = step_ray(rays_y[i], q, e)
                ray_x = step_ray(ray_x, clear_of_x(q, ratio), e)
            images[0].append(ray_x[0])
            images[1].append(ray_x[1])
        for i in range(len(planes)):
            cy_ref[i, at], ty_ref[i, at] = rays_y[i]
    for d in range(layers // SUB):
        for j in range(many_y):
            near, far = d * many_y + j, (d + layers // SUB) * many_y + j
            q = images[1][near]
            at = pl.ds(d * SUB, SUB)
            image_ref[0, j, at] = images[0][near] + q * images[0][far]
            image_ref[1, j, at] = q * images[1][far]


def ends_first_kernel(
    counts,
    steps,
    wide_ref,
    pair_ref,
    other_ref,
    win_ref,
    wout_ref,
    once_in_ref,
    twice_in_ref,
    ridge_in_ref,
    slope_in_ref,
    cx_ref,
    tx_ref,
    twice_ref,
    ridge_ref,
    slope_ref,
    cy_ref,
    ty_ref,
    kept_ref,
    sent_ref,
    image_ref,
    raw_ref,
    once_ref,
):
    half, rows, _ = wide_ref.shape
    run = cx_ref.shape[0]
    layers = LANES // 2
    stencil = Stencil(run, counts)
    part = rows // 2
    front = iota((part, LANES), 1) < layers
    at_x = lax.axis_index("bx")
    for j in range(REACH):
        before, after = from_partners("bx", counts[0], pair_ref[j], other_ref[j])
        halo, own = before, wide_ref[half - REACH + j]
        raw_ref[0, j, :part] = jnp.where(front, halo, roll(own[:part], layers))
        raw_ref[0, j, part:] = jnp.where(front, roll(halo, layers), roll(own[part:], layers))
        halo, own = after, wide_ref[j]
        raw_ref[1, 2 + j, :part] = jnp.where(front, roll(own[:part], layers), roll(halo, layers))
        raw_ref[1, 2 + j, part:] = jnp.where(front, roll(own[part:], layers), halo)
    for j in range(2):
        raw_ref[0, REACH + j] = wide_ref[j]
        raw_ref[1, j] = wide_ref[half - 2 + j]
    for k in range(4):
        once_ref[0, 3 + k] = once_in_ref[0, k]
        once_ref[1, k] = once_in_ref[1, k]
    for k in range(2):
        twice_ref[0, 3 + k] = twice_in_ref[0, k]
        twice_ref[1, k] = twice_in_ref[1, k]
        ridge_ref[0, 3 + k] = ridge_in_ref[0, k]
        ridge_ref[1, k] = ridge_in_ref[1, k]
        slope_ref[0, 3 + k] = slope_in_ref[0, k]
        slope_ref[1, k] = slope_in_ref[1, k]
    for side, edge in enumerate((stencil.x_low, stencil.x_high)):
        outside = (0, 1) if side == 0 else (1, 2)
        for k in range(3):
            kept = edge if k in outside else None
            stencil.once(raw_ref.at[side], k + 1, once_ref.at[side], k + 4 * side, kept)
    for side, edge in enumerate((stencil.x_low, stencil.x_high)):
        for k in range(3):
            kept = edge if k == 2 * side else None
            at = k + 2 * side
            outs = [ref.at[side] for ref in (twice_ref, ridge_ref, slope_ref)]
            stencil.twice(once_ref.at[side], at + 1, *outs, at, kept)
    for k in range(2 * REACH):
        ty_ref[k] = jnp.ones((LANES, LANES), F32)
        cy_ref[k] = jnp.zeros((LANES, LANES), F32)
    march_ends(
        stencil,
        steps,
        0,
        (win_ref, wout_ref),
        (twice_ref, ridge_ref, slope_ref),
        (cx_ref, tx_ref),
        (cy_ref, ty_ref),
        image_ref,
    )
    parts_of(image_ref, kept_ref, sent_ref, at_x & 1)


def ends_last_kernel(
    counts,
    steps,
    win_ref,
    wout_ref,
    twice_ref,
    ridge_ref,
    slope_ref,
    cx_ref,
    tx_ref,
    cy_in_ref,
    ty_in_ref,
    cy_middle_ref,
    ty_middle_ref,
    kept_ref,
    sent_ref,
    kept_y_ref,
    sent_y_ref,
    image_ref,
    cy_ref,
    ty_ref,
    rows_ref,
    columns_ref,
):
    run = cx_ref.shape[0]
    stencil = Stencil(run, counts)
    layers = stencil.layers
    cy_ref[...] = cy_in_ref[...]
    ty_ref[...] = ty_in_ref[...]
    march_ends(
        stencil,
        steps,
        run - image_ref.shape[1],
        (win_ref, wout_ref),
        (twice_ref, ridge_ref, slope_ref),
        (cx_ref, tx_ref),
        (cy_ref, ty_ref),
        image_ref,
    )
    parts_of(image_ref, kept_ref, sent_ref, lax.axis_index("bx") & 1)
    inner = cy_middle_ref.shape[0]
    half = inner + 2 * REACH
    for k in range(half):
        if REACH <= k < REACH + inner:
            image = column_image(cy_middle_ref[k - REACH], ty_middle_ref[k - REACH])
        else:
            i = k if k < REACH else k - inner
            image = column_image(cy_ref[i], ty_ref[i])
        for kind in range(2):
            rows_ref[kind, k * SUB : (k + 1) * SUB] = image[kind]
    for kind in range(2):
        turned = rows_ref[kind].T
        for part in range(2):
            columns_ref[kind, part] = turned[part * layers : (part + 1) * layers]
    parts_of(columns_ref, kept_y_ref, sent_y_ref, lax.axis_index("by") & 1)


def column_image(colours, clears):
    colours, clears = colours.T, clears.T
    colour, clear = colours[:SUB], clears[:SUB]
    for c in range(1, CHUNKS):
        at = slice(c * SUB, (c + 1) * SUB)
        colour = colour + clear * colours[at]
        clear = clear * clears[at]
    return colour, clear


def merge_kernel(level, kept_ref, received_ref, *refs):
    me = lax.axis_index("by") >> (level - 1)
    later = (me & 1) == 1
    kept, received = kept_ref[...], received_ref[...]
    front = jnp.where(later, received, kept)
    back = jnp.where(later, kept, received)
    many = kept.shape[0]
    colour = front[:, 0] + front[:, 1] * back[:, 0]
    clear = front[:, 1] * back[:, 1]
    if many == 1:
        refs[0][0] = colour[0]
        refs[0][1] = clear[0]
        return
    out_kept_ref, out_sent_ref = refs
    bit = ((me >> 1) & 1) == 1
    for r in range(many // 2):
        for kind, value in enumerate((colour, clear)):
            even, odd = value[2 * r], value[2 * r + 1]
            out_kept_ref[r, kind] = jnp.where(bit, odd, even)
            out_sent_ref[r, kind] = jnp.where(bit, even, odd)


def merge_x_kernel(kept_ref, received_ref, *refs):
    many, _, some, _, _ = kept_ref.shape
    outs = refs[-many:]
    at = lax.axis_index("bx")
    later = (at & 1) == 1
    for t in range(many):
        r = lax.rem((at >> 1) + t, many)
        kept, received = kept_ref[r], received_ref[r]
        front = jnp.where(later, received, kept)
        back = jnp.where(later, kept, received)
        outs[t][0] = front[0] + front[1] * back[0]
        outs[t][1] = front[1] * back[1]


def fold_x_kernel(*refs):
    out_ref = refs[-1]
    many = (len(refs) - 1) // 2
    _, some, share, _ = refs[0].shape
    run = 2 * some
    lane = iota((share, LANES), 1)
    me = lax.axis_index("bx") >> 1
    kinds = [[], []]
    for y in range(run):
        pieces = refs[(y // some) * many :][:many]
        behind = colour, clear = jnp.zeros((share, LANES), F32), jnp.ones((share, LANES), F32)
        for s in reversed(range(many)):
            start = me == s
            behind = jnp.where(start, colour, behind[0]), jnp.where(start, clear, behind[1])
            colour, clear = jnp.where(start, 0.0, colour), jnp.where(start, 1.0, clear)
            colour = colour + clear * pieces[s][0, y % some]
            clear = clear * pieces[s][1, y % some]
        kinds[0].append(colour + clear * behind[0])
        kinds[1].append(clear * behind[1])
    for kind, values in enumerate(kinds):
        for s in (1, 2, 4):
            for i in range(run):
                if not i & s:
                    a, b = values[i], values[i | s]
                    odd = (lane & s) != 0
                    values[i] = jnp.where(odd, pltpu.roll(b, s, axis=1), a)
                    values[i | s] = jnp.where(odd, b, pltpu.roll(a, LANES - s, axis=1))
        for band, value in enumerate(values):
            out_ref[kind, band] = value


def exchange(pair, other, axis, around):
    peers = lax.axis_size(axis)
    sides = [(i, (i + 1) % peers if i & 1 else (i - 1) % peers) for i in range(peers)]
    if not around:
        sides = [(i, i) if i in (0, peers - 1) else (i, j) for i, j in sides]
    return swap(pair, axis, 1), lax.ppermute(other, axis, sides)


def swap(value, axis, bit):
    return lax.ppermute(value, axis, [(i, i ^ bit) for i in range(lax.axis_size(axis))])


def body(scalar_field, transfer_in, transfer_out):
    layers, local_x, local_y = scalar_field.shape
    units, feats = transfer_in.shape
    channels = transfer_out.shape[0]
    bands = channels // 2
    count_x, count_y = lax.axis_size("bx"), lax.axis_size("by")
    steps = (2.0 / (local_x * count_x), 2.0 / (local_y * count_y))
    half, run, rows = local_x // 2, local_y // CHUNKS, rows_of(local_y)
    sds = lambda *shape: jax.ShapeDtypeStruct(shape, F32)
    weights = [
        jax.ShapeDtypeStruct((feats * CHUNKS, units * CHUNKS), BF16),
        jax.ShapeDtypeStruct((units * CHUNKS, channels * CHUNKS), BF16),
    ]

    edge = sds(REACH, half, LANES)
    pair, other, turned = call(turn_kernel, "turn", [edge, edge, sds(half, rows, LANES)], 1)(
        scalar_field
    )
    pair, other = exchange(pair, other, "by", True)
    edge = sds(REACH, rows // 2, LANES)
    wide, pair, other = call(
        functools.partial(sides_kernel, local_y, count_y), "sides", [sds(half, rows, LANES), edge, edge], 3
    )(turned, pair, other)
    pair, other = exchange(pair, other, "bx", False)
    inner = half - 2 * REACH
    counts = (count_x, count_y)
    plane = lambda *lead: sds(*lead, CHUNKS, LANES)
    many_x, many_y = inner, 2
    win, wout, once, twice, ridge, slope, colour_x, clear_x, colour_y, clear_y = call(
        functools.partial(middle_kernel, (many_x, many_y), counts, steps),
        "middle",
        weights + [plane(2, 4, run + 4)] + [plane(2, 2, run + 2)] * 3
        + [sds(run, LANES, LANES)] * 2
        + [sds(inner, LANES, LANES)] * 2,
        3,
        [
            pltpu.VMEM((inner + 4, run + 4, CHUNKS, LANES), F32),
            pltpu.VMEM((inner + 2, run + 2, CHUNKS, LANES), F32),
            pltpu.VMEM((inner + 2, run + 2, CHUNKS, LANES), F32),
            pltpu.VMEM((inner + 2, run + 2, CHUNKS, LANES), F32),
        ],
    )(wide, transfer_in, transfer_out)
    share = layers // count_x
    share_y = layers // count_y
    parts = sds(count_x // 2, 2, run // 2, share, LANES)
    parts_y = sds(count_y // 2, 2, 2, share_y, LANES)
    image = pltpu.VMEM((2, run // 2, layers, LANES), F32)
    ray = pltpu.VMEM((2 * REACH, LANES, LANES), F32)
    field = plane(2, 5, run + 2)
    twice, ridge, slope, colour_ends, clear_ends, kept, sent = call(
        functools.partial(ends_first_kernel, counts, steps),
        "ends_first",
        [field] * 3 + [sds(2 * REACH, LANES, LANES)] * 2 + [parts] * 2,
        11,
        [
            image,
            pltpu.VMEM((2, 5, rows, LANES), F32),
            pltpu.VMEM((2, 7, run + 4, CHUNKS, LANES), F32),
        ],
    )(wide, pair, other, win, wout, once, twice, ridge, slope, colour_x, clear_x)
    halves = [(kept, swap(sent, "bx", 1))]
    kept, sent, kept_y, sent_y = call(
        functools.partial(ends_last_kernel, counts, steps),
        "ends_last",
        [parts] * 2 + [parts_y] * 2,
        11,
        [
            image,
            ray,
            ray,
            pltpu.VMEM((2, LANES, LANES), F32),
            pltpu.VMEM((2, 2, layers, LANES), F32),
        ],
    )(
        win, wout, twice, ridge, slope, colour_x, clear_x, colour_ends, clear_ends, colour_y, clear_y
    )
    halves += [(kept, swap(sent, "bx", 1))]

    def send_round(*operands):
        many = count_x // 2
        piece = sds(2, run // 2, share, LANES)
        pieces = list(call(merge_x_kernel, "merge_x", [piece] * many, len(operands))(*operands))
        for t in range(1, many):
            pairs = [(i, (i + 2 * t) % count_x) for i in range(count_x)]
            pieces[t] = lax.ppermute(pieces[t], "bx", pairs)
        return pieces

    pieces = send_round(*halves[0])
    level, many = 1, count_y // 2
    while many:
        received = swap(sent_y, "by", level)
        merge = functools.partial(merge_kernel, level.bit_length())
        if many > 1:
            half_parts = sds(many // 2, 2, 2, share_y, LANES)
            kept_y, sent_y = call(merge, "merge", [half_parts] * 2, 2)(kept_y, received)
        else:
            view_y = call(merge, "merge", sds(2, 2, share_y, LANES), 2)(kept_y, received)
        level, many = 2 * level, many // 2
    pieces += send_round(*halves[1], sent_y)
    view_x = call(fold_x_kernel, "fold_x", sds(2, bands, share, local_y), count_x)(*pieces)
    view_y = view_y.reshape(2, 2, share_y, half, bands)
    view_y = jnp.transpose(view_y, (0, 4, 2, 1, 3)).reshape(2, bands, share_y, local_x)
    return (view_x, view_y)


def solution(mesh):
    return jax.shard_map(
        body,
        mesh=mesh,
        in_specs=(P(None, "bx", "by"), P(), P()),
        out_specs=(P(None, None, "bx", "by"), P(None, None, "by", "bx")),
        check_vma=False,
    )
```

```python
import functools

import jax
import jax.numpy as jnp
from jax import lax
from jax.experimental import pallas as pl
from jax.experimental.pallas import tpu as pltpu
from jax.sharding import PartitionSpec as P

F32 = jnp.float32
BF16 = jnp.bfloat16
LOG2E = 1.4426950408889634
SUB = 8
LANES = 128
CHUNKS = 16
REACH = 3
AHEAD = 2
VMEM = pl.BlockSpec(memory_space=pltpu.VMEM)
PARAMS = pltpu.CompilerParams(vmem_limit_bytes=36 * 1024 * 1024)


def call(kernel, name, outs, count, scratch=()):
    return pl.pallas_call(
        kernel,
        out_shape=outs,
        in_specs=[VMEM] * count,
        out_specs=jax.tree.map(lambda _: VMEM, outs),
        scratch_shapes=scratch,
        compiler_params=PARAMS,
        name=name,
    )


def rows_of(width):
    return -(-(width + 2 * REACH) // 16) * 16


def iota(shape, dim):
    return lax.broadcasted_iota(jnp.int32, shape, dim)


def one_hot(mask):
    return jnp.where(mask, 1.0, 0.0).astype(BF16)


def spread(weights, left, right, mask):
    inner = lax.dot_general(
        left, weights, (((1,), (1,)), ((), ())), preferred_element_type=F32
    ).astype(BF16)
    return jnp.where(mask, jnp.dot(inner, right, preferred_element_type=F32), 0.0)


def inside_grid(axis, peers, before, after):
    at = lax.axis_index(axis)
    return jnp.where(at == 0, 0.0, before), jnp.where(at == peers - 1, 0.0, after)


def turn_kernel(field_ref, turned_ref, first_ref, last_ref):
    layers, length, width = field_ref.shape
    half = length // 2
    for k in range(half):
        turned = jnp.concatenate([field_ref[:, k, :], field_ref[:, k + half, :]], axis=0).T
        turned_ref[k, REACH : REACH + width] = turned
        for j in range(REACH):
            first_ref[j, k : k + 1] = turned[j : j + 1]
            last_ref[j, k : k + 1] = turned[width - REACH + j : width - REACH + j + 1]


def spread_weights(in_ref, out_ref, win_ref, wout_ref):
    units, feats = in_ref.shape
    channels = out_ref.shape[0]
    bands = channels // 2
    rows, cols = feats * CHUNKS, units * CHUNKS
    left = one_hot(iota((rows, feats), 0) // CHUNKS == iota((rows, feats), 1))
    right = one_hot(iota((units, cols), 1) // CHUNKS == iota((units, cols), 0))
    mask = iota((rows, cols), 0) % CHUNKS == iota((rows, cols), 1) % CHUNKS
    win_ref[...] = (0.5 * spread(in_ref[...], left, right, mask)).astype(BF16)
    rows, cols = cols, channels * CHUNKS
    left = one_hot(iota((rows, units), 0) // CHUNKS == iota((rows, units), 1))
    at = iota((channels, cols), 1)
    right = one_hot((at // LANES) * bands + at % bands == iota((channels, cols), 0))
    mask = iota((rows, cols), 0) % CHUNKS == (iota((rows, cols), 1) % LANES) // bands
    wout_ref[...] = spread(out_ref[...], left, right, mask).astype(BF16)


def sides_kernel(
    width, count_y, turned_ref, before_ref, after_ref, wide_ref, first_ref, last_ref
):
    half, rows, _ = turned_ref.shape
    layers = LANES // 2
    part = rows // 2
    front = iota((part, LANES), 1) < layers
    befores, afters = inside_grid("by", count_y, before_ref[...], after_ref[...])
    for k in range(half):
        wide_ref[k, REACH : REACH + width] = turned_ref[k, REACH : REACH + width]
        for j in range(REACH):
            at = REACH + width + j
            wide_ref[k, j : j + 1] = befores[j, k : k + 1]
            wide_ref[k, at : at + 1] = afters[j, k : k + 1]
        wide_ref[k, 2 * REACH + width :] = jnp.zeros((rows - 2 * REACH - width, LANES), F32)
    for j in range(REACH):
        top, low = wide_ref[j, :part], wide_ref[j, part:]
        first_ref[j] = jnp.where(front, top, pltpu.roll(low, layers, axis=1))
        k = half - REACH + j
        top, low = wide_ref[k, :part], wide_ref[k, part:]
        last_ref[j] = jnp.where(front, pltpu.roll(top, layers, axis=1), low)


class Stencil:
    def __init__(self, run, counts):
        self.run = run
        self.layers = layers = LANES // 2
        self.shape = (CHUNKS, LANES)
        lane, chunk = iota(self.shape, 1), iota(self.shape, 0)
        z = lane % layers
        self.near = (z > 0).astype(F32)
        self.far = (z < layers - 1).astype(F32)
        at_x, at_y = lax.axis_index("bx"), lax.axis_index("by")
        count_x, count_y = counts
        self.x_low = jnp.where((lane < layers) & (at_x == 0), 0.0, 1.0)
        self.x_high = jnp.where((lane >= layers) & (at_x == count_x - 1), 0.0, 1.0)
        self.y_low = jnp.where((chunk == 0) & (at_y == 0), 0.0, 1.0)
        self.y_high = jnp.where((chunk == CHUNKS - 1) & (at_y == count_y - 1), 0.0, 1.0)

    def z_sum(self, value):
        return roll(value, 1) * self.near + roll(value, -1) * self.far

    def inside(self, value, y, edge):
        if edge is not None:
            value = value * edge
        if y < 0:
            value = value * self.y_low
        if y >= self.run:
            value = value * self.y_high
        return value

    def smooth(self, centre, others):
        total = self.z_sum(centre)
        for other in others:
            total = total + other
        return 0.4 * centre + 0.1 * total

    def raw(self, ref, k, y):
        return ref[k, pl.ds(y + REACH, CHUNKS, stride=self.run), :]

    def once(self, raw, k, out, at, edge=None):
        column = [self.raw(raw, k, y) for y in range(-3, self.run + 3)]
        for i in range(1, len(column) - 1):
            y = i - 3
            sides = [self.raw(raw, k - 1, y), self.raw(raw, k + 1, y)]
            value = self.smooth(column[i], [column[i - 1], column[i + 1]] + sides)
            out[at, i - 1] = self.inside(value, y, edge)

    def twice(self, once, k, out, ridge, slope, at, edge=None):
        column = [once[k, i] for i in range(self.run + 4)]
        for i in range(1, len(column) - 1):
            sides = [once[k - 1, i], once[k + 1, i]]
            value = self.smooth(column[i], [column[i - 1], column[i + 1]] + sides)
            value = self.inside(value, i - 2, edge)
            out[at, i - 1] = value
            below, above = roll(value, 1) * self.near, roll(value, -1) * self.far
            ridge[at, i - 1] = 2.0 * value + (below + above)
            slope[at, i - 1] = above - below

    def features(self, twice, ridge, slope, k, y):
        p = lambda a, b: twice[k + a, y + 1 + b]
        r = lambda a, b: ridge[k + a, y + 1 + b]
        centre = p(0, 0)
        main, cross = p(1, 1) - p(-1, -1), p(1, -1) - p(-1, 1)
        third = 1.0 / 3.0
        gx = (main + cross + (r(1, 0) - r(-1, 0))) * third
        gy = (main - cross + (r(0, 1) - r(0, -1))) * third
        d = lambda a, b: slope[k + a, y + 1 + b]
        gz = (2.0 * d(0, 0) + ((d(1, 0) + d(-1, 0)) + (d(0, 1) + d(0, -1)))) * third
        square = 1.0 + gx * gx + gy * gy + gz * gz
        m = square * lax.rsqrt(square)
        parts = [centre, gx, gy, gz, m, centre * m, centre * centre]
        packed = [part.astype(BF16) for part in parts] + [jnp.ones(self.shape, BF16)]
        return jnp.concatenate(packed, axis=0).T


def roll(value, shift):
    return pltpu.roll(value, shift % LANES, axis=1)


def network(tiles, win_ref, wout_ref, step):
    cells = jnp.concatenate(tiles, axis=0)
    half_v = jnp.dot(cells, win_ref[...], preferred_element_type=F32)
    hidden = (half_v + half_v * jnp.tanh(half_v)).astype(BF16)
    v = jnp.dot(hidden, wout_ref[...], preferred_element_type=F32)
    soft = jnp.maximum(v, jnp.log(1.0 + jnp.exp2(jnp.minimum(v * LOG2E, 126.0))))
    return soft[:, :LANES], jnp.exp2(soft[:, LANES:] * (-LOG2E * step))


def clear_of_x(q, ratio):
    if ratio == 1.0:
        return q
    if ratio == 2.0:
        return q * q
    return jnp.exp2(jnp.log(q) * (LOG2E * ratio))


def step_ray(ray, clear, emission):
    colour, light = ray
    later = light * clear
    return colour + (light - later) * emission, later


def middle_kernel(
    spans,
    counts,
    steps,
    wide_ref,
    in_ref,
    out_ref,
    win_ref,
    wout_ref,
    once_out_ref,
    twice_out_ref,
    ridge_out_ref,
    slope_out_ref,
    cx_ref,
    tx_ref,
    cy_ref,
    ty_ref,
    once_ref,
    twice_ref,
    ridge_ref,
    slope_ref,
):
    half = wide_ref.shape[0]
    run = cx_ref.shape[0]
    stencil = Stencil(run, counts)
    inner = half - 2 * REACH
    spread_weights(in_ref, out_ref, win_ref, wout_ref)
    for k in range(run):
        tx_ref[k] = jnp.ones((LANES, LANES), F32)
        cx_ref[k] = jnp.zeros((LANES, LANES), F32)
    for k in range(inner):
        ty_ref[k] = jnp.ones((LANES, LANES), F32)
        cy_ref[k] = jnp.zeros((LANES, LANES), F32)
    ratio = steps[0] / steps[1]

    def prepare(first, last):
        start = 0 if first == 0 else first + 2
        for k in range(start, last + 2):
            stencil.once(wide_ref, k + 1, once_ref, k)
        for k in range(first, last):
            stencil.twice(once_ref, k + 1, twice_ref, ridge_ref, slope_ref, k)

    def block(x0, y0, many_x, many_y):
        tiles = [
            stencil.features(twice_ref, ridge_ref, slope_ref, x0 + i + 1, y0 + j)
            for j in range(many_y)
            for i in range(many_x)
        ]
        emission, clear = network(tiles, win_ref, wout_ref, steps[1])
        for g in range(LANES // SUB):
            at = pl.ds(g * SUB, SUB)
            rays_y = [(cy_ref[x0 + i, at], ty_ref[x0 + i, at]) for i in range(many_x)]
            for j in range(many_y):
                ray_x = cx_ref[y0 + j, at], tx_ref[y0 + j, at]
                for i in range(many_x):
                    start = (j * many_x + i) * LANES + g * SUB
                    e, q = emission[start : start + SUB], clear[start : start + SUB]
                    rays_y[i] = step_ray(rays_y[i], q, e)
                    ray_x = step_ray(ray_x, clear_of_x(q, ratio), e)
                cx_ref[y0 + j, at], tx_ref[y0 + j, at] = ray_x
            for i in range(many_x):
                cy_ref[x0 + i, at], ty_ref[x0 + i, at] = rays_y[i]

    many_x, many_y = spans
    ready = 0
    for x0 in range(0, inner, many_x):
        ahead = min(inner + 2, x0 + many_x + 2 + AHEAD)
        prepare(ready, ahead)
        ready = ahead
        for y0 in range(0, run, many_y):
            block(x0, y0, many_x, many_y)
    for k in range(4):
        once_out_ref[0, k] = once_ref[k]
        once_out_ref[1, k] = once_ref[inner + k]
    for k in range(2):
        for out_ref, ref in ((twice_out_ref, twice_ref), (ridge_out_ref, ridge_ref)):
            out_ref[0, k] = ref[k]
            out_ref[1, k] = ref[inner + k]
        slope_out_ref[0, k] = slope_ref[k]
        slope_out_ref[1, k] = slope_ref[inner + k]


def parts_of(image_ref, kept_ref, sent_ref, mine):
    many, share = kept_ref.shape[0], kept_ref.shape[3]
    for r in range(many):
        for out_ref, bit in ((kept_ref, mine), (sent_ref, 1 - mine)):
            start = pl.multiple_of((2 * r + bit) * share, share)
            out_ref[r] = image_ref[:, :, pl.ds(start, share), :]


def march_ends(stencil, steps, first, weights, fields, middle, rays, image_ref):
    cx_ref, tx_ref = middle
    cy_ref, ty_ref = rays
    layers = stencil.layers
    many_y = image_ref.shape[1]
    ratio = steps[0] / steps[1]
    planes = [(0, 1), (0, 2), (0, 3), (1, 1), (1, 2), (1, 3)]
    tiles = [
        stencil.features(*[ref.at[side] for ref in fields], k, first + j)
        for j in range(many_y)
        for side, k in planes
    ]
    emission, clear = network(tiles, *weights, steps[1])
    images = [[], []]
    for g in range(LANES // SUB):
        at = pl.ds(g * SUB, SUB)
        rays_y = [(cy_ref[i, at], ty_ref[i, at]) for i in range(len(planes))]
        for j in range(many_y):
            ray_x = jnp.zeros((SUB, LANES), F32), jnp.ones((SUB, LANES), F32)
            for i in range(len(planes)):
                if i == REACH:
                    colour, light = ray_x
                    colour = colour + light * cx_ref[first + j, at]
                    ray_x = colour, light * tx_ref[first + j, at]
                start = (j * len(planes) + i) * LANES + g * SUB
                e, q = emission[start : start + SUB], clear[start : start + SUB]
                rays_y[i] = step_ray(rays_y[i], q, e)
                ray_x = step_ray(ray_x, clear_of_x(q, ratio), e)
            images[0].append(ray_x[0])
            images[1].append(ray_x[1])
        for i in range(len(planes)):
            cy_ref[i, at], ty_ref[i, at] = rays_y[i]
    for d in range(layers // SUB):
        for j in range(many_y):
            near, far = d * many_y + j, (d + layers // SUB) * many_y + j
            q = images[1][near]
            at = pl.ds(d * SUB, SUB)
            image_ref[0, j, at] = images[0][near] + q * images[0][far]
            image_ref[1, j, at] = q * images[1][far]


def ends_first_kernel(
    counts,
    steps,
    wide_ref,
    before_ref,
    after_ref,
    win_ref,
    wout_ref,
    once_in_ref,
    twice_in_ref,
    ridge_in_ref,
    slope_in_ref,
    cx_ref,
    tx_ref,
    twice_ref,
    ridge_ref,
    slope_ref,
    cy_ref,
    ty_ref,
    kept_ref,
    sent_ref,
    image_ref,
    raw_ref,
    once_ref,
):
    half, rows, _ = wide_ref.shape
    run = cx_ref.shape[0]
    layers = LANES // 2
    stencil = Stencil(run, counts)
    part = rows // 2
    front = iota((part, LANES), 1) < layers
    at_x = lax.axis_index("bx")
    for j in range(REACH):
        before, after = inside_grid("bx", counts[0], before_ref[j], after_ref[j])
        halo, own = before, wide_ref[half - REACH + j]
        raw_ref[0, j, :part] = jnp.where(front, halo, roll(own[:part], layers))
        raw_ref[0, j, part:] = jnp.where(front, roll(halo, layers), roll(own[part:], layers))
        halo, own = after, wide_ref[j]
        raw_ref[1, 2 + j, :part] = jnp.where(front, roll(own[:part], layers), roll(halo, layers))
        raw_ref[1, 2 + j, part:] = jnp.where(front, roll(own[part:], layers), halo)
    for j in range(2):
        raw_ref[0, REACH + j] = wide_ref[j]
        raw_ref[1, j] = wide_ref[half - 2 + j]
    for k in range(4):
        once_ref[0, 3 + k] = once_in_ref[0, k]
        once_ref[1, k] = once_in_ref[1, k]
    for k in range(2):
        twice_ref[0, 3 + k] = twice_in_ref[0, k]
        twice_ref[1, k] = twice_in_ref[1, k]
        ridge_ref[0, 3 + k] = ridge_in_ref[0, k]
        ridge_ref[1, k] = ridge_in_ref[1, k]
        slope_ref[0, 3 + k] = slope_in_ref[0, k]
        slope_ref[1, k] = slope_in_ref[1, k]
    for side, edge in enumerate((stencil.x_low, stencil.x_high)):
        outside = (0, 1) if side == 0 else (1, 2)
        for k in range(3):
            kept = edge if k in outside else None
            stencil.once(raw_ref.at[side], k + 1, once_ref.at[side], k + 4 * side, kept)
    for side, edge in enumerate((stencil.x_low, stencil.x_high)):
        for k in range(3):
            kept = edge if k == 2 * side else None
            at = k + 2 * side
            outs = [ref.at[side] for ref in (twice_ref, ridge_ref, slope_ref)]
            stencil.twice(once_ref.at[side], at + 1, *outs, at, kept)
    for k in range(2 * REACH):
        ty_ref[k] = jnp.ones((LANES, LANES), F32)
        cy_ref[k] = jnp.zeros((LANES, LANES), F32)
    march_ends(
        stencil,
        steps,
        0,
        (win_ref, wout_ref),
        (twice_ref, ridge_ref, slope_ref),
        (cx_ref, tx_ref),
        (cy_ref, ty_ref),
        image_ref,
    )
    parts_of(image_ref, kept_ref, sent_ref, at_x & 1)


def ends_last_kernel(
    counts,
    steps,
    win_ref,
    wout_ref,
    twice_ref,
    ridge_ref,
    slope_ref,
    cx_ref,
    tx_ref,
    cy_in_ref,
    ty_in_ref,
    cy_middle_ref,
    ty_middle_ref,
    kept_ref,
    sent_ref,
    kept_y_ref,
    sent_y_ref,
    image_ref,
    cy_ref,
    ty_ref,
    rows_ref,
    columns_ref,
):
    run = cx_ref.shape[0]
    stencil = Stencil(run, counts)
    layers = stencil.layers
    cy_ref[...] = cy_in_ref[...]
    ty_ref[...] = ty_in_ref[...]
    march_ends(
        stencil,
        steps,
        run - image_ref.shape[1],
        (win_ref, wout_ref),
        (twice_ref, ridge_ref, slope_ref),
        (cx_ref, tx_ref),
        (cy_ref, ty_ref),
        image_ref,
    )
    parts_of(image_ref, kept_ref, sent_ref, lax.axis_index("bx") & 1)
    inner = cy_middle_ref.shape[0]
    half = inner + 2 * REACH
    for k in range(half):
        if REACH <= k < REACH + inner:
            image = column_image(cy_middle_ref[k - REACH], ty_middle_ref[k - REACH])
        else:
            i = k if k < REACH else k - inner
            image = column_image(cy_ref[i], ty_ref[i])
        for kind in range(2):
            rows_ref[kind, k * SUB : (k + 1) * SUB] = image[kind]
    for kind in range(2):
        turned = rows_ref[kind].T
        for part in range(2):
            columns_ref[kind, part] = turned[part * layers : (part + 1) * layers]
    parts_of(columns_ref, kept_y_ref, sent_y_ref, lax.axis_index("by") & 1)


def column_image(colours, clears):
    colours, clears = colours.T, clears.T
    colour, clear = colours[:SUB], clears[:SUB]
    for c in range(1, CHUNKS):
        at = slice(c * SUB, (c + 1) * SUB)
        colour = colour + clear * colours[at]
        clear = clear * clears[at]
    return colour, clear


def merge_kernel(level, kept_ref, received_ref, *refs):
    me = lax.axis_index("by") >> (level - 1)
    later = (me & 1) == 1
    kept, received = kept_ref[...], received_ref[...]
    front = jnp.where(later, received, kept)
    back = jnp.where(later, kept, received)
    many = kept.shape[0]
    colour = front[:, 0] + front[:, 1] * back[:, 0]
    clear = front[:, 1] * back[:, 1]
    if many == 1:
        refs[0][0] = colour[0]
        refs[0][1] = clear[0]
        return
    out_kept_ref, out_sent_ref = refs
    bit = ((me >> 1) & 1) == 1
    for r in range(many // 2):
        for kind, value in enumerate((colour, clear)):
            even, odd = value[2 * r], value[2 * r + 1]
            out_kept_ref[r, kind] = jnp.where(bit, odd, even)
            out_sent_ref[r, kind] = jnp.where(bit, even, odd)


def merge_x_kernel(*refs):
    many, _, some, _, _ = refs[0].shape
    ins, outs = refs[:4], refs[-many:]
    at = lax.axis_index("bx")
    later = (at & 1) == 1
    for i in range(2):
        kept_ref, received_ref = ins[2 * i], ins[2 * i + 1]
        for t in range(many):
            r = lax.rem((at >> 1) + t, many)
            kept, received = kept_ref[r], received_ref[r]
            front = jnp.where(later, received, kept)
            back = jnp.where(later, kept, received)
            outs[t][0, i * some : (i + 1) * some] = front[0] + front[1] * back[0]
            outs[t][1, i * some : (i + 1) * some] = front[1] * back[1]


def fold_x_kernel(*refs):
    pieces, out_ref = refs[:-1], refs[-1]
    _, run, share, _ = pieces[0].shape
    lane = iota((share, LANES), 1)
    me = lax.axis_index("bx") >> 1
    kinds = [[], []]
    for y in range(run):
        behind = colour, clear = jnp.zeros((share, LANES), F32), jnp.ones((share, LANES), F32)
        for s in reversed(range(len(pieces))):
            start = me == s
            behind = jnp.where(start, colour, behind[0]), jnp.where(start, clear, behind[1])
            colour, clear = jnp.where(start, 0.0, colour), jnp.where(start, 1.0, clear)
            colour = colour + clear * pieces[s][0, y]
            clear = clear * pieces[s][1, y]
        kinds[0].append(colour + clear * behind[0])
        kinds[1].append(clear * behind[1])
    for kind, values in enumerate(kinds):
        for s in (1, 2, 4):
            for i in range(run):
                if not i & s:
                    a, b = values[i], values[i | s]
                    odd = (lane & s) != 0
                    values[i] = jnp.where(odd, pltpu.roll(b, s, axis=1), a)
                    values[i | s] = jnp.where(odd, b, pltpu.roll(a, LANES - s, axis=1))
        for band, value in enumerate(values):
            out_ref[kind, band] = value


def exchange(last, first, axis):
    peers = lax.axis_size(axis)
    up = [(i, (i + 1) % peers) for i in range(peers)]
    down = [(j, i) for i, j in up]
    return lax.ppermute(last, axis, up), lax.ppermute(first, axis, down)


def swap(value, axis, bit):
    return lax.ppermute(value, axis, [(i, i ^ bit) for i in range(lax.axis_size(axis))])


def body(scalar_field, transfer_in, transfer_out):
    layers, local_x, local_y = scalar_field.shape
    units, feats = transfer_in.shape
    channels = transfer_out.shape[0]
    bands = channels // 2
    count_x, count_y = lax.axis_size("bx"), lax.axis_size("by")
    steps = (2.0 / (local_x * count_x), 2.0 / (local_y * count_y))
    half, run, rows = local_x // 2, local_y // CHUNKS, rows_of(local_y)
    sds = lambda *shape: jax.ShapeDtypeStruct(shape, F32)
    weights = [
        jax.ShapeDtypeStruct((feats * CHUNKS, units * CHUNKS), BF16),
        jax.ShapeDtypeStruct((units * CHUNKS, channels * CHUNKS), BF16),
    ]

    edge = sds(REACH, half, LANES)
    turned, first, last = call(turn_kernel, "turn", [sds(half, rows, LANES), edge, edge], 1)(
        scalar_field
    )
    before, after = exchange(last, first, "by")
    edge = sds(REACH, rows // 2, LANES)
    wide, first, last = call(
        functools.partial(sides_kernel, local_y, count_y), "sides", [sds(half, rows, LANES), edge, edge], 3
    )(turned, before, after)
    before, after = exchange(last, first, "bx")
    inner = half - 2 * REACH
    counts = (count_x, count_y)
    plane = lambda *lead: sds(*lead, CHUNKS, LANES)
    many_x, many_y = inner, 2
    win, wout, once, twice, ridge, slope, colour_x, clear_x, colour_y, clear_y = call(
        functools.partial(middle_kernel, (many_x, many_y), counts, steps),
        "middle",
        weights + [plane(2, 4, run + 4)] + [plane(2, 2, run + 2)] * 3
        + [sds(run, LANES, LANES)] * 2
        + [sds(inner, LANES, LANES)] * 2,
        3,
        [
            pltpu.VMEM((inner + 4, run + 4, CHUNKS, LANES), F32),
            pltpu.VMEM((inner + 2, run + 2, CHUNKS, LANES), F32),
            pltpu.VMEM((inner + 2, run + 2, CHUNKS, LANES), F32),
            pltpu.VMEM((inner + 2, run + 2, CHUNKS, LANES), F32),
        ],
    )(wide, transfer_in, transfer_out)
    share = layers // count_x
    share_y = layers // count_y
    parts = sds(count_x // 2, 2, run // 2, share, LANES)
    parts_y = sds(count_y // 2, 2, 2, share_y, LANES)
    image = pltpu.VMEM((2, run // 2, layers, LANES), F32)
    ray = pltpu.VMEM((2 * REACH, LANES, LANES), F32)
    field = plane(2, 5, run + 2)
    twice, ridge, slope, colour_ends, clear_ends, kept, sent = call(
        functools.partial(ends_first_kernel, counts, steps),
        "ends_first",
        [field] * 3 + [sds(2 * REACH, LANES, LANES)] * 2 + [parts] * 2,
        11,
        [
            image,
            pltpu.VMEM((2, 5, rows, LANES), F32),
            pltpu.VMEM((2, 7, run + 4, CHUNKS, LANES), F32),
        ],
    )(wide, before, after, win, wout, once, twice, ridge, slope, colour_x, clear_x)
    halves = [(kept, swap(sent, "bx", 1))]
    kept, sent, kept_y, sent_y = call(
        functools.partial(ends_last_kernel, counts, steps),
        "ends_last",
        [parts] * 2 + [parts_y] * 2,
        11,
        [
            image,
            ray,
            ray,
            pltpu.VMEM((2, LANES, LANES), F32),
            pltpu.VMEM((2, 2, layers, LANES), F32),
        ],
    )(
        win, wout, twice, ridge, slope, colour_x, clear_x, colour_ends, clear_ends, colour_y, clear_y
    )
    halves += [(kept, swap(sent, "bx", 1))]

    level, many = 1, count_y // 2
    while many:
        received = swap(sent_y, "by", level)
        merge = functools.partial(merge_kernel, level.bit_length())
        if many > 1:
            half_parts = sds(many // 2, 2, 2, share_y, LANES)
            kept_y, sent_y = call(merge, "merge", [half_parts] * 2, 2)(kept_y, received)
        else:
            view_y = call(merge, "merge", sds(2, 2, share_y, LANES), 2)(kept_y, received)
        level, many = 2 * level, many // 2
    many = count_x // 2
    piece = sds(2, run, share, LANES)
    operands = [*halves[0], *halves[1], sent_y]
    pieces = list(call(merge_x_kernel, "merge_x", [piece] * many, len(operands))(*operands))
    for t in range(1, many):
        pairs = [(i, (i + 2 * t) % count_x) for i in range(count_x)]
        pieces[t] = lax.ppermute(pieces[t], "bx", pairs)
    view_x = call(fold_x_kernel, "fold_x", sds(2, bands, share, local_y), many)(*pieces)
    view_y = view_y.reshape(2, 2, share_y, half, bands)
    view_y = jnp.transpose(view_y, (0, 4, 2, 1, 3)).reshape(2, bands, share_y, local_x)
    return (view_x, view_y)


def solution(mesh):
    return jax.shard_map(
        body,
        mesh=mesh,
        in_specs=(P(None, "bx", "by"), P(), P()),
        out_specs=(P(None, None, "bx", "by"), P(None, None, "by", "bx")),
        check_vma=False,
    )
```

```python
import functools

import jax
import jax.numpy as jnp
from jax import lax
from jax.experimental import pallas as pl
from jax.experimental.pallas import tpu as pltpu
from jax.sharding import PartitionSpec as P

F32 = jnp.float32
BF16 = jnp.bfloat16
LOG2E = 1.4426950408889634
SUB = 8
LANES = 128
CHUNKS = 16
REACH = 3
AHEAD = 2
VMEM = pl.BlockSpec(memory_space=pltpu.VMEM)
PARAMS = pltpu.CompilerParams(vmem_limit_bytes=36 * 1024 * 1024)


def call(kernel, name, outs, count, scratch=()):
    return pl.pallas_call(
        kernel,
        out_shape=outs,
        in_specs=[VMEM] * count,
        out_specs=jax.tree.map(lambda _: VMEM, outs),
        scratch_shapes=scratch,
        compiler_params=PARAMS,
        name=name,
    )


def rows_of(width):
    return -(-(width + 2 * REACH) // 16) * 16


def iota(shape, dim):
    return lax.broadcasted_iota(jnp.int32, shape, dim)


def one_hot(mask):
    return jnp.where(mask, 1.0, 0.0).astype(BF16)


def spread(weights, left, right, mask):
    inner = lax.dot_general(
        left, weights, (((1,), (1,)), ((), ())), preferred_element_type=F32
    ).astype(BF16)
    return jnp.where(mask, jnp.dot(inner, right, preferred_element_type=F32), 0.0)


def inside_grid(axis, peers, before, after):
    at = lax.axis_index(axis)
    return jnp.where(at == 0, 0.0, before), jnp.where(at == peers - 1, 0.0, after)


def turn_kernel(field_ref, turned_ref, first_ref, last_ref):
    layers, length, width = field_ref.shape
    half = length // 2
    for k in range(half):
        turned = jnp.concatenate([field_ref[:, k, :], field_ref[:, k + half, :]], axis=0).T
        turned_ref[k, REACH : REACH + width] = turned
        for j in range(REACH):
            first_ref[j, k : k + 1] = turned[j : j + 1]
            last_ref[j, k : k + 1] = turned[width - REACH + j : width - REACH + j + 1]


def spread_weights(in_ref, out_ref, win_ref, wout_ref):
    units, feats = in_ref.shape
    channels = out_ref.shape[0]
    bands = channels // 2
    rows, cols = feats * CHUNKS, units * CHUNKS
    left = one_hot(iota((rows, feats), 0) // CHUNKS == iota((rows, feats), 1))
    right = one_hot(iota((units, cols), 1) // CHUNKS == iota((units, cols), 0))
    mask = iota((rows, cols), 0) % CHUNKS == iota((rows, cols), 1) % CHUNKS
    win_ref[...] = (0.5 * spread(in_ref[...], left, right, mask)).astype(BF16)
    rows, cols = cols, channels * CHUNKS
    left = one_hot(iota((rows, units), 0) // CHUNKS == iota((rows, units), 1))
    at = iota((channels, cols), 1)
    right = one_hot((at // LANES) * bands + at % bands == iota((channels, cols), 0))
    mask = iota((rows, cols), 0) % CHUNKS == (iota((rows, cols), 1) % LANES) // bands
    wout_ref[...] = spread(out_ref[...], left, right, mask).astype(BF16)


def sides_kernel(
    width, count_y, turned_ref, before_ref, after_ref, wide_ref, first_ref, last_ref
):
    half, rows, _ = turned_ref.shape
    layers = LANES // 2
    part = rows // 2
    front = iota((part, LANES), 1) < layers
    befores, afters = inside_grid("by", count_y, before_ref[...], after_ref[...])
    for k in range(half):
        wide_ref[k, REACH : REACH + width] = turned_ref[k, REACH : REACH + width]
        for j in range(REACH):
            at = REACH + width + j
            wide_ref[k, j : j + 1] = befores[j, k : k + 1]
            wide_ref[k, at : at + 1] = afters[j, k : k + 1]
        wide_ref[k, 2 * REACH + width :] = jnp.zeros((rows - 2 * REACH - width, LANES), F32)
    for j in range(REACH):
        top, low = wide_ref[j, :part], wide_ref[j, part:]
        first_ref[j] = jnp.where(front, top, pltpu.roll(low, layers, axis=1))
        k = half - REACH + j
        top, low = wide_ref[k, :part], wide_ref[k, part:]
        last_ref[j] = jnp.where(front, pltpu.roll(top, layers, axis=1), low)


class Stencil:
    def __init__(self, run, counts):
        self.run = run
        self.layers = layers = LANES // 2
        self.shape = (CHUNKS, LANES)
        lane, chunk = iota(self.shape, 1), iota(self.shape, 0)
        z = lane % layers
        self.near = (z > 0).astype(F32)
        self.far = (z < layers - 1).astype(F32)
        at_x, at_y = lax.axis_index("bx"), lax.axis_index("by")
        count_x, count_y = counts
        self.x_low = jnp.where((lane < layers) & (at_x == 0), 0.0, 1.0)
        self.x_high = jnp.where((lane >= layers) & (at_x == count_x - 1), 0.0, 1.0)
        self.y_low = jnp.where((chunk == 0) & (at_y == 0), 0.0, 1.0)
        self.y_high = jnp.where((chunk == CHUNKS - 1) & (at_y == count_y - 1), 0.0, 1.0)

    def z_sum(self, value):
        return roll(value, 1) * self.near + roll(value, -1) * self.far

    def inside(self, value, y, edge):
        if edge is not None:
            value = value * edge
        if y < 0:
            value = value * self.y_low
        if y >= self.run:
            value = value * self.y_high
        return value

    def smooth(self, centre, others):
        total = self.z_sum(centre)
        for other in others:
            total = total + other
        return 0.4 * centre + 0.1 * total

    def raw(self, ref, k, y):
        return ref[k, pl.ds(y + REACH, CHUNKS, stride=self.run), :]

    def once(self, raw, k, out, at, edge=None):
        column = [self.raw(raw, k, y) for y in range(-3, self.run + 3)]
        for i in range(1, len(column) - 1):
            y = i - 3
            sides = [self.raw(raw, k - 1, y), self.raw(raw, k + 1, y)]
            value = self.smooth(column[i], [column[i - 1], column[i + 1]] + sides)
            out[at, i - 1] = self.inside(value, y, edge)

    def twice(self, once, k, out, ridge, slope, at, edge=None):
        column = [once[k, i] for i in range(self.run + 4)]
        for i in range(1, len(column) - 1):
            sides = [once[k - 1, i], once[k + 1, i]]
            value = self.smooth(column[i], [column[i - 1], column[i + 1]] + sides)
            value = self.inside(value, i - 2, edge)
            out[at, i - 1] = value
            below, above = roll(value, 1) * self.near, roll(value, -1) * self.far
            ridge[at, i - 1] = 2.0 * value + (below + above)
            slope[at, i - 1] = above - below

    def features(self, twice, ridge, slope, k, y):
        p = lambda a, b: twice[k + a, y + 1 + b]
        r = lambda a, b: ridge[k + a, y + 1 + b]
        centre = p(0, 0)
        main, cross = p(1, 1) - p(-1, -1), p(1, -1) - p(-1, 1)
        third = 1.0 / 3.0
        gx = (main + cross + (r(1, 0) - r(-1, 0))) * third
        gy = (main - cross + (r(0, 1) - r(0, -1))) * third
        d = lambda a, b: slope[k + a, y + 1 + b]
        gz = (2.0 * d(0, 0) + ((d(1, 0) + d(-1, 0)) + (d(0, 1) + d(0, -1)))) * third
        square = 1.0 + gx * gx + gy * gy + gz * gz
        m = square * lax.rsqrt(square)
        parts = [centre, gx, gy, gz, m, centre * m, centre * centre]
        packed = [part.astype(BF16) for part in parts] + [jnp.ones(self.shape, BF16)]
        return jnp.concatenate(packed, axis=0).T


def roll(value, shift):
    return pltpu.roll(value, shift % LANES, axis=1)


def network(tiles, win_ref, wout_ref, step):
    cells = jnp.concatenate(tiles, axis=0)
    half_v = jnp.dot(cells, win_ref[...], preferred_element_type=F32)
    hidden = (half_v + half_v * jnp.tanh(half_v)).astype(BF16)
    v = jnp.dot(hidden, wout_ref[...], preferred_element_type=F32)
    soft = jnp.maximum(v, jnp.log(1.0 + jnp.exp2(jnp.minimum(v * LOG2E, 126.0))))
    return soft[:, :LANES], jnp.exp2(soft[:, LANES:] * (-LOG2E * step))


def clear_of_x(q, ratio):
    if ratio == 1.0:
        return q
    if ratio == 2.0:
        return q * q
    return jnp.exp2(jnp.log(q) * (LOG2E * ratio))


def step_ray(ray, clear, emission):
    colour, light = ray
    later = light * clear
    return colour + (light - later) * emission, later


def middle_kernel(
    spans,
    counts,
    steps,
    wide_ref,
    in_ref,
    out_ref,
    win_ref,
    wout_ref,
    once_out_ref,
    twice_out_ref,
    ridge_out_ref,
    slope_out_ref,
    cx_ref,
    tx_ref,
    cy_ref,
    ty_ref,
    once_ref,
    twice_ref,
    ridge_ref,
    slope_ref,
):
    half = wide_ref.shape[0]
    run = cx_ref.shape[0]
    stencil = Stencil(run, counts)
    inner = half - 2 * REACH
    spread_weights(in_ref, out_ref, win_ref, wout_ref)
    for k in range(run):
        tx_ref[k] = jnp.ones((LANES, LANES), F32)
        cx_ref[k] = jnp.zeros((LANES, LANES), F32)
    for k in range(inner):
        ty_ref[k] = jnp.ones((LANES, LANES), F32)
        cy_ref[k] = jnp.zeros((LANES, LANES), F32)
    ratio = steps[0] / steps[1]

    def prepare(first, last):
        start = 0 if first == 0 else first + 2
        for k in range(start, last + 2):
            stencil.once(wide_ref, k + 1, once_ref, k)
        for k in range(first, last):
            stencil.twice(once_ref, k + 1, twice_ref, ridge_ref, slope_ref, k)

    def block(x0, y0, many_x, many_y):
        tiles = [
            stencil.features(twice_ref, ridge_ref, slope_ref, x0 + i + 1, y0 + j)
            for j in range(many_y)
            for i in range(many_x)
        ]
        emission, clear = network(tiles, win_ref, wout_ref, steps[1])
        for g in range(LANES // SUB):
            at = pl.ds(g * SUB, SUB)
            rays_y = [(cy_ref[x0 + i, at], ty_ref[x0 + i, at]) for i in range(many_x)]
            for j in range(many_y):
                ray_x = cx_ref[y0 + j, at], tx_ref[y0 + j, at]
                for i in range(many_x):
                    start = (j * many_x + i) * LANES + g * SUB
                    e, q = emission[start : start + SUB], clear[start : start + SUB]
                    rays_y[i] = step_ray(rays_y[i], q, e)
                    ray_x = step_ray(ray_x, clear_of_x(q, ratio), e)
                cx_ref[y0 + j, at], tx_ref[y0 + j, at] = ray_x
            for i in range(many_x):
                cy_ref[x0 + i, at], ty_ref[x0 + i, at] = rays_y[i]

    many_x, many_y = spans
    ready = 0
    for x0 in range(0, inner, many_x):
        ahead = min(inner + 2, x0 + many_x + 2 + AHEAD)
        prepare(ready, ahead)
        ready = ahead
        for y0 in range(0, run, many_y):
            block(x0, y0, many_x, many_y)
    for k in range(4):
        once_out_ref[0, k] = once_ref[k]
        once_out_ref[1, k] = once_ref[inner + k]
    for k in range(2):
        for out_ref, ref in ((twice_out_ref, twice_ref), (ridge_out_ref, ridge_ref)):
            out_ref[0, k] = ref[k]
            out_ref[1, k] = ref[inner + k]
        slope_out_ref[0, k] = slope_ref[k]
        slope_out_ref[1, k] = slope_ref[inner + k]


def parts_of(image_ref, kept_ref, sent_ref, mine):
    many, share = kept_ref.shape[0], kept_ref.shape[3]
    for r in range(many):
        for out_ref, bit in ((kept_ref, mine), (sent_ref, 1 - mine)):
            start = pl.multiple_of((2 * r + bit) * share, share)
            out_ref[r] = image_ref[:, :, pl.ds(start, share), :]


def march_ends(stencil, steps, first, weights, fields, middle, rays, image_ref):
    cx_ref, tx_ref = middle
    cy_ref, ty_ref = rays
    layers = stencil.layers
    many_y = image_ref.shape[1]
    ratio = steps[0] / steps[1]
    planes = [(0, 1), (0, 2), (0, 3), (1, 1), (1, 2), (1, 3)]
    tiles = [
        stencil.features(*[ref.at[side] for ref in fields], k, first + j)
        for j in range(many_y)
        for side, k in planes
    ]
    emission, clear = network(tiles, *weights, steps[1])
    images = [[], []]
    for g in range(LANES // SUB):
        at = pl.ds(g * SUB, SUB)
        rays_y = [(cy_ref[i, at], ty_ref[i, at]) for i in range(len(planes))]
        for j in range(many_y):
            ray_x = jnp.zeros((SUB, LANES), F32), jnp.ones((SUB, LANES), F32)
            for i in range(len(planes)):
                if i == REACH:
                    colour, light = ray_x
                    colour = colour + light * cx_ref[first + j, at]
                    ray_x = colour, light * tx_ref[first + j, at]
                start = (j * len(planes) + i) * LANES + g * SUB
                e, q = emission[start : start + SUB], clear[start : start + SUB]
                rays_y[i] = step_ray(rays_y[i], q, e)
                ray_x = step_ray(ray_x, clear_of_x(q, ratio), e)
            images[0].append(ray_x[0])
            images[1].append(ray_x[1])
        for i in range(len(planes)):
            cy_ref[i, at], ty_ref[i, at] = rays_y[i]
    for d in range(layers // SUB):
        for j in range(many_y):
            near, far = d * many_y + j, (d + layers // SUB) * many_y + j
            q = images[1][near]
            at = pl.ds(d * SUB, SUB)
            image_ref[0, j, at] = images[0][near] + q * images[0][far]
            image_ref[1, j, at] = q * images[1][far]


def ends_first_kernel(
    counts,
    steps,
    wide_ref,
    before_ref,
    after_ref,
    win_ref,
    wout_ref,
    once_in_ref,
    twice_in_ref,
    ridge_in_ref,
    slope_in_ref,
    cx_ref,
    tx_ref,
    twice_ref,
    ridge_ref,
    slope_ref,
    cy_ref,
    ty_ref,
    kept_ref,
    sent_ref,
    image_ref,
    raw_ref,
    once_ref,
):
    half, rows, _ = wide_ref.shape
    run = cx_ref.shape[0]
    layers = LANES // 2
    stencil = Stencil(run, counts)
    part = rows // 2
    front = iota((part, LANES), 1) < layers
    at_x = lax.axis_index("bx")
    for j in range(REACH):
        before, after = inside_grid("bx", counts[0], before_ref[j], after_ref[j])
        halo, own = before, wide_ref[half - REACH + j]
        raw_ref[0, j, :part] = jnp.where(front, halo, roll(own[:part], layers))
        raw_ref[0, j, part:] = jnp.where(front, roll(halo, layers), roll(own[part:], layers))
        halo, own = after, wide_ref[j]
        raw_ref[1, 2 + j, :part] = jnp.where(front, roll(own[:part], layers), roll(halo, layers))
        raw_ref[1, 2 + j, part:] = jnp.where(front, roll(own[part:], layers), halo)
    for j in range(2):
        raw_ref[0, REACH + j] = wide_ref[j]
        raw_ref[1, j] = wide_ref[half - 2 + j]
    for k in range(4):
        once_ref[0, 3 + k] = once_in_ref[0, k]
        once_ref[1, k] = once_in_ref[1, k]
    for k in range(2):
        twice_ref[0, 3 + k] = twice_in_ref[0, k]
        twice_ref[1, k] = twice_in_ref[1, k]
        ridge_ref[0, 3 + k] = ridge_in_ref[0, k]
        ridge_ref[1, k] = ridge_in_ref[1, k]
        slope_ref[0, 3 + k] = slope_in_ref[0, k]
        slope_ref[1, k] = slope_in_ref[1, k]
    for side, edge in enumerate((stencil.x_low, stencil.x_high)):
        outside = (0, 1) if side == 0 else (1, 2)
        for k in range(3):
            kept = edge if k in outside else None
            stencil.once(raw_ref.at[side], k + 1, once_ref.at[side], k + 4 * side, kept)
    for side, edge in enumerate((stencil.x_low, stencil.x_high)):
        for k in range(3):
            kept = edge if k == 2 * side else None
            at = k + 2 * side
            outs = [ref.at[side] for ref in (twice_ref, ridge_ref, slope_ref)]
            stencil.twice(once_ref.at[side], at + 1, *outs, at, kept)
    for k in range(2 * REACH):
        ty_ref[k] = jnp.ones((LANES, LANES), F32)
        cy_ref[k] = jnp.zeros((LANES, LANES), F32)
    march_ends(
        stencil,
        steps,
        0,
        (win_ref, wout_ref),
        (twice_ref, ridge_ref, slope_ref),
        (cx_ref, tx_ref),
        (cy_ref, ty_ref),
        image_ref,
    )
    parts_of(image_ref, kept_ref, sent_ref, at_x & 1)


def ends_last_kernel(
    counts,
    steps,
    win_ref,
    wout_ref,
    twice_ref,
    ridge_ref,
    slope_ref,
    cx_ref,
    tx_ref,
    cy_in_ref,
    ty_in_ref,
    cy_middle_ref,
    ty_middle_ref,
    kept_ref,
    sent_ref,
    kept_y_ref,
    sent_y_ref,
    image_ref,
    cy_ref,
    ty_ref,
    rows_ref,
    columns_ref,
):
    run = cx_ref.shape[0]
    stencil = Stencil(run, counts)
    layers = stencil.layers
    cy_ref[...] = cy_in_ref[...]
    ty_ref[...] = ty_in_ref[...]
    march_ends(
        stencil,
        steps,
        run - image_ref.shape[1],
        (win_ref, wout_ref),
        (twice_ref, ridge_ref, slope_ref),
        (cx_ref, tx_ref),
        (cy_ref, ty_ref),
        image_ref,
    )
    parts_of(image_ref, kept_ref, sent_ref, lax.axis_index("bx") & 1)
    inner = cy_middle_ref.shape[0]
    half = inner + 2 * REACH
    for k in range(half):
        if REACH <= k < REACH + inner:
            image = column_image(cy_middle_ref[k - REACH], ty_middle_ref[k - REACH])
        else:
            i = k if k < REACH else k - inner
            image = column_image(cy_ref[i], ty_ref[i])
        for kind in range(2):
            rows_ref[kind, k * SUB : (k + 1) * SUB] = image[kind]
    for kind in range(2):
        turned = rows_ref[kind].T
        for part in range(2):
            columns_ref[kind, part] = turned[part * layers : (part + 1) * layers]
    parts_of(columns_ref, kept_y_ref, sent_y_ref, lax.axis_index("by") & 1)


def column_image(colours, clears):
    colours, clears = colours.T, clears.T
    colour, clear = colours[:SUB], clears[:SUB]
    for c in range(1, CHUNKS):
        at = slice(c * SUB, (c + 1) * SUB)
        colour = colour + clear * colours[at]
        clear = clear * clears[at]
    return colour, clear


def merge_kernel(level, kept_ref, received_ref, *refs):
    me = lax.axis_index("by") >> (level - 1)
    later = (me & 1) == 1
    kept, received = kept_ref[...], received_ref[...]
    front = jnp.where(later, received, kept)
    back = jnp.where(later, kept, received)
    many = kept.shape[0]
    colour = front[:, 0] + front[:, 1] * back[:, 0]
    clear = front[:, 1] * back[:, 1]
    if many == 1:
        refs[0][0] = colour[0]
        refs[0][1] = clear[0]
        return
    out_kept_ref, out_sent_ref = refs
    bit = ((me >> 1) & 1) == 1
    for r in range(many // 2):
        for kind, value in enumerate((colour, clear)):
            even, odd = value[2 * r], value[2 * r + 1]
            out_kept_ref[r, kind] = jnp.where(bit, odd, even)
            out_sent_ref[r, kind] = jnp.where(bit, even, odd)


def merge_x_kernel(*refs):
    many = refs[0].shape[0]
    ins, outs = refs[:4], refs[-many:]
    at = lax.axis_index("bx")
    later = (at & 1) == 1
    first = 0
    for kept_ref, received_ref in (ins[:2], ins[2:]):
        last = first + kept_ref.shape[2]
        for t in range(many):
            r = lax.rem((at >> 1) + t, many)
            kept, received = kept_ref[r], received_ref[r]
            front = jnp.where(later, received, kept)
            back = jnp.where(later, kept, received)
            outs[t][0, first:last] = front[0] + front[1] * back[0]
            outs[t][1, first:last] = front[1] * back[1]
        first = last


def fold_x_kernel(*refs):
    pieces, out_ref = refs[:-1], refs[-1]
    _, run, share, _ = pieces[0].shape
    lane = iota((share, LANES), 1)
    me = lax.axis_index("bx") >> 1
    kinds = [[], []]
    for y in range(run):
        behind = colour, clear = jnp.zeros((share, LANES), F32), jnp.ones((share, LANES), F32)
        for s in reversed(range(len(pieces))):
            start = me == s
            behind = jnp.where(start, colour, behind[0]), jnp.where(start, clear, behind[1])
            colour, clear = jnp.where(start, 0.0, colour), jnp.where(start, 1.0, clear)
            colour = colour + clear * pieces[s][0, y]
            clear = clear * pieces[s][1, y]
        kinds[0].append(colour + clear * behind[0])
        kinds[1].append(clear * behind[1])
    for kind, values in enumerate(kinds):
        for s in (1, 2, 4):
            for i in range(run):
                if not i & s:
                    a, b = values[i], values[i | s]
                    odd = (lane & s) != 0
                    values[i] = jnp.where(odd, pltpu.roll(b, s, axis=1), a)
                    values[i | s] = jnp.where(odd, b, pltpu.roll(a, LANES - s, axis=1))
        for band, value in enumerate(values):
            out_ref[kind, band] = value


def exchange(last, first, axis):
    peers = lax.axis_size(axis)
    up = [(i, (i + 1) % peers) for i in range(peers)]
    down = [(j, i) for i, j in up]
    return lax.ppermute(last, axis, up), lax.ppermute(first, axis, down)


def swap(value, axis, bit):
    return lax.ppermute(value, axis, [(i, i ^ bit) for i in range(lax.axis_size(axis))])


def body(scalar_field, transfer_in, transfer_out):
    layers, local_x, local_y = scalar_field.shape
    units, feats = transfer_in.shape
    channels = transfer_out.shape[0]
    bands = channels // 2
    count_x, count_y = lax.axis_size("bx"), lax.axis_size("by")
    steps = (2.0 / (local_x * count_x), 2.0 / (local_y * count_y))
    half, run, rows = local_x // 2, local_y // CHUNKS, rows_of(local_y)
    sds = lambda *shape: jax.ShapeDtypeStruct(shape, F32)
    weights = [
        jax.ShapeDtypeStruct((feats * CHUNKS, units * CHUNKS), BF16),
        jax.ShapeDtypeStruct((units * CHUNKS, channels * CHUNKS), BF16),
    ]

    edge = sds(REACH, half, LANES)
    turned, first, last = call(turn_kernel, "turn", [sds(half, rows, LANES), edge, edge], 1)(
        scalar_field
    )
    before, after = exchange(last, first, "by")
    edge = sds(REACH, rows // 2, LANES)
    wide, first, last = call(
        functools.partial(sides_kernel, local_y, count_y), "sides", [sds(half, rows, LANES), edge, edge], 3
    )(turned, before, after)
    before, after = exchange(last, first, "bx")
    inner = half - 2 * REACH
    counts = (count_x, count_y)
    plane = lambda *lead: sds(*lead, CHUNKS, LANES)
    many_x, many_y = inner, 2
    win, wout, once, twice, ridge, slope, colour_x, clear_x, colour_y, clear_y = call(
        functools.partial(middle_kernel, (many_x, many_y), counts, steps),
        "middle",
        weights + [plane(2, 4, run + 4)] + [plane(2, 2, run + 2)] * 3
        + [sds(run, LANES, LANES)] * 2
        + [sds(inner, LANES, LANES)] * 2,
        3,
        [
            pltpu.VMEM((inner + 4, run + 4, CHUNKS, LANES), F32),
            pltpu.VMEM((inner + 2, run + 2, CHUNKS, LANES), F32),
            pltpu.VMEM((inner + 2, run + 2, CHUNKS, LANES), F32),
            pltpu.VMEM((inner + 2, run + 2, CHUNKS, LANES), F32),
        ],
    )(wide, transfer_in, transfer_out)
    share = layers // count_x
    share_y = layers // count_y
    ahead = run - run // 4
    parts = lambda many: [sds(count_x // 2, 2, many, share, LANES)] * 2
    parts_y = sds(count_y // 2, 2, 2, share_y, LANES)
    image = lambda many: pltpu.VMEM((2, many, layers, LANES), F32)
    ray = pltpu.VMEM((2 * REACH, LANES, LANES), F32)
    field = plane(2, 5, run + 2)
    twice, ridge, slope, colour_ends, clear_ends, kept, sent = call(
        functools.partial(ends_first_kernel, counts, steps),
        "ends_first",
        [field] * 3 + [sds(2 * REACH, LANES, LANES)] * 2 + parts(ahead),
        11,
        [
            image(ahead),
            pltpu.VMEM((2, 5, rows, LANES), F32),
            pltpu.VMEM((2, 7, run + 4, CHUNKS, LANES), F32),
        ],
    )(wide, before, after, win, wout, once, twice, ridge, slope, colour_x, clear_x)
    halves = [(kept, swap(sent, "bx", 1))]
    kept, sent, kept_y, sent_y = call(
        functools.partial(ends_last_kernel, counts, steps),
        "ends_last",
        parts(run - ahead) + [parts_y] * 2,
        11,
        [
            image(run - ahead),
            ray,
            ray,
            pltpu.VMEM((2, LANES, LANES), F32),
            pltpu.VMEM((2, 2, layers, LANES), F32),
        ],
    )(
        win, wout, twice, ridge, slope, colour_x, clear_x, colour_ends, clear_ends, colour_y, clear_y
    )
    halves += [(kept, swap(sent, "bx", 1))]

    level, many = 1, count_y // 2
    while many:
        received = swap(sent_y, "by", level)
        merge = functools.partial(merge_kernel, level.bit_length())
        if many > 1:
            half_parts = sds(many // 2, 2, 2, share_y, LANES)
            kept_y, sent_y = call(merge, "merge", [half_parts] * 2, 2)(kept_y, received)
        else:
            view_y = call(merge, "merge", sds(2, 2, share_y, LANES), 2)(kept_y, received)
        level, many = 2 * level, many // 2
    many = count_x // 2
    piece = sds(2, run, share, LANES)
    operands = [*halves[0], *halves[1], received]
    pieces = list(call(merge_x_kernel, "merge_x", [piece] * many, len(operands))(*operands))
    for t in range(1, many):
        pairs = [(i, (i + 2 * t) % count_x) for i in range(count_x)]
        pieces[t] = lax.ppermute(pieces[t], "bx", pairs)
    view_x = call(fold_x_kernel, "fold_x", sds(2, bands, share, local_y), many)(*pieces)
    view_y = view_y.reshape(2, 2, share_y, half, bands)
    view_y = jnp.transpose(view_y, (0, 4, 2, 1, 3)).reshape(2, bands, share_y, local_x)
    return (view_x, view_y)


def solution(mesh):
    return jax.shard_map(
        body,
        mesh=mesh,
        in_specs=(P(None, "bx", "by"), P(), P()),
        out_specs=(P(None, None, "bx", "by"), P(None, None, "by", "bx")),
        check_vma=False,
    )
```

```python
import functools

import jax
import jax.numpy as jnp
from jax import lax
from jax.experimental import pallas as pl
from jax.experimental.pallas import tpu as pltpu
from jax.sharding import PartitionSpec as P

F32 = jnp.float32
BF16 = jnp.bfloat16
LOG2E = 1.4426950408889634
SUB = 8
LANES = 128
CHUNKS = 16
REACH = 3
VMEM = pl.BlockSpec(memory_space=pltpu.VMEM)
PARAMS = pltpu.CompilerParams(vmem_limit_bytes=36 * 1024 * 1024)


def call(kernel, name, outs, count, scratch=()):
    return pl.pallas_call(
        kernel,
        out_shape=outs,
        in_specs=[VMEM] * count,
        out_specs=jax.tree.map(lambda _: VMEM, outs),
        scratch_shapes=scratch,
        compiler_params=PARAMS,
        name=name,
    )


def rows_of(width):
    return -(-(width + 2 * REACH) // 16) * 16


def iota(shape, dim):
    return lax.broadcasted_iota(jnp.int32, shape, dim)


def one_hot(mask):
    return jnp.where(mask, 1.0, 0.0).astype(BF16)


def spread(weights, left, right, mask):
    inner = lax.dot_general(
        left, weights, (((1,), (1,)), ((), ())), preferred_element_type=F32
    ).astype(BF16)
    return jnp.where(mask, jnp.dot(inner, right, preferred_element_type=F32), 0.0)


def inside_grid(axis, peers, before, after):
    at = lax.axis_index(axis)
    return jnp.where(at == 0, 0.0, before), jnp.where(at == peers - 1, 0.0, after)


def turn_kernel(field_ref, turned_ref, first_ref, last_ref):
    layers, length, width = field_ref.shape
    half = length // 2
    for k in range(half):
        turned = jnp.concatenate([field_ref[:, k, :], field_ref[:, k + half, :]], axis=0).T
        turned_ref[k, REACH : REACH + width] = turned
        for j in range(REACH):
            first_ref[j, k : k + 1] = turned[j : j + 1]
            last_ref[j, k : k + 1] = turned[width - REACH + j : width - REACH + j + 1]


def spread_weights(in_ref, out_ref, win_ref, wout_ref):
    units, feats = in_ref.shape
    channels = out_ref.shape[0]
    bands = channels // 2
    rows, cols = feats * CHUNKS, units * CHUNKS
    left = one_hot(iota((rows, feats), 0) // CHUNKS == iota((rows, feats), 1))
    right = one_hot(iota((units, cols), 1) // CHUNKS == iota((units, cols), 0))
    mask = iota((rows, cols), 0) % CHUNKS == iota((rows, cols), 1) % CHUNKS
    win_ref[...] = (0.5 * spread(in_ref[...], left, right, mask)).astype(BF16)
    rows, cols = cols, channels * CHUNKS
    left = one_hot(iota((rows, units), 0) // CHUNKS == iota((rows, units), 1))
    at = iota((channels, cols), 1)
    right = one_hot((at // LANES) * bands + at % bands == iota((channels, cols), 0))
    mask = iota((rows, cols), 0) % CHUNKS == (iota((rows, cols), 1) % LANES) // bands
    wout_ref[...] = spread(out_ref[...], left, right, mask).astype(BF16)


def sides_kernel(
    width, count_y, turned_ref, before_ref, after_ref, wide_ref, first_ref, last_ref
):
    half, rows, _ = turned_ref.shape
    layers = LANES // 2
    part = rows // 2
    front = iota((part, LANES), 1) < layers
    befores, afters = inside_grid("by", count_y, before_ref[...], after_ref[...])
    for k in range(half):
        wide_ref[k, REACH : REACH + width] = turned_ref[k, REACH : REACH + width]
        for j in range(REACH):
            at = REACH + width + j
            wide_ref[k, j : j + 1] = befores[j, k : k + 1]
            wide_ref[k, at : at + 1] = afters[j, k : k + 1]
        wide_ref[k, 2 * REACH + width :] = jnp.zeros((rows - 2 * REACH - width, LANES), F32)
    for j in range(REACH):
        top, low = wide_ref[j, :part], wide_ref[j, part:]
        first_ref[j] = jnp.where(front, top, pltpu.roll(low, layers, axis=1))
        k = half - REACH + j
        top, low = wide_ref[k, :part], wide_ref[k, part:]
        last_ref[j] = jnp.where(front, pltpu.roll(top, layers, axis=1), low)


class Stencil:
    def __init__(self, run, counts):
        self.run = run
        self.layers = layers = LANES // 2
        self.shape = (CHUNKS, LANES)
        lane, chunk = iota(self.shape, 1), iota(self.shape, 0)
        z = lane % layers
        self.near = (z > 0).astype(F32)
        self.far = (z < layers - 1).astype(F32)
        at_x, at_y = lax.axis_index("bx"), lax.axis_index("by")
        count_x, count_y = counts
        self.x_low = jnp.where((lane < layers) & (at_x == 0), 0.0, 1.0)
        self.x_high = jnp.where((lane >= layers) & (at_x == count_x - 1), 0.0, 1.0)
        self.y_low = jnp.where((chunk == 0) & (at_y == 0), 0.0, 1.0)
        self.y_high = jnp.where((chunk == CHUNKS - 1) & (at_y == count_y - 1), 0.0, 1.0)

    def z_sum(self, value):
        return roll(value, 1) * self.near + roll(value, -1) * self.far

    def inside(self, value, y, edge):
        if edge is not None:
            value = value * edge
        if y < 0:
            value = value * self.y_low
        if y >= self.run:
            value = value * self.y_high
        return value

    def smooth(self, centre, others):
        total = self.z_sum(centre)
        for other in others:
            total = total + other
        return 0.4 * centre + 0.1 * total

    def raw(self, ref, k, y):
        return ref[k, pl.ds(y + REACH, CHUNKS, stride=self.run), :]

    def once(self, raw, k, out, at, edge=None):
        column = [self.raw(raw, k, y) for y in range(-3, self.run + 3)]
        for i in range(1, len(column) - 1):
            y = i - 3
            sides = [self.raw(raw, k - 1, y), self.raw(raw, k + 1, y)]
            value = self.smooth(column[i], [column[i - 1], column[i + 1]] + sides)
            out[at, i - 1] = self.inside(value, y, edge)

    def twice(self, once, k, out, ridge, slope, at, edge=None):
        column = [once[k, i] for i in range(self.run + 4)]
        for i in range(1, len(column) - 1):
            sides = [once[k - 1, i], once[k + 1, i]]
            value = self.smooth(column[i], [column[i - 1], column[i + 1]] + sides)
            value = self.inside(value, i - 2, edge)
            out[at, i - 1] = value
            below, above = roll(value, 1) * self.near, roll(value, -1) * self.far
            ridge[at, i - 1] = 2.0 * value + (below + above)
            slope[at, i - 1] = above - below

    def features(self, twice, ridge, slope, k, y):
        p = lambda a, b: twice[k + a, y + 1 + b]
        r = lambda a, b: ridge[k + a, y + 1 + b]
        centre = p(0, 0)
        main, cross = p(1, 1) - p(-1, -1), p(1, -1) - p(-1, 1)
        third = 1.0 / 3.0
        gx = (main + cross + (r(1, 0) - r(-1, 0))) * third
        gy = (main - cross + (r(0, 1) - r(0, -1))) * third
        d = lambda a, b: slope[k + a, y + 1 + b]
        gz = (2.0 * d(0, 0) + ((d(1, 0) + d(-1, 0)) + (d(0, 1) + d(0, -1)))) * third
        square = 1.0 + gx * gx + gy * gy + gz * gz
        m = square * lax.rsqrt(square)
        parts = [centre, gx, gy, gz, m, centre * m, centre * centre]
        packed = [part.astype(BF16) for part in parts] + [jnp.ones(self.shape, BF16)]
        return jnp.concatenate(packed, axis=0).T


def roll(value, shift):
    return pltpu.roll(value, shift % LANES, axis=1)


def network(tiles, win_ref, wout_ref, step):
    cells = jnp.concatenate(tiles, axis=0)
    half_v = jnp.dot(cells, win_ref[...], preferred_element_type=F32)
    hidden = (half_v + half_v * jnp.tanh(half_v)).astype(BF16)
    v = jnp.dot(hidden, wout_ref[...], preferred_element_type=F32)
    soft = jnp.maximum(v, jnp.log(1.0 + jnp.exp2(jnp.minimum(v * LOG2E, 126.0))))
    return soft[:, :LANES], jnp.exp2(soft[:, LANES:] * (-LOG2E * step))


def clear_of_x(q, ratio):
    if ratio == 1.0:
        return q
    if ratio == 2.0:
        return q * q
    return jnp.exp2(jnp.log(q) * (LOG2E * ratio))


def step_ray(ray, clear, emission):
    colour, light = ray
    later = light * clear
    return colour + (light - later) * emission, later


def middle_kernel(
    counts,
    steps,
    wide_ref,
    in_ref,
    out_ref,
    win_ref,
    wout_ref,
    once_out_ref,
    twice_out_ref,
    ridge_out_ref,
    slope_out_ref,
    cx_ref,
    tx_ref,
    cy_ref,
    ty_ref,
    *refs,
):
    later_refs, (once_ref, twice_ref, ridge_ref, slope_ref) = refs[:3], refs[3:]
    half = wide_ref.shape[0]
    run, ahead = once_ref.shape[1] - 4, cx_ref.shape[0]
    stencil = Stencil(run, counts)
    inner = half - 2 * REACH
    spread_weights(in_ref, out_ref, win_ref, wout_ref)
    for k in range(ahead):
        tx_ref[k] = jnp.ones((LANES, LANES), F32)
        cx_ref[k] = jnp.zeros((LANES, LANES), F32)
    for k in range(inner):
        ty_ref[k] = jnp.ones((LANES, LANES), F32)
        cy_ref[k] = jnp.zeros((LANES, LANES), F32)
    ratio = steps[0] / steps[1]

    def block(x0, y0, many_x, many_y):
        tiles = [
            stencil.features(twice_ref, ridge_ref, slope_ref, x0 + i + 1, y0 + j)
            for j in range(many_y)
            for i in range(many_x)
        ]
        emission, clear = network(tiles, win_ref, wout_ref, steps[1])
        for g in range(LANES // SUB):
            at = pl.ds(g * SUB, SUB)
            rays_y = [(cy_ref[x0 + i, at], ty_ref[x0 + i, at]) for i in range(many_x)]
            for j in range(many_y):
                ray_x = cx_ref[y0 + j, at], tx_ref[y0 + j, at]
                for i in range(many_x):
                    start = (j * many_x + i) * LANES + g * SUB
                    e, q = emission[start : start + SUB], clear[start : start + SUB]
                    rays_y[i] = step_ray(rays_y[i], q, e)
                    ray_x = step_ray(ray_x, clear_of_x(q, ratio), e)
                cx_ref[y0 + j, at], tx_ref[y0 + j, at] = ray_x
            for i in range(many_x):
                cy_ref[x0 + i, at], ty_ref[x0 + i, at] = rays_y[i]

    many_y = 2 if ahead % 2 == 0 else 1
    for k in range(inner + 4):
        stencil.once(wide_ref, k + 1, once_ref, k)
    for k in range(inner + 2):
        stencil.twice(once_ref, k + 1, twice_ref, ridge_ref, slope_ref, k)
    for y0 in range(0, ahead, many_y):
        block(0, y0, inner, many_y)
    for k in range(4):
        once_out_ref[0, k] = once_ref[k]
        once_out_ref[1, k] = once_ref[inner + k]
    fields = (twice_ref, ridge_ref, slope_ref)
    outs = (twice_out_ref, ridge_out_ref, slope_out_ref)
    for out_ref, later_ref, ref in zip(outs, later_refs, fields):
        for k in range(2):
            out_ref[0, k] = ref[k]
            out_ref[1, k] = ref[inner + k]
        later_ref[...] = ref[:, ahead:]


def parts_of(image_ref, kept_ref, sent_ref, mine):
    many, share = kept_ref.shape[0], kept_ref.shape[3]
    for r in range(many):
        for out_ref, bit in ((kept_ref, mine), (sent_ref, 1 - mine)):
            start = pl.multiple_of((2 * r + bit) * share, share)
            out_ref[r] = image_ref[:, :, pl.ds(start, share), :]


def march_planes(stencil, steps, tiles, many_y, weights, rays, middle, image_ref):
    layers = stencil.layers
    ratio = steps[0] / steps[1]
    many_x = len(rays)
    emission, clear = network(tiles, *weights, steps[1])
    images = [[], []]
    for g in range(LANES // SUB):
        at = pl.ds(g * SUB, SUB)
        rays_y = [(cy_ref[at], ty_ref[at]) for cy_ref, ty_ref in rays]
        for j in range(many_y):
            ray_x = jnp.zeros((SUB, LANES), F32), jnp.ones((SUB, LANES), F32)
            for i in range(many_x):
                if i == REACH and middle is not None:
                    colour, light = ray_x
                    colour = colour + light * middle[0][j, at]
                    ray_x = colour, light * middle[1][j, at]
                start = (j * many_x + i) * LANES + g * SUB
                e, q = emission[start : start + SUB], clear[start : start + SUB]
                rays_y[i] = step_ray(rays_y[i], q, e)
                ray_x = step_ray(ray_x, clear_of_x(q, ratio), e)
            images[0].append(ray_x[0])
            images[1].append(ray_x[1])
        for (cy_ref, ty_ref), ray in zip(rays, rays_y):
            cy_ref[at], ty_ref[at] = ray
    for d in range(layers // SUB):
        for j in range(many_y):
            near, far = d * many_y + j, (d + layers // SUB) * many_y + j
            q = images[1][near]
            at = pl.ds(d * SUB, SUB)
            image_ref[0, j, at] = images[0][near] + q * images[0][far]
            image_ref[1, j, at] = q * images[1][far]


def ends_first_kernel(
    counts,
    steps,
    wide_ref,
    before_ref,
    after_ref,
    win_ref,
    wout_ref,
    once_in_ref,
    twice_in_ref,
    ridge_in_ref,
    slope_in_ref,
    cx_ref,
    tx_ref,
    twice_ref,
    ridge_ref,
    slope_ref,
    cy_ref,
    ty_ref,
    kept_ref,
    sent_ref,
    image_ref,
    raw_ref,
    once_ref,
):
    half, rows, _ = wide_ref.shape
    run = once_ref.shape[2] - 4
    layers = LANES // 2
    stencil = Stencil(run, counts)
    part = rows // 2
    front = iota((part, LANES), 1) < layers
    at_x = lax.axis_index("bx")
    for j in range(REACH):
        before, after = inside_grid("bx", counts[0], before_ref[j], after_ref[j])
        halo, own = before, wide_ref[half - REACH + j]
        raw_ref[0, j, :part] = jnp.where(front, halo, roll(own[:part], layers))
        raw_ref[0, j, part:] = jnp.where(front, roll(halo, layers), roll(own[part:], layers))
        halo, own = after, wide_ref[j]
        raw_ref[1, 2 + j, :part] = jnp.where(front, roll(own[:part], layers), roll(halo, layers))
        raw_ref[1, 2 + j, part:] = jnp.where(front, roll(own[part:], layers), halo)
    for j in range(2):
        raw_ref[0, REACH + j] = wide_ref[j]
        raw_ref[1, j] = wide_ref[half - 2 + j]
    for k in range(4):
        once_ref[0, 3 + k] = once_in_ref[0, k]
        once_ref[1, k] = once_in_ref[1, k]
    for k in range(2):
        twice_ref[0, 3 + k] = twice_in_ref[0, k]
        twice_ref[1, k] = twice_in_ref[1, k]
        ridge_ref[0, 3 + k] = ridge_in_ref[0, k]
        ridge_ref[1, k] = ridge_in_ref[1, k]
        slope_ref[0, 3 + k] = slope_in_ref[0, k]
        slope_ref[1, k] = slope_in_ref[1, k]
    for side, edge in enumerate((stencil.x_low, stencil.x_high)):
        outside = (0, 1) if side == 0 else (1, 2)
        for k in range(3):
            kept = edge if k in outside else None
            stencil.once(raw_ref.at[side], k + 1, once_ref.at[side], k + 4 * side, kept)
    for side, edge in enumerate((stencil.x_low, stencil.x_high)):
        for k in range(3):
            kept = edge if k == 2 * side else None
            at = k + 2 * side
            outs = [ref.at[side] for ref in (twice_ref, ridge_ref, slope_ref)]
            stencil.twice(once_ref.at[side], at + 1, *outs, at, kept)
    for k in range(2 * REACH):
        ty_ref[k] = jnp.ones((LANES, LANES), F32)
        cy_ref[k] = jnp.zeros((LANES, LANES), F32)
    fields = (twice_ref, ridge_ref, slope_ref)
    ahead = image_ref.shape[1]
    tiles = [
        stencil.features(*[ref.at[side] for ref in fields], k, y)
        for y in range(ahead)
        for side in range(2)
        for k in range(1, REACH + 1)
    ]
    rays = [(cy_ref.at[k], ty_ref.at[k]) for k in range(2 * REACH)]
    march_planes(
        stencil, steps, tiles, ahead, (win_ref, wout_ref), rays, (cx_ref, tx_ref), image_ref
    )
    parts_of(image_ref, kept_ref, sent_ref, at_x & 1)


def last_kernel(counts, steps, *refs):
    win_ref, wout_ref, *refs = refs
    ends, middle, refs = refs[:3], refs[3:6], refs[6:]
    cy_ends_ref, ty_ends_ref, cy_middle_ref, ty_middle_ref = refs[:4]
    kept_ref, sent_ref, kept_y_ref, sent_y_ref = refs[4:8]
    image_ref, cy_ref, ty_ref, rows_ref, columns_ref = refs[8:]
    run = ends[0].shape[2] - 2
    stencil = Stencil(run, counts)
    layers = stencil.layers
    inner = cy_middle_ref.shape[0]
    half = inner + 2 * REACH
    many_y = image_ref.shape[1]
    for old, new in ((cy_ends_ref, cy_ref), (ty_ends_ref, ty_ref)):
        new[:REACH], new[half - REACH :] = old[:REACH], old[REACH:]
    for old, new in ((cy_middle_ref, cy_ref), (ty_middle_ref, ty_ref)):
        new[REACH : half - REACH] = old[...]
    tiles = []
    for j in range(many_y):
        for k in range(half):
            if REACH <= k < half - REACH:
                tiles.append(stencil.features(*middle, k - REACH + 1, j))
            else:
                side, k = (0, k + 1) if k < REACH else (1, k - half + REACH + 1)
                fields = [ref.at[side] for ref in ends]
                tiles.append(stencil.features(*fields, k, run - many_y + j))
    rays = [(cy_ref.at[k], ty_ref.at[k]) for k in range(half)]
    march_planes(stencil, steps, tiles, many_y, (win_ref, wout_ref), rays, None, image_ref)
    parts_of(image_ref, kept_ref, sent_ref, lax.axis_index("bx") & 1)
    for k in range(half):
        image = column_image(cy_ref[k], ty_ref[k])
        for kind in range(2):
            rows_ref[kind, k * SUB : (k + 1) * SUB] = image[kind]
    for kind in range(2):
        turned = rows_ref[kind].T
        for part in range(2):
            columns_ref[kind, part] = turned[part * layers : (part + 1) * layers]
    parts_of(columns_ref, kept_y_ref, sent_y_ref, lax.axis_index("by") & 1)


def column_image(colours, clears):
    colours, clears = colours.T, clears.T
    colour, clear = colours[:SUB], clears[:SUB]
    for c in range(1, CHUNKS):
        at = slice(c * SUB, (c + 1) * SUB)
        colour = colour + clear * colours[at]
        clear = clear * clears[at]
    return colour, clear


def merge_kernel(level, kept_ref, received_ref, *refs):
    me = lax.axis_index("by") >> (level - 1)
    later = (me & 1) == 1
    kept, received = kept_ref[...], received_ref[...]
    front = jnp.where(later, received, kept)
    back = jnp.where(later, kept, received)
    many = kept.shape[0]
    colour = front[:, 0] + front[:, 1] * back[:, 0]
    clear = front[:, 1] * back[:, 1]
    if many == 1:
        refs[0][0] = colour[0]
        refs[0][1] = clear[0]
        return
    out_kept_ref, out_sent_ref = refs
    bit = ((me >> 1) & 1) == 1
    for r in range(many // 2):
        for kind, value in enumerate((colour, clear)):
            even, odd = value[2 * r], value[2 * r + 1]
            out_kept_ref[r, kind] = jnp.where(bit, odd, even)
            out_sent_ref[r, kind] = jnp.where(bit, even, odd)


def merge_x_kernel(*refs):
    many = refs[0].shape[0]
    ins, outs = refs[:4], refs[-many:]
    at = lax.axis_index("bx")
    later = (at & 1) == 1
    first = 0
    for kept_ref, received_ref in (ins[:2], ins[2:]):
        last = first + kept_ref.shape[2]
        for t in range(many):
            r = lax.rem((at >> 1) + t, many)
            kept, received = kept_ref[r], received_ref[r]
            front = jnp.where(later, received, kept)
            back = jnp.where(later, kept, received)
            outs[t][0, first:last] = front[0] + front[1] * back[0]
            outs[t][1, first:last] = front[1] * back[1]
        first = last


def fold_x_kernel(*refs):
    pieces, out_ref = refs[:-1], refs[-1]
    _, run, share, _ = pieces[0].shape
    lane = iota((share, LANES), 1)
    me = lax.axis_index("bx") >> 1
    kinds = [[], []]
    for y in range(run):
        behind = colour, clear = jnp.zeros((share, LANES), F32), jnp.ones((share, LANES), F32)
        for s in reversed(range(len(pieces))):
            start = me == s
            behind = jnp.where(start, colour, behind[0]), jnp.where(start, clear, behind[1])
            colour, clear = jnp.where(start, 0.0, colour), jnp.where(start, 1.0, clear)
            colour = colour + clear * pieces[s][0, y]
            clear = clear * pieces[s][1, y]
        kinds[0].append(colour + clear * behind[0])
        kinds[1].append(clear * behind[1])
    for kind, values in enumerate(kinds):
        for s in (1, 2, 4):
            for i in range(run):
                if not i & s:
                    a, b = values[i], values[i | s]
                    odd = (lane & s) != 0
                    values[i] = jnp.where(odd, pltpu.roll(b, s, axis=1), a)
                    values[i | s] = jnp.where(odd, b, pltpu.roll(a, LANES - s, axis=1))
        for band, value in enumerate(values):
            out_ref[kind, band] = value


def exchange(last, first, axis):
    peers = lax.axis_size(axis)
    up = [(i, (i + 1) % peers) for i in range(peers)]
    down = [(j, i) for i, j in up]
    return lax.ppermute(last, axis, up), lax.ppermute(first, axis, down)


def swap(value, axis, bit):
    return lax.ppermute(value, axis, [(i, i ^ bit) for i in range(lax.axis_size(axis))])


def body(scalar_field, transfer_in, transfer_out):
    layers, local_x, local_y = scalar_field.shape
    units, feats = transfer_in.shape
    channels = transfer_out.shape[0]
    bands = channels // 2
    count_x, count_y = lax.axis_size("bx"), lax.axis_size("by")
    steps = (2.0 / (local_x * count_x), 2.0 / (local_y * count_y))
    half, run, rows = local_x // 2, local_y // CHUNKS, rows_of(local_y)
    sds = lambda *shape: jax.ShapeDtypeStruct(shape, F32)
    weights = [
        jax.ShapeDtypeStruct((feats * CHUNKS, units * CHUNKS), BF16),
        jax.ShapeDtypeStruct((units * CHUNKS, channels * CHUNKS), BF16),
    ]

    edge = sds(REACH, half, LANES)
    turned, first, last = call(turn_kernel, "turn", [sds(half, rows, LANES), edge, edge], 1)(
        scalar_field
    )
    before, after = exchange(last, first, "by")
    edge = sds(REACH, rows // 2, LANES)
    wide, first, last = call(
        functools.partial(sides_kernel, local_y, count_y), "sides", [sds(half, rows, LANES), edge, edge], 3
    )(turned, before, after)
    before, after = exchange(last, first, "bx")
    inner = half - 2 * REACH
    counts = (count_x, count_y)
    plane = lambda *lead: sds(*lead, CHUNKS, LANES)
    ahead = run - run // 4
    later = run - ahead
    win, wout, once, twice, ridge, slope, colour_x, clear_x, colour_y, clear_y, *fields = call(
        functools.partial(middle_kernel, counts, steps),
        "middle",
        weights
        + [plane(2, 4, run + 4)]
        + [plane(2, 2, run + 2)] * 3
        + [sds(ahead, LANES, LANES)] * 2
        + [sds(inner, LANES, LANES)] * 2
        + [plane(inner + 2, later + 2)] * 3,
        3,
        [
            pltpu.VMEM((inner + 4, run + 4, CHUNKS, LANES), F32),
            pltpu.VMEM((inner + 2, run + 2, CHUNKS, LANES), F32),
            pltpu.VMEM((inner + 2, run + 2, CHUNKS, LANES), F32),
            pltpu.VMEM((inner + 2, run + 2, CHUNKS, LANES), F32),
        ],
    )(wide, transfer_in, transfer_out)
    share = layers // count_x
    share_y = layers // count_y
    parts = lambda many: [sds(count_x // 2, 2, many, share, LANES)] * 2
    parts_y = sds(count_y // 2, 2, 2, share_y, LANES)
    image = lambda many: pltpu.VMEM((2, many, layers, LANES), F32)
    field = plane(2, 5, run + 2)
    twice, ridge, slope, colour_ends, clear_ends, kept, sent = call(
        functools.partial(ends_first_kernel, counts, steps),
        "ends_first",
        [field] * 3 + [sds(2 * REACH, LANES, LANES)] * 2 + parts(ahead),
        11,
        [
            image(ahead),
            pltpu.VMEM((2, 5, rows, LANES), F32),
            pltpu.VMEM((2, 7, run + 4, CHUNKS, LANES), F32),
        ],
    )(wide, before, after, win, wout, once, twice, ridge, slope, colour_x, clear_x)
    halves = [(kept, swap(sent, "bx", 1))]
    ray = pltpu.VMEM((half, LANES, LANES), F32)
    kept, sent, kept_y, sent_y = call(
        functools.partial(last_kernel, counts, steps),
        "last",
        parts(later) + [parts_y] * 2,
        12,
        [
            image(later),
            ray,
            ray,
            pltpu.VMEM((2, LANES, LANES), F32),
            pltpu.VMEM((2, 2, layers, LANES), F32),
        ],
    )(win, wout, twice, ridge, slope, *fields, colour_ends, clear_ends, colour_y, clear_y)
    halves += [(kept, swap(sent, "bx", 1))]

    level, many = 1, count_y // 2
    while many:
        received = swap(sent_y, "by", level)
        merge = functools.partial(merge_kernel, level.bit_length())
        if many > 1:
            half_parts = sds(many // 2, 2, 2, share_y, LANES)
            kept_y, sent_y = call(merge, "merge", [half_parts] * 2, 2)(kept_y, received)
        else:
            view_y = call(merge, "merge", sds(2, 2, share_y, LANES), 2)(kept_y, received)
        level, many = 2 * level, many // 2
    many = count_x // 2
    piece = sds(2, run, share, LANES)
    operands = [*halves[0], *halves[1], received]
    pieces = list(call(merge_x_kernel, "merge_x", [piece] * many, len(operands))(*operands))
    for t in range(1, many):
        pairs = [(i, (i + 2 * t) % count_x) for i in range(count_x)]
        pieces[t] = lax.ppermute(pieces[t], "bx", pairs)
    view_x = call(fold_x_kernel, "fold_x", sds(2, bands, share, local_y), many)(*pieces)
    view_y = view_y.reshape(2, 2, share_y, half, bands)
    view_y = jnp.transpose(view_y, (0, 4, 2, 1, 3)).reshape(2, bands, share_y, local_x)
    return (view_x, view_y)


def solution(mesh):
    return jax.shard_map(
        body,
        mesh=mesh,
        in_specs=(P(None, "bx", "by"), P(), P()),
        out_specs=(P(None, None, "bx", "by"), P(None, None, "by", "bx")),
        check_vma=False,
    )
```

```python
import functools

import jax
import jax.numpy as jnp
from jax import lax
from jax.experimental import pallas as pl
from jax.experimental.pallas import tpu as pltpu
from jax.sharding import PartitionSpec as P

F32 = jnp.float32
BF16 = jnp.bfloat16
LOG2E = 1.4426950408889634
SUB = 8
LANES = 128
CHUNKS = 16
REACH = 3
VMEM = pl.BlockSpec(memory_space=pltpu.VMEM)
PARAMS = pltpu.CompilerParams(vmem_limit_bytes=36 * 1024 * 1024)


def call(kernel, name, outs, count, scratch=()):
    return pl.pallas_call(
        kernel,
        out_shape=outs,
        in_specs=[VMEM] * count,
        out_specs=jax.tree.map(lambda _: VMEM, outs),
        scratch_shapes=scratch,
        compiler_params=PARAMS,
        name=name,
    )


def rows_of(width):
    return -(-(width + 2 * REACH) // 16) * 16


def iota(shape, dim):
    return lax.broadcasted_iota(jnp.int32, shape, dim)


def one_hot(mask):
    return jnp.where(mask, 1.0, 0.0).astype(BF16)


def spread(weights, left, right, mask):
    inner = lax.dot_general(
        left, weights, (((1,), (1,)), ((), ())), preferred_element_type=F32
    ).astype(BF16)
    return jnp.where(mask, jnp.dot(inner, right, preferred_element_type=F32), 0.0)


def inside_grid(axis, peers, before, after):
    at = lax.axis_index(axis)
    return jnp.where(at == 0, 0.0, before), jnp.where(at == peers - 1, 0.0, after)


def turn_kernel(field_ref, turned_ref, first_ref, last_ref):
    layers, length, width = field_ref.shape
    half = length // 2
    for k in range(half):
        turned = jnp.concatenate([field_ref[:, k, :], field_ref[:, k + half, :]], axis=0).T
        turned_ref[k, REACH : REACH + width] = turned
        for j in range(REACH):
            first_ref[j, k : k + 1] = turned[j : j + 1]
            last_ref[j, k : k + 1] = turned[width - REACH + j : width - REACH + j + 1]


def spread_weights(in_ref, out_ref, win_ref, wout_ref):
    units, feats = in_ref.shape
    channels = out_ref.shape[0]
    bands = channels // 2
    rows, cols = feats * CHUNKS, units * CHUNKS
    left = one_hot(iota((rows, feats), 0) // CHUNKS == iota((rows, feats), 1))
    right = one_hot(iota((units, cols), 1) // CHUNKS == iota((units, cols), 0))
    mask = iota((rows, cols), 0) % CHUNKS == iota((rows, cols), 1) % CHUNKS
    win_ref[...] = (0.5 * spread(in_ref[...], left, right, mask)).astype(BF16)
    rows, cols = cols, channels * CHUNKS
    left = one_hot(iota((rows, units), 0) // CHUNKS == iota((rows, units), 1))
    at = iota((channels, cols), 1)
    right = one_hot((at // LANES) * bands + at % bands == iota((channels, cols), 0))
    mask = iota((rows, cols), 0) % CHUNKS == (iota((rows, cols), 1) % LANES) // bands
    wout_ref[...] = spread(out_ref[...], left, right, mask).astype(BF16)


def sides_kernel(
    width, count_y, turned_ref, before_ref, after_ref, wide_ref, first_ref, last_ref
):
    half, rows, _ = turned_ref.shape
    layers = LANES // 2
    part = rows // 2
    front = iota((part, LANES), 1) < layers
    befores, afters = inside_grid("by", count_y, before_ref[...], after_ref[...])
    for k in range(half):
        wide_ref[k, REACH : REACH + width] = turned_ref[k, REACH : REACH + width]
        for j in range(REACH):
            at = REACH + width + j
            wide_ref[k, j : j + 1] = befores[j, k : k + 1]
            wide_ref[k, at : at + 1] = afters[j, k : k + 1]
        wide_ref[k, 2 * REACH + width :] = jnp.zeros((rows - 2 * REACH - width, LANES), F32)
    for j in range(REACH):
        top, low = wide_ref[j, :part], wide_ref[j, part:]
        first_ref[j] = jnp.where(front, top, pltpu.roll(low, layers, axis=1))
        k = half - REACH + j
        top, low = wide_ref[k, :part], wide_ref[k, part:]
        last_ref[j] = jnp.where(front, pltpu.roll(top, layers, axis=1), low)


class Stencil:
    def __init__(self, run, counts):
        self.run = run
        self.layers = layers = LANES // 2
        self.shape = (CHUNKS, LANES)
        lane, chunk = iota(self.shape, 1), iota(self.shape, 0)
        z = lane % layers
        self.near = (z > 0).astype(F32)
        self.far = (z < layers - 1).astype(F32)
        at_x, at_y = lax.axis_index("bx"), lax.axis_index("by")
        count_x, count_y = counts
        self.x_low = jnp.where((lane < layers) & (at_x == 0), 0.0, 1.0)
        self.x_high = jnp.where((lane >= layers) & (at_x == count_x - 1), 0.0, 1.0)
        self.y_low = jnp.where((chunk == 0) & (at_y == 0), 0.0, 1.0)
        self.y_high = jnp.where((chunk == CHUNKS - 1) & (at_y == count_y - 1), 0.0, 1.0)

    def z_sum(self, value):
        return roll(value, 1) * self.near + roll(value, -1) * self.far

    def inside(self, value, y, edge):
        if edge is not None:
            value = value * edge
        if y < 0:
            value = value * self.y_low
        if y >= self.run:
            value = value * self.y_high
        return value

    def smooth(self, centre, others):
        total = self.z_sum(centre)
        for other in others:
            total = total + other
        return 0.4 * centre + 0.1 * total

    def raw(self, ref, k, y):
        return ref[k, pl.ds(y + REACH, CHUNKS, stride=self.run), :]

    def once(self, raw, k, out, at, edge=None):
        column = [self.raw(raw, k, y) for y in range(-3, self.run + 3)]
        for i in range(1, len(column) - 1):
            y = i - 3
            sides = [self.raw(raw, k - 1, y), self.raw(raw, k + 1, y)]
            value = self.smooth(column[i], [column[i - 1], column[i + 1]] + sides)
            out[at, i - 1] = self.inside(value, y, edge)

    def twice(self, once, k, out, ridge, slope, at, edge=None):
        column = [once[k, i] for i in range(self.run + 4)]
        for i in range(1, len(column) - 1):
            sides = [once[k - 1, i], once[k + 1, i]]
            value = self.smooth(column[i], [column[i - 1], column[i + 1]] + sides)
            value = self.inside(value, i - 2, edge)
            out[at, i - 1] = value
            below, above = roll(value, 1) * self.near, roll(value, -1) * self.far
            ridge[at, i - 1] = 2.0 * value + (below + above)
            slope[at, i - 1] = above - below

    def features(self, twice, ridge, slope, k, y):
        p = lambda a, b: twice[k + a, y + 1 + b]
        r = lambda a, b: ridge[k + a, y + 1 + b]
        centre = p(0, 0)
        main, cross = p(1, 1) - p(-1, -1), p(1, -1) - p(-1, 1)
        third = 1.0 / 3.0
        gx = (main + cross + (r(1, 0) - r(-1, 0))) * third
        gy = (main - cross + (r(0, 1) - r(0, -1))) * third
        d = lambda a, b: slope[k + a, y + 1 + b]
        gz = (2.0 * d(0, 0) + ((d(1, 0) + d(-1, 0)) + (d(0, 1) + d(0, -1)))) * third
        square = 1.0 + gx * gx + gy * gy + gz * gz
        m = square * lax.rsqrt(square)
        parts = [centre, gx, gy, gz, m, centre * m, centre * centre]
        packed = [part.astype(BF16) for part in parts] + [jnp.ones(self.shape, BF16)]
        return jnp.concatenate(packed, axis=0).T


def roll(value, shift):
    return pltpu.roll(value, shift % LANES, axis=1)


def network(tiles, win_ref, wout_ref, step):
    cells = jnp.concatenate(tiles, axis=0)
    half_v = jnp.dot(cells, win_ref[...], preferred_element_type=F32)
    hidden = (half_v + half_v * jnp.tanh(half_v)).astype(BF16)
    v = jnp.dot(hidden, wout_ref[...], preferred_element_type=F32)
    soft = jnp.maximum(v, jnp.log(1.0 + jnp.exp2(jnp.minimum(v * LOG2E, 126.0))))
    return soft[:, :LANES], jnp.exp2(soft[:, LANES:] * (-LOG2E * step))


def clear_of_x(q, ratio):
    if ratio == 1.0:
        return q
    if ratio == 2.0:
        return q * q
    return jnp.exp2(jnp.log(q) * (LOG2E * ratio))


def step_ray(ray, clear, emission):
    colour, light = ray
    later = light * clear
    return colour + (light - later) * emission, later


def middle_kernel(
    counts,
    steps,
    wide_ref,
    in_ref,
    out_ref,
    win_ref,
    wout_ref,
    once_out_ref,
    twice_out_ref,
    ridge_out_ref,
    slope_out_ref,
    cx_ref,
    tx_ref,
    cy_ref,
    ty_ref,
    *refs,
):
    later_refs, (once_ref, twice_ref, ridge_ref, slope_ref) = refs[:3], refs[3:]
    half = wide_ref.shape[0]
    run, ahead = once_ref.shape[1] - 4, cx_ref.shape[0]
    stencil = Stencil(run, counts)
    inner = half - 2 * REACH
    spread_weights(in_ref, out_ref, win_ref, wout_ref)
    for k in range(ahead):
        tx_ref[k] = jnp.ones((LANES, LANES), F32)
        cx_ref[k] = jnp.zeros((LANES, LANES), F32)
    for k in range(inner):
        ty_ref[k] = jnp.ones((LANES, LANES), F32)
        cy_ref[k] = jnp.zeros((LANES, LANES), F32)
    ratio = steps[0] / steps[1]

    def block(x0, y0, many_x, many_y):
        tiles = [
            stencil.features(twice_ref, ridge_ref, slope_ref, x0 + i + 1, y0 + j)
            for j in range(many_y)
            for i in range(many_x)
        ]
        emission, clear = network(tiles, win_ref, wout_ref, steps[1])
        for g in range(LANES // SUB):
            at = pl.ds(g * SUB, SUB)
            rays_y = [(cy_ref[x0 + i, at], ty_ref[x0 + i, at]) for i in range(many_x)]
            for j in range(many_y):
                ray_x = cx_ref[y0 + j, at], tx_ref[y0 + j, at]
                for i in range(many_x):
                    start = (j * many_x + i) * LANES + g * SUB
                    e, q = emission[start : start + SUB], clear[start : start + SUB]
                    rays_y[i] = step_ray(rays_y[i], q, e)
                    ray_x = step_ray(ray_x, clear_of_x(q, ratio), e)
                cx_ref[y0 + j, at], tx_ref[y0 + j, at] = ray_x
            for i in range(many_x):
                cy_ref[x0 + i, at], ty_ref[x0 + i, at] = rays_y[i]

    many_y = 2 if ahead % 2 == 0 else 1
    for k in range(inner + 4):
        stencil.once(wide_ref, k + 1, once_ref, k)
    for k in range(inner + 2):
        stencil.twice(once_ref, k + 1, twice_ref, ridge_ref, slope_ref, k)
    for y0 in range(0, ahead, many_y):
        block(0, y0, inner, many_y)
    for k in range(4):
        once_out_ref[0, k] = once_ref[k]
        once_out_ref[1, k] = once_ref[inner + k]
    fields = (twice_ref, ridge_ref, slope_ref)
    outs = (twice_out_ref, ridge_out_ref, slope_out_ref)
    for out_ref, later_ref, ref in zip(outs, later_refs, fields):
        for k in range(2):
            out_ref[0, k] = ref[k]
            out_ref[1, k] = ref[inner + k]
        later_ref[...] = ref[:, ahead:]


def parts_of(image_ref, kept_ref, sent_ref, mine):
    many, share = kept_ref.shape[0], kept_ref.shape[3]
    for r in range(many):
        for out_ref, bit in ((kept_ref, mine), (sent_ref, 1 - mine)):
            start = pl.multiple_of((2 * r + bit) * share, share)
            out_ref[r] = image_ref[:, :, pl.ds(start, share), :]


def march_planes(stencil, steps, tiles, many_y, weights, rays, middle, image_ref):
    layers = stencil.layers
    ratio = steps[0] / steps[1]
    many_x = len(rays)
    emission, clear = network(tiles, *weights, steps[1])
    images = [[], []]
    for g in range(LANES // SUB):
        at = pl.ds(g * SUB, SUB)
        rays_y = [(cy_ref[at], ty_ref[at]) for cy_ref, ty_ref in rays]
        for j in range(many_y):
            ray_x = jnp.zeros((SUB, LANES), F32), jnp.ones((SUB, LANES), F32)
            for i in range(many_x):
                if i == REACH and middle is not None:
                    colour, light = ray_x
                    colour = colour + light * middle[0][j, at]
                    ray_x = colour, light * middle[1][j, at]
                start = (j * many_x + i) * LANES + g * SUB
                e, q = emission[start : start + SUB], clear[start : start + SUB]
                rays_y[i] = step_ray(rays_y[i], q, e)
                ray_x = step_ray(ray_x, clear_of_x(q, ratio), e)
            images[0].append(ray_x[0])
            images[1].append(ray_x[1])
        for (cy_ref, ty_ref), ray in zip(rays, rays_y):
            cy_ref[at], ty_ref[at] = ray
    for d in range(layers // SUB):
        for j in range(many_y):
            near, far = d * many_y + j, (d + layers // SUB) * many_y + j
            q = images[1][near]
            at = pl.ds(d * SUB, SUB)
            image_ref[0, j, at] = images[0][near] + q * images[0][far]
            image_ref[1, j, at] = q * images[1][far]


def ends_first_kernel(
    counts,
    steps,
    wide_ref,
    before_ref,
    after_ref,
    win_ref,
    wout_ref,
    once_in_ref,
    twice_in_ref,
    ridge_in_ref,
    slope_in_ref,
    cx_ref,
    tx_ref,
    twice_ref,
    ridge_ref,
    slope_ref,
    cy_ref,
    ty_ref,
    kept_ref,
    sent_ref,
    image_ref,
    raw_ref,
    once_ref,
):
    half, rows, _ = wide_ref.shape
    run = once_ref.shape[2] - 4
    layers = LANES // 2
    stencil = Stencil(run, counts)
    part = rows // 2
    front = iota((part, LANES), 1) < layers
    at_x = lax.axis_index("bx")
    for j in range(REACH):
        before, after = inside_grid("bx", counts[0], before_ref[j], after_ref[j])
        halo, own = before, wide_ref[half - REACH + j]
        raw_ref[0, j, :part] = jnp.where(front, halo, roll(own[:part], layers))
        raw_ref[0, j, part:] = jnp.where(front, roll(halo, layers), roll(own[part:], layers))
        halo, own = after, wide_ref[j]
        raw_ref[1, 2 + j, :part] = jnp.where(front, roll(own[:part], layers), roll(halo, layers))
        raw_ref[1, 2 + j, part:] = jnp.where(front, roll(own[part:], layers), halo)
    for j in range(2):
        raw_ref[0, REACH + j] = wide_ref[j]
        raw_ref[1, j] = wide_ref[half - 2 + j]
    for k in range(4):
        once_ref[0, 3 + k] = once_in_ref[0, k]
        once_ref[1, k] = once_in_ref[1, k]
    for k in range(2):
        twice_ref[0, 3 + k] = twice_in_ref[0, k]
        twice_ref[1, k] = twice_in_ref[1, k]
        ridge_ref[0, 3 + k] = ridge_in_ref[0, k]
        ridge_ref[1, k] = ridge_in_ref[1, k]
        slope_ref[0, 3 + k] = slope_in_ref[0, k]
        slope_ref[1, k] = slope_in_ref[1, k]
    for side, edge in enumerate((stencil.x_low, stencil.x_high)):
        outside = (0, 1) if side == 0 else (1, 2)
        for k in range(3):
            kept = edge if k in outside else None
            stencil.once(raw_ref.at[side], k + 1, once_ref.at[side], k + 4 * side, kept)
    for side, edge in enumerate((stencil.x_low, stencil.x_high)):
        for k in range(3):
            kept = edge if k == 2 * side else None
            at = k + 2 * side
            outs = [ref.at[side] for ref in (twice_ref, ridge_ref, slope_ref)]
            stencil.twice(once_ref.at[side], at + 1, *outs, at, kept)
    for k in range(2 * REACH):
        ty_ref[k] = jnp.ones((LANES, LANES), F32)
        cy_ref[k] = jnp.zeros((LANES, LANES), F32)
    fields = (twice_ref, ridge_ref, slope_ref)
    ahead = image_ref.shape[1]
    tiles = [
        stencil.features(*[ref.at[side] for ref in fields], k, y)
        for y in range(ahead)
        for side in range(2)
        for k in range(1, REACH + 1)
    ]
    rays = [(cy_ref.at[k], ty_ref.at[k]) for k in range(2 * REACH)]
    march_planes(
        stencil, steps, tiles, ahead, (win_ref, wout_ref), rays, (cx_ref, tx_ref), image_ref
    )
    parts_of(image_ref, kept_ref, sent_ref, at_x & 1)


def last_kernel(counts, steps, *refs):
    win_ref, wout_ref, *refs = refs
    ends, middle, refs = refs[:3], refs[3:6], refs[6:]
    cy_ends_ref, ty_ends_ref, cy_middle_ref, ty_middle_ref = refs[:4]
    kept_ref, sent_ref, kept_y_ref, sent_y_ref = refs[4:8]
    image_ref, cy_ref, ty_ref, rows_ref, columns_ref = refs[8:]
    run = ends[0].shape[2] - 2
    stencil = Stencil(run, counts)
    layers = stencil.layers
    inner = cy_middle_ref.shape[0]
    half = inner + 2 * REACH
    many_y = image_ref.shape[1]
    for old, new in ((cy_ends_ref, cy_ref), (ty_ends_ref, ty_ref)):
        new[:REACH], new[half - REACH :] = old[:REACH], old[REACH:]
    for old, new in ((cy_middle_ref, cy_ref), (ty_middle_ref, ty_ref)):
        new[REACH : half - REACH] = old[...]
    tiles = []
    for j in range(many_y):
        for k in range(half):
            if REACH <= k < half - REACH:
                tiles.append(stencil.features(*middle, k - REACH + 1, j))
            else:
                side, k = (0, k + 1) if k < REACH else (1, k - half + REACH + 1)
                fields = [ref.at[side] for ref in ends]
                tiles.append(stencil.features(*fields, k, run - many_y + j))
    rays = [(cy_ref.at[k], ty_ref.at[k]) for k in range(half)]
    march_planes(stencil, steps, tiles, many_y, (win_ref, wout_ref), rays, None, image_ref)
    parts_of(image_ref, kept_ref, sent_ref, lax.axis_index("bx") & 1)
    for k in range(half):
        image = column_image(cy_ref[k], ty_ref[k])
        for kind in range(2):
            rows_ref[kind, k * SUB : (k + 1) * SUB] = image[kind]
    for kind in range(2):
        turned = rows_ref[kind].T
        for part in range(2):
            columns_ref[kind, part] = turned[part * layers : (part + 1) * layers]
    parts_of(columns_ref, kept_y_ref, sent_y_ref, lax.axis_index("by") & 1)


def column_image(colours, clears):
    colours, clears = colours.T, clears.T
    colour, clear = colours[:SUB], clears[:SUB]
    for c in range(1, CHUNKS):
        at = slice(c * SUB, (c + 1) * SUB)
        colour = colour + clear * colours[at]
        clear = clear * clears[at]
    return colour, clear


def combine(later, kept, received):
    front = jnp.where(later, received, kept)
    back = jnp.where(later, kept, received)
    colour = front[:, 0] + front[:, 1] * back[:, 0]
    return colour, front[:, 1] * back[:, 1]


def merge_kernel(axis, level, kept_ref, received_ref, *refs):
    me = lax.axis_index(axis) >> (level - 1)
    images = combine((me & 1) == 1, kept_ref[...], received_ref[...])
    if kept_ref.shape[0] == 1:
        for kind, value in enumerate(images):
            refs[0][kind] = value[0]
        return
    out_kept_ref, out_sent_ref = refs[-2:]
    bit = ((me >> 1) & 1) == 1
    for r in range(kept_ref.shape[0] // 2):
        for kind, value in enumerate(images):
            even, odd = value[2 * r], value[2 * r + 1]
            out_kept_ref[r, kind] = jnp.where(bit, odd, even)
            out_sent_ref[r, kind] = jnp.where(bit, even, odd)


def fold_x_kernel(level, *refs):
    out_ref = refs[-1]
    later = ((lax.axis_index("bx") >> (level - 1)) & 1) == 1
    kinds = [[], []]
    for kept_ref, received_ref in (refs[:2], refs[2:4]):
        images = combine(later, kept_ref[...], received_ref[...])
        for values, image in zip(kinds, images):
            values += [image[0, y] for y in range(image.shape[1])]
    run, share = len(kinds[0]), kinds[0][0].shape[0]
    lane = iota((share, LANES), 1)
    for kind, values in enumerate(kinds):
        for s in (1, 2, 4):
            for i in range(run):
                if not i & s:
                    a, b = values[i], values[i | s]
                    odd = (lane & s) != 0
                    values[i] = jnp.where(odd, pltpu.roll(b, s, axis=1), a)
                    values[i | s] = jnp.where(odd, b, pltpu.roll(a, LANES - s, axis=1))
        for band, value in enumerate(values):
            out_ref[kind, band] = value


def exchange(last, first, axis):
    peers = lax.axis_size(axis)
    up = [(i, (i + 1) % peers) for i in range(peers)]
    down = [(j, i) for i, j in up]
    return lax.ppermute(last, axis, up), lax.ppermute(first, axis, down)


def swap(value, axis, bit):
    return lax.ppermute(value, axis, [(i, i ^ bit) for i in range(lax.axis_size(axis))])


def body(scalar_field, transfer_in, transfer_out):
    layers, local_x, local_y = scalar_field.shape
    units, feats = transfer_in.shape
    channels = transfer_out.shape[0]
    bands = channels // 2
    count_x, count_y = lax.axis_size("bx"), lax.axis_size("by")
    steps = (2.0 / (local_x * count_x), 2.0 / (local_y * count_y))
    half, run, rows = local_x // 2, local_y // CHUNKS, rows_of(local_y)
    sds = lambda *shape: jax.ShapeDtypeStruct(shape, F32)
    weights = [
        jax.ShapeDtypeStruct((feats * CHUNKS, units * CHUNKS), BF16),
        jax.ShapeDtypeStruct((units * CHUNKS, channels * CHUNKS), BF16),
    ]

    edge = sds(REACH, half, LANES)
    turned, first, last = call(turn_kernel, "turn", [sds(half, rows, LANES), edge, edge], 1)(
        scalar_field
    )
    before, after = exchange(last, first, "by")
    edge = sds(REACH, rows // 2, LANES)
    wide, first, last = call(
        functools.partial(sides_kernel, local_y, count_y), "sides", [sds(half, rows, LANES), edge, edge], 3
    )(turned, before, after)
    before, after = exchange(last, first, "bx")
    inner = half - 2 * REACH
    counts = (count_x, count_y)
    plane = lambda *lead: sds(*lead, CHUNKS, LANES)
    ahead = run - run // 4
    later = run - ahead
    win, wout, once, twice, ridge, slope, colour_x, clear_x, colour_y, clear_y, *fields = call(
        functools.partial(middle_kernel, counts, steps),
        "middle",
        weights
        + [plane(2, 4, run + 4)]
        + [plane(2, 2, run + 2)] * 3
        + [sds(ahead, LANES, LANES)] * 2
        + [sds(inner, LANES, LANES)] * 2
        + [plane(inner + 2, later + 2)] * 3,
        3,
        [
            pltpu.VMEM((inner + 4, run + 4, CHUNKS, LANES), F32),
            pltpu.VMEM((inner + 2, run + 2, CHUNKS, LANES), F32),
            pltpu.VMEM((inner + 2, run + 2, CHUNKS, LANES), F32),
            pltpu.VMEM((inner + 2, run + 2, CHUNKS, LANES), F32),
        ],
    )(wide, transfer_in, transfer_out)
    share = layers // count_x
    share_y = layers // count_y
    parts = lambda many: [sds(count_x // 2, 2, many, share, LANES)] * 2
    parts_y = sds(count_y // 2, 2, 2, share_y, LANES)
    image = lambda many: pltpu.VMEM((2, many, layers, LANES), F32)
    field = plane(2, 5, run + 2)
    twice, ridge, slope, colour_ends, clear_ends, kept, sent = call(
        functools.partial(ends_first_kernel, counts, steps),
        "ends_first",
        [field] * 3 + [sds(2 * REACH, LANES, LANES)] * 2 + parts(ahead),
        11,
        [
            image(ahead),
            pltpu.VMEM((2, 5, rows, LANES), F32),
            pltpu.VMEM((2, 7, run + 4, CHUNKS, LANES), F32),
        ],
    )(wide, before, after, win, wout, once, twice, ridge, slope, colour_x, clear_x)
    halves = [(kept, swap(sent, "bx", 1))]
    ray = pltpu.VMEM((half, LANES, LANES), F32)
    kept, sent, kept_y, sent_y = call(
        functools.partial(last_kernel, counts, steps),
        "last",
        parts(later) + [parts_y] * 2,
        12,
        [
            image(later),
            ray,
            ray,
            pltpu.VMEM((2, LANES, LANES), F32),
            pltpu.VMEM((2, 2, layers, LANES), F32),
        ],
    )(win, wout, twice, ridge, slope, *fields, colour_ends, clear_ends, colour_y, clear_y)
    halves += [(kept, swap(sent, "bx", 1))]

    def merge(axis, level, kept, received, *order):
        kernel = functools.partial(merge_kernel, axis, level)
        many, *rest = kept.shape
        outs = [sds(many // 2, *rest)] * 2 if many > 1 else sds(*rest)
        operands = (kept, received, *order)
        return call(kernel, "merge", outs, len(operands))(*operands)

    order = (sent_y,)
    level = 1
    while kept_y.shape[0] > 1:
        kept_y, sent_y = merge("by", level, kept_y, swap(sent_y, "by", 1 << (level - 1)))
        level += 1
    view_y = merge("by", level, kept_y, swap(sent_y, "by", 1 << (level - 1)))
    level = 1
    while halves[0][0].shape[0] > 1:
        for i, part in enumerate(halves):
            kept, sent = merge("bx", level, *part, *order)
            halves[i] = (kept, swap(sent, "bx", 1 << level))
        level, order = level + 1, ()
    view_x = call(
        functools.partial(fold_x_kernel, level), "fold_x", sds(2, bands, share, local_y), 4
    )(*halves[0], *halves[1])
    view_y = view_y.reshape(2, 2, share_y, half, bands)
    view_y = jnp.transpose(view_y, (0, 4, 2, 1, 3)).reshape(2, bands, share_y, local_x)
    return (view_x, view_y)


def solution(mesh):
    return jax.shard_map(
        body,
        mesh=mesh,
        in_specs=(P(None, "bx", "by"), P(), P()),
        out_specs=(P(None, None, "bx", "by"), P(None, None, "by", "bx")),
        check_vma=False,
    )
```

```python
import functools

import jax
import jax.numpy as jnp
from jax import lax
from jax.experimental import pallas as pl
from jax.experimental.pallas import tpu as pltpu
from jax.sharding import PartitionSpec as P

F32 = jnp.float32
BF16 = jnp.bfloat16
LOG2E = 1.4426950408889634
SUB = 8
LANES = 128
CHUNKS = 16
REACH = 3
VMEM = pl.BlockSpec(memory_space=pltpu.VMEM)
PARAMS = pltpu.CompilerParams(vmem_limit_bytes=36 * 1024 * 1024)


def call(kernel, name, outs, count, scratch=()):
    return pl.pallas_call(
        kernel,
        out_shape=outs,
        in_specs=[VMEM] * count,
        out_specs=jax.tree.map(lambda _: VMEM, outs),
        scratch_shapes=scratch,
        compiler_params=PARAMS,
        name=name,
    )


def rows_of(width):
    return -(-(width + 2 * REACH) // 16) * 16


def iota(shape, dim):
    return lax.broadcasted_iota(jnp.int32, shape, dim)


def one_hot(mask):
    return jnp.where(mask, 1.0, 0.0).astype(BF16)


def spread(weights, left, right, mask):
    inner = lax.dot_general(
        left, weights, (((1,), (1,)), ((), ())), preferred_element_type=F32
    ).astype(BF16)
    return jnp.where(mask, jnp.dot(inner, right, preferred_element_type=F32), 0.0)


def inside_grid(axis, peers, before, after):
    at = lax.axis_index(axis)
    return jnp.where(at == 0, 0.0, before), jnp.where(at == peers - 1, 0.0, after)


def turn_kernel(field_ref, turned_ref, first_ref, last_ref):
    layers, length, width = field_ref.shape
    half = length // 2
    for k in range(half):
        turned = jnp.concatenate([field_ref[:, k, :], field_ref[:, k + half, :]], axis=0).T
        turned_ref[k, REACH : REACH + width] = turned
        for j in range(REACH):
            first_ref[j, k : k + 1] = turned[j : j + 1]
            last_ref[j, k : k + 1] = turned[width - REACH + j : width - REACH + j + 1]


def spread_weights(in_ref, out_ref, win_ref, wout_ref):
    units, feats = in_ref.shape
    channels = out_ref.shape[0]
    bands = channels // 2
    rows, cols = feats * CHUNKS, units * CHUNKS
    left = one_hot(iota((rows, feats), 0) // CHUNKS == iota((rows, feats), 1))
    right = one_hot(iota((units, cols), 1) // CHUNKS == iota((units, cols), 0))
    mask = iota((rows, cols), 0) % CHUNKS == iota((rows, cols), 1) % CHUNKS
    win_ref[...] = (0.5 * spread(in_ref[...], left, right, mask)).astype(BF16)
    rows, cols = cols, channels * CHUNKS
    left = one_hot(iota((rows, units), 0) // CHUNKS == iota((rows, units), 1))
    at = iota((channels, cols), 1)
    right = one_hot((at // LANES) * bands + at % bands == iota((channels, cols), 0))
    mask = iota((rows, cols), 0) % CHUNKS == (iota((rows, cols), 1) % LANES) // bands
    wout_ref[...] = spread(out_ref[...], left, right, mask).astype(BF16)


def sides_kernel(
    width, count_y, turned_ref, before_ref, after_ref, early_ref, wide_ref, first_ref, last_ref
):
    del early_ref
    half, rows, _ = turned_ref.shape
    layers = LANES // 2
    part = rows // 2
    front = iota((part, LANES), 1) < layers
    befores, afters = inside_grid("by", count_y, before_ref[...], after_ref[...])
    for k in range(half):
        wide_ref[k, REACH : REACH + width] = turned_ref[k, REACH : REACH + width]
        for j in range(REACH):
            at = REACH + width + j
            wide_ref[k, j : j + 1] = befores[j, k : k + 1]
            wide_ref[k, at : at + 1] = afters[j, k : k + 1]
        wide_ref[k, 2 * REACH + width :] = jnp.zeros((rows - 2 * REACH - width, LANES), F32)
    for j in range(REACH):
        top, low = wide_ref[j, :part], wide_ref[j, part:]
        first_ref[j] = jnp.where(front, top, pltpu.roll(low, layers, axis=1))
        k = half - REACH + j
        top, low = wide_ref[k, :part], wide_ref[k, part:]
        last_ref[j] = jnp.where(front, pltpu.roll(top, layers, axis=1), low)


class Stencil:
    def __init__(self, run, counts):
        self.run = run
        self.layers = layers = LANES // 2
        self.shape = (CHUNKS, LANES)
        lane, chunk = iota(self.shape, 1), iota(self.shape, 0)
        z = lane % layers
        self.near = (z > 0).astype(F32)
        self.far = (z < layers - 1).astype(F32)
        at_x, at_y = lax.axis_index("bx"), lax.axis_index("by")
        count_x, count_y = counts
        self.x_low = jnp.where((lane < layers) & (at_x == 0), 0.0, 1.0)
        self.x_high = jnp.where((lane >= layers) & (at_x == count_x - 1), 0.0, 1.0)
        self.y_low = jnp.where((chunk == 0) & (at_y == 0), 0.0, 1.0)
        self.y_high = jnp.where((chunk == CHUNKS - 1) & (at_y == count_y - 1), 0.0, 1.0)

    def z_sum(self, value):
        return roll(value, 1) * self.near + roll(value, -1) * self.far

    def inside(self, value, y, edge):
        if edge is not None:
            value = value * edge
        if y < 0:
            value = value * self.y_low
        if y >= self.run:
            value = value * self.y_high
        return value

    def smooth(self, centre, others):
        total = self.z_sum(centre)
        for other in others:
            total = total + other
        return 0.4 * centre + 0.1 * total

    def raw(self, ref, k, y):
        return ref[k, pl.ds(y + REACH, CHUNKS, stride=self.run), :]

    def once(self, raw, k, out, at, edge=None, offsets=None):
        offsets = range(-2, self.run + 2) if offsets is None else offsets
        held = {y + d: None for y in offsets for d in (-1, 0, 1)}
        held = {y: self.raw(raw, k, y) for y in held}
        for y in offsets:
            i = y + 3
            sides = [self.raw(raw, k - 1, y), self.raw(raw, k + 1, y)]
            value = self.smooth(held[y], [held[y - 1], held[y + 1]] + sides)
            out[at, i - 1] = self.inside(value, y, edge)

    def twice(self, once, k, out, ridge, slope, at, edge=None, offsets=None):
        offsets = range(-1, self.run + 1) if offsets is None else offsets
        held = {y + 2 + d: None for y in offsets for d in (-1, 0, 1)}
        column = {i: once[k, i] for i in held}
        for i in (y + 2 for y in offsets):
            sides = [once[k - 1, i], once[k + 1, i]]
            value = self.smooth(column[i], [column[i - 1], column[i + 1]] + sides)
            value = self.inside(value, i - 2, edge)
            out[at, i - 1] = value
            below, above = roll(value, 1) * self.near, roll(value, -1) * self.far
            ridge[at, i - 1] = 2.0 * value + (below + above)
            slope[at, i - 1] = above - below

    def features(self, twice, ridge, slope, k, y):
        p = lambda a, b: twice[k + a, y + 1 + b]
        r = lambda a, b: ridge[k + a, y + 1 + b]
        centre = p(0, 0)
        main, cross = p(1, 1) - p(-1, -1), p(1, -1) - p(-1, 1)
        third = 1.0 / 3.0
        gx = (main + cross + (r(1, 0) - r(-1, 0))) * third
        gy = (main - cross + (r(0, 1) - r(0, -1))) * third
        d = lambda a, b: slope[k + a, y + 1 + b]
        gz = (2.0 * d(0, 0) + ((d(1, 0) + d(-1, 0)) + (d(0, 1) + d(0, -1)))) * third
        square = 1.0 + gx * gx + gy * gy + gz * gz
        m = square * lax.rsqrt(square)
        parts = [centre, gx, gy, gz, m, centre * m, centre * centre]
        packed = [part.astype(BF16) for part in parts] + [jnp.ones(self.shape, BF16)]
        return jnp.concatenate(packed, axis=0).T


def roll(value, shift):
    return pltpu.roll(value, shift % LANES, axis=1)


def network(tiles, win_ref, wout_ref, step):
    cells = jnp.concatenate(tiles, axis=0)
    half_v = jnp.dot(cells, win_ref[...], preferred_element_type=F32)
    hidden = (half_v + half_v * jnp.tanh(half_v)).astype(BF16)
    v = jnp.dot(hidden, wout_ref[...], preferred_element_type=F32)
    soft = jnp.maximum(v, jnp.log(1.0 + jnp.exp2(jnp.minimum(v * LOG2E, 126.0))))
    return soft[:, :LANES], jnp.exp2(soft[:, LANES:] * (-LOG2E * step))


def clear_of_x(q, ratio):
    if ratio == 1.0:
        return q
    if ratio == 2.0:
        return q * q
    return jnp.exp2(jnp.log(q) * (LOG2E * ratio))


def step_ray(ray, clear, emission):
    colour, light = ray
    later = light * clear
    return colour + (light - later) * emission, later


def early_kernel(
    counts, turned_ref, order_ref, once_ref, twice_ref, ridge_ref, slope_ref
):
    order_ref[...] = jnp.zeros_like(order_ref)
    run = once_ref.shape[1] - 4
    stencil = Stencil(run, counts)
    for k in range(once_ref.shape[0]):
        stencil.once(turned_ref, k + 1, once_ref, k, offsets=range(1, run - 1))
    for k in range(twice_ref.shape[0]):
        outs = (twice_ref, ridge_ref, slope_ref)
        stencil.twice(once_ref, k + 1, *outs, k, offsets=range(2, run - 2))


def middle_kernel(
    counts,
    steps,
    wide_ref,
    in_ref,
    out_ref,
    once_in_ref,
    twice_in_ref,
    ridge_in_ref,
    slope_in_ref,
    win_ref,
    wout_ref,
    once_out_ref,
    twice_out_ref,
    ridge_out_ref,
    slope_out_ref,
    cx_ref,
    tx_ref,
    cy_ref,
    ty_ref,
    *refs,
):
    later_refs, (once_ref, twice_ref, ridge_ref, slope_ref) = refs[:3], refs[3:]
    half = wide_ref.shape[0]
    run, ahead = once_ref.shape[1] - 4, cx_ref.shape[0]
    stencil = Stencil(run, counts)
    inner = half - 2 * REACH
    spread_weights(in_ref, out_ref, win_ref, wout_ref)
    for k in range(ahead):
        tx_ref[k] = jnp.ones((LANES, LANES), F32)
        cx_ref[k] = jnp.zeros((LANES, LANES), F32)
    for k in range(inner):
        ty_ref[k] = jnp.ones((LANES, LANES), F32)
        cy_ref[k] = jnp.zeros((LANES, LANES), F32)
    ratio = steps[0] / steps[1]

    def block(x0, y0, many_x, many_y):
        tiles = [
            stencil.features(twice_ref, ridge_ref, slope_ref, x0 + i + 1, y0 + j)
            for j in range(many_y)
            for i in range(many_x)
        ]
        emission, clear = network(tiles, win_ref, wout_ref, steps[1])
        for g in range(LANES // SUB):
            at = pl.ds(g * SUB, SUB)
            rays_y = [(cy_ref[x0 + i, at], ty_ref[x0 + i, at]) for i in range(many_x)]
            for j in range(many_y):
                ray_x = cx_ref[y0 + j, at], tx_ref[y0 + j, at]
                for i in range(many_x):
                    start = (j * many_x + i) * LANES + g * SUB
                    e, q = emission[start : start + SUB], clear[start : start + SUB]
                    rays_y[i] = step_ray(rays_y[i], q, e)
                    ray_x = step_ray(ray_x, clear_of_x(q, ratio), e)
                cx_ref[y0 + j, at], tx_ref[y0 + j, at] = ray_x
            for i in range(many_x):
                cy_ref[x0 + i, at], ty_ref[x0 + i, at] = rays_y[i]

    many_y = 2 if ahead % 2 == 0 else 1
    once_ref[:, 3 : run + 1] = once_in_ref[:, 3 : run + 1]
    fields = (twice_ref, ridge_ref, slope_ref)
    for ref, in_ref in zip(fields, (twice_in_ref, ridge_in_ref, slope_in_ref)):
        ref[:, 3 : run - 1] = in_ref[:, 3 : run - 1]
    ends = [-2, -1, 0, run - 1, run, run + 1]
    for k in range(inner + 4):
        stencil.once(wide_ref, k + 1, once_ref, k, offsets=ends)
    ends = [-1, 0, 1, run - 2, run - 1, run]
    for k in range(inner + 2):
        stencil.twice(once_ref, k + 1, *fields, k, offsets=ends)
    for y0 in range(0, ahead, many_y):
        block(0, y0, inner, many_y)
    for k in range(4):
        once_out_ref[0, k] = once_ref[k]
        once_out_ref[1, k] = once_ref[inner + k]
    outs = (twice_out_ref, ridge_out_ref, slope_out_ref)
    for out_ref, later_ref, ref in zip(outs, later_refs, fields):
        for k in range(2):
            out_ref[0, k] = ref[k]
            out_ref[1, k] = ref[inner + k]
        later_ref[...] = ref[:, ahead:]


def parts_of(image_ref, kept_ref, sent_ref, mine):
    many, share = kept_ref.shape[0], kept_ref.shape[3]
    for r in range(many):
        for out_ref, bit in ((kept_ref, mine), (sent_ref, 1 - mine)):
            start = pl.multiple_of((2 * r + bit) * share, share)
            out_ref[r] = image_ref[:, :, pl.ds(start, share), :]


def march_planes(stencil, steps, tiles, many_y, weights, rays, middle, image_ref):
    layers = stencil.layers
    ratio = steps[0] / steps[1]
    many_x = len(rays)
    emission, clear = network(tiles, *weights, steps[1])
    images = [[], []]
    for g in range(LANES // SUB):
        at = pl.ds(g * SUB, SUB)
        rays_y = [(cy_ref[at], ty_ref[at]) for cy_ref, ty_ref in rays]
        for j in range(many_y):
            ray_x = jnp.zeros((SUB, LANES), F32), jnp.ones((SUB, LANES), F32)
            for i in range(many_x):
                if i == REACH and middle is not None:
                    colour, light = ray_x
                    colour = colour + light * middle[0][j, at]
                    ray_x = colour, light * middle[1][j, at]
                start = (j * many_x + i) * LANES + g * SUB
                e, q = emission[start : start + SUB], clear[start : start + SUB]
                rays_y[i] = step_ray(rays_y[i], q, e)
                ray_x = step_ray(ray_x, clear_of_x(q, ratio), e)
            images[0].append(ray_x[0])
            images[1].append(ray_x[1])
        for (cy_ref, ty_ref), ray in zip(rays, rays_y):
            cy_ref[at], ty_ref[at] = ray
    for d in range(layers // SUB):
        for j in range(many_y):
            near, far = d * many_y + j, (d + layers // SUB) * many_y + j
            q = images[1][near]
            at = pl.ds(d * SUB, SUB)
            image_ref[0, j, at] = images[0][near] + q * images[0][far]
            image_ref[1, j, at] = q * images[1][far]


def ends_first_kernel(
    counts,
    steps,
    wide_ref,
    before_ref,
    after_ref,
    win_ref,
    wout_ref,
    once_in_ref,
    twice_in_ref,
    ridge_in_ref,
    slope_in_ref,
    cx_ref,
    tx_ref,
    twice_ref,
    ridge_ref,
    slope_ref,
    cy_ref,
    ty_ref,
    kept_ref,
    sent_ref,
    image_ref,
    raw_ref,
    once_ref,
):
    half, rows, _ = wide_ref.shape
    run = once_ref.shape[2] - 4
    layers = LANES // 2
    stencil = Stencil(run, counts)
    part = rows // 2
    front = iota((part, LANES), 1) < layers
    at_x = lax.axis_index("bx")
    for j in range(REACH):
        before, after = inside_grid("bx", counts[0], before_ref[j], after_ref[j])
        halo, own = before, wide_ref[half - REACH + j]
        raw_ref[0, j, :part] = jnp.where(front, halo, roll(own[:part], layers))
        raw_ref[0, j, part:] = jnp.where(front, roll(halo, layers), roll(own[part:], layers))
        halo, own = after, wide_ref[j]
        raw_ref[1, 2 + j, :part] = jnp.where(front, roll(own[:part], layers), roll(halo, layers))
        raw_ref[1, 2 + j, part:] = jnp.where(front, roll(own[part:], layers), halo)
    for j in range(2):
        raw_ref[0, REACH + j] = wide_ref[j]
        raw_ref[1, j] = wide_ref[half - 2 + j]
    for k in range(4):
        once_ref[0, 3 + k] = once_in_ref[0, k]
        once_ref[1, k] = once_in_ref[1, k]
    for k in range(2):
        twice_ref[0, 3 + k] = twice_in_ref[0, k]
        twice_ref[1, k] = twice_in_ref[1, k]
        ridge_ref[0, 3 + k] = ridge_in_ref[0, k]
        ridge_ref[1, k] = ridge_in_ref[1, k]
        slope_ref[0, 3 + k] = slope_in_ref[0, k]
        slope_ref[1, k] = slope_in_ref[1, k]
    for side, edge in enumerate((stencil.x_low, stencil.x_high)):
        outside = (0, 1) if side == 0 else (1, 2)
        for k in range(3):
            kept = edge if k in outside else None
            stencil.once(raw_ref.at[side], k + 1, once_ref.at[side], k + 4 * side, kept)
    for side, edge in enumerate((stencil.x_low, stencil.x_high)):
        for k in range(3):
            kept = edge if k == 2 * side else None
            at = k + 2 * side
            outs = [ref.at[side] for ref in (twice_ref, ridge_ref, slope_ref)]
            stencil.twice(once_ref.at[side], at + 1, *outs, at, kept)
    for k in range(2 * REACH):
        ty_ref[k] = jnp.ones((LANES, LANES), F32)
        cy_ref[k] = jnp.zeros((LANES, LANES), F32)
    fields = (twice_ref, ridge_ref, slope_ref)
    ahead = image_ref.shape[1]
    tiles = [
        stencil.features(*[ref.at[side] for ref in fields], k, y)
        for y in range(ahead)
        for side in range(2)
        for k in range(1, REACH + 1)
    ]
    rays = [(cy_ref.at[k], ty_ref.at[k]) for k in range(2 * REACH)]
    march_planes(
        stencil, steps, tiles, ahead, (win_ref, wout_ref), rays, (cx_ref, tx_ref), image_ref
    )
    parts_of(image_ref, kept_ref, sent_ref, at_x & 1)


def last_kernel(counts, steps, *refs):
    win_ref, wout_ref, *refs = refs
    ends, middle, refs = refs[:3], refs[3:6], refs[6:]
    cy_ends_ref, ty_ends_ref, cy_middle_ref, ty_middle_ref = refs[:4]
    kept_ref, sent_ref, kept_y_ref, sent_y_ref = refs[4:8]
    image_ref, cy_ref, ty_ref, rows_ref, columns_ref = refs[8:]
    run = ends[0].shape[2] - 2
    stencil = Stencil(run, counts)
    layers = stencil.layers
    inner = cy_middle_ref.shape[0]
    half = inner + 2 * REACH
    many_y = image_ref.shape[1]
    for old, new in ((cy_ends_ref, cy_ref), (ty_ends_ref, ty_ref)):
        new[:REACH], new[half - REACH :] = old[:REACH], old[REACH:]
    for old, new in ((cy_middle_ref, cy_ref), (ty_middle_ref, ty_ref)):
        new[REACH : half - REACH] = old[...]
    tiles = []
    for j in range(many_y):
        for k in range(half):
            if REACH <= k < half - REACH:
                tiles.append(stencil.features(*middle, k - REACH + 1, j))
            else:
                side, k = (0, k + 1) if k < REACH else (1, k - half + REACH + 1)
                fields = [ref.at[side] for ref in ends]
                tiles.append(stencil.features(*fields, k, run - many_y + j))
    rays = [(cy_ref.at[k], ty_ref.at[k]) for k in range(half)]
    march_planes(stencil, steps, tiles, many_y, (win_ref, wout_ref), rays, None, image_ref)
    parts_of(image_ref, kept_ref, sent_ref, lax.axis_index("bx") & 1)
    for k in range(half):
        image = column_image(cy_ref[k], ty_ref[k])
        for kind in range(2):
            rows_ref[kind, k * SUB : (k + 1) * SUB] = image[kind]
    for kind in range(2):
        turned = rows_ref[kind].T
        for part in range(2):
            columns_ref[kind, part] = turned[part * layers : (part + 1) * layers]
    parts_of(columns_ref, kept_y_ref, sent_y_ref, lax.axis_index("by") & 1)


def column_image(colours, clears):
    colours, clears = colours.T, clears.T
    colour, clear = colours[:SUB], clears[:SUB]
    for c in range(1, CHUNKS):
        at = slice(c * SUB, (c + 1) * SUB)
        colour = colour + clear * colours[at]
        clear = clear * clears[at]
    return colour, clear


def merge_kernel(level, kept_ref, received_ref, *refs):
    me = lax.axis_index("by") >> (level - 1)
    later = (me & 1) == 1
    kept, received = kept_ref[...], received_ref[...]
    front = jnp.where(later, received, kept)
    back = jnp.where(later, kept, received)
    many = kept.shape[0]
    colour = front[:, 0] + front[:, 1] * back[:, 0]
    clear = front[:, 1] * back[:, 1]
    if many == 1:
        refs[0][0] = colour[0]
        refs[0][1] = clear[0]
        return
    out_kept_ref, out_sent_ref = refs
    bit = ((me >> 1) & 1) == 1
    for r in range(many // 2):
        for kind, value in enumerate((colour, clear)):
            even, odd = value[2 * r], value[2 * r + 1]
            out_kept_ref[r, kind] = jnp.where(bit, odd, even)
            out_sent_ref[r, kind] = jnp.where(bit, even, odd)


def merge_x_kernel(*refs):
    many = refs[0].shape[0]
    ins, outs = refs[:4], refs[-many:]
    at = lax.axis_index("bx")
    later = (at & 1) == 1
    first = 0
    for kept_ref, received_ref in (ins[:2], ins[2:]):
        last = first + kept_ref.shape[2]
        for t in range(many):
            r = lax.rem((at >> 1) + t, many)
            kept, received = kept_ref[r], received_ref[r]
            front = jnp.where(later, received, kept)
            back = jnp.where(later, kept, received)
            outs[t][0, first:last] = front[0] + front[1] * back[0]
            outs[t][1, first:last] = front[1] * back[1]
        first = last


def fold_x_kernel(*refs):
    pieces, out_ref = refs[:-1], refs[-1]
    _, run, share, _ = pieces[0].shape
    lane = iota((share, LANES), 1)
    me = lax.axis_index("bx") >> 1
    kinds = [[], []]
    for y in range(run):
        behind = colour, clear = jnp.zeros((share, LANES), F32), jnp.ones((share, LANES), F32)
        for s in reversed(range(len(pieces))):
            start = me == s
            behind = jnp.where(start, colour, behind[0]), jnp.where(start, clear, behind[1])
            colour, clear = jnp.where(start, 0.0, colour), jnp.where(start, 1.0, clear)
            colour = colour + clear * pieces[s][0, y]
            clear = clear * pieces[s][1, y]
        kinds[0].append(colour + clear * behind[0])
        kinds[1].append(clear * behind[1])
    for kind, values in enumerate(kinds):
        for s in (1, 2, 4):
            for i in range(run):
                if not i & s:
                    a, b = values[i], values[i | s]
                    odd = (lane & s) != 0
                    values[i] = jnp.where(odd, pltpu.roll(b, s, axis=1), a)
                    values[i | s] = jnp.where(odd, b, pltpu.roll(a, LANES - s, axis=1))
        for band, value in enumerate(values):
            out_ref[kind, band] = value


def exchange(last, first, axis):
    peers = lax.axis_size(axis)
    up = [(i, (i + 1) % peers) for i in range(peers)]
    down = [(j, i) for i, j in up]
    return lax.ppermute(last, axis, up), lax.ppermute(first, axis, down)


def swap(value, axis, bit):
    return lax.ppermute(value, axis, [(i, i ^ bit) for i in range(lax.axis_size(axis))])


def body(scalar_field, transfer_in, transfer_out):
    layers, local_x, local_y = scalar_field.shape
    units, feats = transfer_in.shape
    channels = transfer_out.shape[0]
    bands = channels // 2
    count_x, count_y = lax.axis_size("bx"), lax.axis_size("by")
    steps = (2.0 / (local_x * count_x), 2.0 / (local_y * count_y))
    half, run, rows = local_x // 2, local_y // CHUNKS, rows_of(local_y)
    sds = lambda *shape: jax.ShapeDtypeStruct(shape, F32)
    weights = [
        jax.ShapeDtypeStruct((feats * CHUNKS, units * CHUNKS), BF16),
        jax.ShapeDtypeStruct((units * CHUNKS, channels * CHUNKS), BF16),
    ]

    edge = sds(REACH, half, LANES)
    turned, first, last = call(turn_kernel, "turn", [sds(half, rows, LANES), edge, edge], 1)(
        scalar_field
    )
    before, after = exchange(last, first, "by")
    inner = half - 2 * REACH
    counts = (count_x, count_y)
    plane = lambda *lead: sds(*lead, CHUNKS, LANES)
    order, *early = call(
        functools.partial(early_kernel, counts),
        "early",
        [sds(SUB, LANES), plane(inner + 4, run + 4)] + [plane(inner + 2, run + 2)] * 3,
        1,
    )(turned)
    edge = sds(REACH, rows // 2, LANES)
    wide, first, last = call(
        functools.partial(sides_kernel, local_y, count_y), "sides", [sds(half, rows, LANES), edge, edge], 4
    )(turned, before, after, order)
    before, after = exchange(last, first, "bx")
    inner = half - 2 * REACH
    counts = (count_x, count_y)
    plane = lambda *lead: sds(*lead, CHUNKS, LANES)
    ahead = run - run // 4
    later = run - ahead
    win, wout, once, twice, ridge, slope, colour_x, clear_x, colour_y, clear_y, *fields = call(
        functools.partial(middle_kernel, counts, steps),
        "middle",
        weights
        + [plane(2, 4, run + 4)]
        + [plane(2, 2, run + 2)] * 3
        + [sds(ahead, LANES, LANES)] * 2
        + [sds(inner, LANES, LANES)] * 2
        + [plane(inner + 2, later + 2)] * 3,
        7,
        [
            pltpu.VMEM((inner + 4, run + 4, CHUNKS, LANES), F32),
            pltpu.VMEM((inner + 2, run + 2, CHUNKS, LANES), F32),
            pltpu.VMEM((inner + 2, run + 2, CHUNKS, LANES), F32),
            pltpu.VMEM((inner + 2, run + 2, CHUNKS, LANES), F32),
        ],
    )(wide, transfer_in, transfer_out, *early)
    share = layers // count_x
    share_y = layers // count_y
    parts = lambda many: [sds(count_x // 2, 2, many, share, LANES)] * 2
    parts_y = sds(count_y // 2, 2, 2, share_y, LANES)
    image = lambda many: pltpu.VMEM((2, many, layers, LANES), F32)
    field = plane(2, 5, run + 2)
    twice, ridge, slope, colour_ends, clear_ends, kept, sent = call(
        functools.partial(ends_first_kernel, counts, steps),
        "ends_first",
        [field] * 3 + [sds(2 * REACH, LANES, LANES)] * 2 + parts(ahead),
        11,
        [
            image(ahead),
            pltpu.VMEM((2, 5, rows, LANES), F32),
            pltpu.VMEM((2, 7, run + 4, CHUNKS, LANES), F32),
        ],
    )(wide, before, after, win, wout, once, twice, ridge, slope, colour_x, clear_x)
    halves = [(kept, swap(sent, "bx", 1))]
    ray = pltpu.VMEM((half, LANES, LANES), F32)
    kept, sent, kept_y, sent_y = call(
        functools.partial(last_kernel, counts, steps),
        "last",
        parts(later) + [parts_y] * 2,
        12,
        [
            image(later),
            ray,
            ray,
            pltpu.VMEM((2, LANES, LANES), F32),
            pltpu.VMEM((2, 2, layers, LANES), F32),
        ],
    )(win, wout, twice, ridge, slope, *fields, colour_ends, clear_ends, colour_y, clear_y)
    halves += [(kept, swap(sent, "bx", 1))]

    level, many = 1, count_y // 2
    while many:
        received = swap(sent_y, "by", level)
        merge = functools.partial(merge_kernel, level.bit_length())
        if many > 1:
            half_parts = sds(many // 2, 2, 2, share_y, LANES)
            kept_y, sent_y = call(merge, "merge", [half_parts] * 2, 2)(kept_y, received)
        else:
            view_y = call(merge, "merge", sds(2, 2, share_y, LANES), 2)(kept_y, received)
        level, many = 2 * level, many // 2
    many = count_x // 2
    piece = sds(2, run, share, LANES)
    operands = [*halves[0], *halves[1], received]
    pieces = list(call(merge_x_kernel, "merge_x", [piece] * many, len(operands))(*operands))
    for t in range(1, many):
        pairs = [(i, (i + 2 * t) % count_x) for i in range(count_x)]
        pieces[t] = lax.ppermute(pieces[t], "bx", pairs)
    view_x = call(fold_x_kernel, "fold_x", sds(2, bands, share, local_y), many)(*pieces)
    view_y = view_y.reshape(2, 2, share_y, half, bands)
    view_y = jnp.transpose(view_y, (0, 4, 2, 1, 3)).reshape(2, bands, share_y, local_x)
    return (view_x, view_y)


def solution(mesh):
    return jax.shard_map(
        body,
        mesh=mesh,
        in_specs=(P(None, "bx", "by"), P(), P()),
        out_specs=(P(None, None, "bx", "by"), P(None, None, "by", "bx")),
        check_vma=False,
    )
```

```python
import functools

import jax
import jax.numpy as jnp
from jax import lax
from jax.experimental import pallas as pl
from jax.experimental.pallas import tpu as pltpu
from jax.sharding import PartitionSpec as P

F32 = jnp.float32
BF16 = jnp.bfloat16
LOG2E = 1.4426950408889634
SUB = 8
LANES = 128
CHUNKS = 16
REACH = 3
VMEM = pl.BlockSpec(memory_space=pltpu.VMEM)
PARAMS = pltpu.CompilerParams(vmem_limit_bytes=24 * 1024 * 1024)


def call(kernel, name, outs, count, scratch=()):
    return pl.pallas_call(
        kernel,
        out_shape=outs,
        in_specs=[VMEM] * count,
        out_specs=jax.tree.map(lambda _: VMEM, outs),
        scratch_shapes=scratch,
        compiler_params=PARAMS,
        name=name,
    )


def rows_of(width):
    return -(-(width + 2 * REACH) // 16) * 16


def iota(shape, dim):
    return lax.broadcasted_iota(jnp.int32, shape, dim)


def one_hot(mask):
    return jnp.where(mask, 1.0, 0.0).astype(BF16)


def spread(weights, left, right, mask):
    inner = lax.dot_general(
        left, weights, (((1,), (1,)), ((), ())), preferred_element_type=F32
    ).astype(BF16)
    return jnp.where(mask, jnp.dot(inner, right, preferred_element_type=F32), 0.0)


def inside_grid(axis, peers, before, after):
    at = lax.axis_index(axis)
    return jnp.where(at == 0, 0.0, before), jnp.where(at == peers - 1, 0.0, after)


def turn_kernel(field_ref, turned_ref, first_ref, last_ref):
    layers, length, width = field_ref.shape
    half = length // 2
    for k in range(half):
        turned = jnp.concatenate([field_ref[:, k, :], field_ref[:, k + half, :]], axis=0).T
        turned_ref[k, REACH : REACH + width] = turned
        for j in range(REACH):
            first_ref[j, k : k + 1] = turned[j : j + 1]
            last_ref[j, k : k + 1] = turned[width - REACH + j : width - REACH + j + 1]


def spread_weights(in_ref, out_ref, win_ref, wout_ref):
    units, feats = in_ref.shape
    channels = out_ref.shape[0]
    bands = channels // 2
    rows, cols = feats * CHUNKS, units * CHUNKS
    left = one_hot(iota((rows, feats), 0) // CHUNKS == iota((rows, feats), 1))
    right = one_hot(iota((units, cols), 1) // CHUNKS == iota((units, cols), 0))
    mask = iota((rows, cols), 0) % CHUNKS == iota((rows, cols), 1) % CHUNKS
    win_ref[...] = (0.5 * spread(in_ref[...], left, right, mask)).astype(BF16)
    rows, cols = cols, channels * CHUNKS
    left = one_hot(iota((rows, units), 0) // CHUNKS == iota((rows, units), 1))
    at = iota((channels, cols), 1)
    right = one_hot((at // LANES) * bands + at % bands == iota((channels, cols), 0))
    mask = iota((rows, cols), 0) % CHUNKS == (iota((rows, cols), 1) % LANES) // bands
    wout_ref[...] = spread(out_ref[...], left, right, mask).astype(BF16)


def sides_kernel(
    width, count_y, turned_ref, before_ref, after_ref, early_ref, wide_ref, first_ref, last_ref
):
    del early_ref
    half, rows, _ = turned_ref.shape
    layers = LANES // 2
    part = rows // 2
    front = iota((part, LANES), 1) < layers
    befores, afters = inside_grid("by", count_y, before_ref[...], after_ref[...])
    for k in range(half):
        wide_ref[k, REACH : REACH + width] = turned_ref[k, REACH : REACH + width]
        for j in range(REACH):
            at = REACH + width + j
            wide_ref[k, j : j + 1] = befores[j, k : k + 1]
            wide_ref[k, at : at + 1] = afters[j, k : k + 1]
        wide_ref[k, 2 * REACH + width :] = jnp.zeros((rows - 2 * REACH - width, LANES), F32)
    for j in range(REACH):
        top, low = wide_ref[j, :part], wide_ref[j, part:]
        first_ref[j] = jnp.where(front, top, pltpu.roll(low, layers, axis=1))
        k = half - REACH + j
        top, low = wide_ref[k, :part], wide_ref[k, part:]
        last_ref[j] = jnp.where(front, pltpu.roll(top, layers, axis=1), low)


class Stencil:
    def __init__(self, run, counts):
        self.run = run
        self.layers = layers = LANES // 2
        self.shape = (CHUNKS, LANES)
        lane, chunk = iota(self.shape, 1), iota(self.shape, 0)
        z = lane % layers
        self.near = (z > 0).astype(F32)
        self.far = (z < layers - 1).astype(F32)
        at_x, at_y = lax.axis_index("bx"), lax.axis_index("by")
        count_x, count_y = counts
        self.x_low = jnp.where((lane < layers) & (at_x == 0), 0.0, 1.0)
        self.x_high = jnp.where((lane >= layers) & (at_x == count_x - 1), 0.0, 1.0)
        self.y_low = jnp.where((chunk == 0) & (at_y == 0), 0.0, 1.0)
        self.y_high = jnp.where((chunk == CHUNKS - 1) & (at_y == count_y - 1), 0.0, 1.0)

    def z_sum(self, value):
        return roll(value, 1) * self.near + roll(value, -1) * self.far

    def inside(self, value, y, edge):
        if edge is not None:
            value = value * edge
        if y < 0:
            value = value * self.y_low
        if y >= self.run:
            value = value * self.y_high
        return value

    def smooth(self, centre, others):
        total = self.z_sum(centre)
        for other in others:
            total = total + other
        return 0.4 * centre + 0.1 * total

    def raw(self, ref, k, y):
        return ref[k, pl.ds(y + REACH, CHUNKS, stride=self.run), :]

    def once(self, raw, k, out, at, edge=None, offsets=None):
        offsets = range(-2, self.run + 2) if offsets is None else offsets
        held = {y + d: None for y in offsets for d in (-1, 0, 1)}
        held = {y: self.raw(raw, k, y) for y in held}
        for y in offsets:
            i = y + 3
            sides = [self.raw(raw, k - 1, y), self.raw(raw, k + 1, y)]
            value = self.smooth(held[y], [held[y - 1], held[y + 1]] + sides)
            out[at, i - 1] = self.inside(value, y, edge)

    def twice(self, once, k, out, ridge, slope, at, edge=None, offsets=None):
        offsets = range(-1, self.run + 1) if offsets is None else offsets
        held = {y + 2 + d: None for y in offsets for d in (-1, 0, 1)}
        column = {i: once[k, i] for i in held}
        for i in (y + 2 for y in offsets):
            sides = [once[k - 1, i], once[k + 1, i]]
            value = self.smooth(column[i], [column[i - 1], column[i + 1]] + sides)
            value = self.inside(value, i - 2, edge)
            out[at, i - 1] = value
            below, above = roll(value, 1) * self.near, roll(value, -1) * self.far
            ridge[at, i - 1] = 2.0 * value + (below + above)
            slope[at, i - 1] = above - below

    def features(self, twice, ridge, slope, k, y):
        p = lambda a, b: twice[k + a, y + 1 + b]
        r = lambda a, b: ridge[k + a, y + 1 + b]
        centre = p(0, 0)
        main, cross = p(1, 1) - p(-1, -1), p(1, -1) - p(-1, 1)
        third = 1.0 / 3.0
        gx = (main + cross + (r(1, 0) - r(-1, 0))) * third
        gy = (main - cross + (r(0, 1) - r(0, -1))) * third
        d = lambda a, b: slope[k + a, y + 1 + b]
        gz = (2.0 * d(0, 0) + ((d(1, 0) + d(-1, 0)) + (d(0, 1) + d(0, -1)))) * third
        square = 1.0 + gx * gx + gy * gy + gz * gz
        m = square * lax.rsqrt(square)
        parts = [centre, gx, gy, gz, m, centre * m, centre * centre]
        packed = [part.astype(BF16) for part in parts] + [jnp.ones(self.shape, BF16)]
        return jnp.concatenate(packed, axis=0).T


def roll(value, shift):
    return pltpu.roll(value, shift % LANES, axis=1)


def network(tiles, win_ref, wout_ref, step):
    cells = jnp.concatenate(tiles, axis=0)
    half_v = jnp.dot(cells, win_ref[...], preferred_element_type=F32)
    hidden = (half_v + half_v * jnp.tanh(half_v)).astype(BF16)
    v = jnp.dot(hidden, wout_ref[...], preferred_element_type=F32)
    soft = jnp.maximum(v, jnp.log(1.0 + jnp.exp2(jnp.minimum(v * LOG2E, 126.0))))
    return soft[:, :LANES], jnp.exp2(soft[:, LANES:] * (-LOG2E * step))


def clear_of_x(q, ratio):
    if ratio == 1.0:
        return q
    if ratio == 2.0:
        return q * q
    return jnp.exp2(jnp.log(q) * (LOG2E * ratio))


def step_ray(ray, clear, emission):
    colour, light = ray
    later = light * clear
    return colour + (light - later) * emission, later


def early_kernel(
    counts, turned_ref, order_ref, *refs
):
    outs, (once_ref, twice_ref, ridge_ref, slope_ref) = refs[:4], refs[4:]
    order_ref[...] = jnp.zeros_like(order_ref)
    run = once_ref.shape[1] - 4
    stencil = Stencil(run, counts)
    for k in range(once_ref.shape[0]):
        stencil.once(turned_ref, k + 1, once_ref, k, offsets=range(1, run - 1))
    for k in range(twice_ref.shape[0]):
        fields = (twice_ref, ridge_ref, slope_ref)
        stencil.twice(once_ref, k + 1, *fields, k, offsets=range(2, run - 2))
    outs[0][...] = once_ref[:, 3 : run + 1]
    for out_ref, ref in zip(outs[1:], (twice_ref, ridge_ref, slope_ref)):
        out_ref[...] = ref[:, 3 : run - 1]


def middle_kernel(
    counts,
    steps,
    wide_ref,
    in_ref,
    out_ref,
    once_in_ref,
    twice_in_ref,
    ridge_in_ref,
    slope_in_ref,
    win_ref,
    wout_ref,
    once_out_ref,
    twice_out_ref,
    ridge_out_ref,
    slope_out_ref,
    cx_ref,
    tx_ref,
    cy_ref,
    ty_ref,
    *refs,
):
    later_refs, (once_ref, twice_ref, ridge_ref, slope_ref) = refs[:3], refs[3:]
    half = wide_ref.shape[0]
    run, ahead = once_ref.shape[1] - 4, cx_ref.shape[0]
    stencil = Stencil(run, counts)
    inner = half - 2 * REACH
    spread_weights(in_ref, out_ref, win_ref, wout_ref)
    for k in range(ahead):
        tx_ref[k] = jnp.ones((LANES, LANES), F32)
        cx_ref[k] = jnp.zeros((LANES, LANES), F32)
    for k in range(inner):
        ty_ref[k] = jnp.ones((LANES, LANES), F32)
        cy_ref[k] = jnp.zeros((LANES, LANES), F32)
    ratio = steps[0] / steps[1]

    def block(x0, y0, many_x, many_y):
        tiles = [
            stencil.features(twice_ref, ridge_ref, slope_ref, x0 + i + 1, y0 + j)
            for j in range(many_y)
            for i in range(many_x)
        ]
        emission, clear = network(tiles, win_ref, wout_ref, steps[1])
        for g in range(LANES // SUB):
            at = pl.ds(g * SUB, SUB)
            rays_y = [(cy_ref[x0 + i, at], ty_ref[x0 + i, at]) for i in range(many_x)]
            for j in range(many_y):
                ray_x = cx_ref[y0 + j, at], tx_ref[y0 + j, at]
                for i in range(many_x):
                    start = (j * many_x + i) * LANES + g * SUB
                    e, q = emission[start : start + SUB], clear[start : start + SUB]
                    rays_y[i] = step_ray(rays_y[i], q, e)
                    ray_x = step_ray(ray_x, clear_of_x(q, ratio), e)
                cx_ref[y0 + j, at], tx_ref[y0 + j, at] = ray_x
            for i in range(many_x):
                cy_ref[x0 + i, at], ty_ref[x0 + i, at] = rays_y[i]

    many_y = 2 if ahead % 2 == 0 else 1
    once_ref[:, 3 : run + 1] = once_in_ref[...]
    fields = (twice_ref, ridge_ref, slope_ref)
    for ref, in_ref in zip(fields, (twice_in_ref, ridge_in_ref, slope_in_ref)):
        ref[:, 3 : run - 1] = in_ref[...]
    ends = [-2, -1, 0, run - 1, run, run + 1]
    for k in range(inner + 4):
        stencil.once(wide_ref, k + 1, once_ref, k, offsets=ends)
    ends = [-1, 0, 1, run - 2, run - 1, run]
    for k in range(inner + 2):
        stencil.twice(once_ref, k + 1, *fields, k, offsets=ends)
    for y0 in range(0, ahead, many_y):
        block(0, y0, inner, many_y)
    for k in range(4):
        once_out_ref[0, k] = once_ref[k]
        once_out_ref[1, k] = once_ref[inner + k]
    outs = (twice_out_ref, ridge_out_ref, slope_out_ref)
    for out_ref, later_ref, ref in zip(outs, later_refs, fields):
        for k in range(2):
            out_ref[0, k] = ref[k]
            out_ref[1, k] = ref[inner + k]
        later_ref[...] = ref[:, ahead:]


def parts_of(image_ref, kept_ref, sent_ref, mine):
    many, share = kept_ref.shape[0], kept_ref.shape[3]
    for r in range(many):
        for out_ref, bit in ((kept_ref, mine), (sent_ref, 1 - mine)):
            start = pl.multiple_of((2 * r + bit) * share, share)
            out_ref[r] = image_ref[:, :, pl.ds(start, share), :]


def march_planes(stencil, steps, tiles, many_y, weights, rays, middle, image_ref):
    layers = stencil.layers
    ratio = steps[0] / steps[1]
    many_x = len(rays)
    emission, clear = network(tiles, *weights, steps[1])
    images = [[], []]
    for g in range(LANES // SUB):
        at = pl.ds(g * SUB, SUB)
        rays_y = [(cy_ref[at], ty_ref[at]) for cy_ref, ty_ref in rays]
        for j in range(many_y):
            ray_x = jnp.zeros((SUB, LANES), F32), jnp.ones((SUB, LANES), F32)
            for i in range(many_x):
                if i == REACH and middle is not None:
                    colour, light = ray_x
                    colour = colour + light * middle[0][j, at]
                    ray_x = colour, light * middle[1][j, at]
                start = (j * many_x + i) * LANES + g * SUB
                e, q = emission[start : start + SUB], clear[start : start + SUB]
                rays_y[i] = step_ray(rays_y[i], q, e)
                ray_x = step_ray(ray_x, clear_of_x(q, ratio), e)
            images[0].append(ray_x[0])
            images[1].append(ray_x[1])
        for (cy_ref, ty_ref), ray in zip(rays, rays_y):
            cy_ref[at], ty_ref[at] = ray
    for d in range(layers // SUB):
        for j in range(many_y):
            near, far = d * many_y + j, (d + layers // SUB) * many_y + j
            q = images[1][near]
            at = pl.ds(d * SUB, SUB)
            image_ref[0, j, at] = images[0][near] + q * images[0][far]
            image_ref[1, j, at] = q * images[1][far]


def ends_first_kernel(
    counts,
    steps,
    wide_ref,
    before_ref,
    after_ref,
    win_ref,
    wout_ref,
    once_in_ref,
    twice_in_ref,
    ridge_in_ref,
    slope_in_ref,
    cx_ref,
    tx_ref,
    twice_ref,
    ridge_ref,
    slope_ref,
    cy_ref,
    ty_ref,
    kept_ref,
    sent_ref,
    image_ref,
    raw_ref,
    once_ref,
):
    half, rows, _ = wide_ref.shape
    run = once_ref.shape[2] - 4
    layers = LANES // 2
    stencil = Stencil(run, counts)
    part = rows // 2
    front = iota((part, LANES), 1) < layers
    at_x = lax.axis_index("bx")
    for j in range(REACH):
        before, after = inside_grid("bx", counts[0], before_ref[j], after_ref[j])
        halo, own = before, wide_ref[half - REACH + j]
        raw_ref[0, j, :part] = jnp.where(front, halo, roll(own[:part], layers))
        raw_ref[0, j, part:] = jnp.where(front, roll(halo, layers), roll(own[part:], layers))
        halo, own = after, wide_ref[j]
        raw_ref[1, 2 + j, :part] = jnp.where(front, roll(own[:part], layers), roll(halo, layers))
        raw_ref[1, 2 + j, part:] = jnp.where(front, roll(own[part:], layers), halo)
    for j in range(2):
        raw_ref[0, REACH + j] = wide_ref[j]
        raw_ref[1, j] = wide_ref[half - 2 + j]
    for k in range(4):
        once_ref[0, 3 + k] = once_in_ref[0, k]
        once_ref[1, k] = once_in_ref[1, k]
    for k in range(2):
        twice_ref[0, 3 + k] = twice_in_ref[0, k]
        twice_ref[1, k] = twice_in_ref[1, k]
        ridge_ref[0, 3 + k] = ridge_in_ref[0, k]
        ridge_ref[1, k] = ridge_in_ref[1, k]
        slope_ref[0, 3 + k] = slope_in_ref[0, k]
        slope_ref[1, k] = slope_in_ref[1, k]
    for side, edge in enumerate((stencil.x_low, stencil.x_high)):
        outside = (0, 1) if side == 0 else (1, 2)
        for k in range(3):
            kept = edge if k in outside else None
            stencil.once(raw_ref.at[side], k + 1, once_ref.at[side], k + 4 * side, kept)
    for side, edge in enumerate((stencil.x_low, stencil.x_high)):
        for k in range(3):
            kept = edge if k == 2 * side else None
            at = k + 2 * side
            outs = [ref.at[side] for ref in (twice_ref, ridge_ref, slope_ref)]
            stencil.twice(once_ref.at[side], at + 1, *outs, at, kept)
    for k in range(2 * REACH):
        ty_ref[k] = jnp.ones((LANES, LANES), F32)
        cy_ref[k] = jnp.zeros((LANES, LANES), F32)
    fields = (twice_ref, ridge_ref, slope_ref)
    ahead = image_ref.shape[1]
    tiles = [
        stencil.features(*[ref.at[side] for ref in fields], k, y)
        for y in range(ahead)
        for side in range(2)
        for k in range(1, REACH + 1)
    ]
    rays = [(cy_ref.at[k], ty_ref.at[k]) for k in range(2 * REACH)]
    march_planes(
        stencil, steps, tiles, ahead, (win_ref, wout_ref), rays, (cx_ref, tx_ref), image_ref
    )
    parts_of(image_ref, kept_ref, sent_ref, at_x & 1)


def last_kernel(counts, steps, *refs):
    win_ref, wout_ref, *refs = refs
    ends, middle, refs = refs[:3], refs[3:6], refs[6:]
    cy_ends_ref, ty_ends_ref, cy_middle_ref, ty_middle_ref = refs[:4]
    kept_ref, sent_ref, kept_y_ref, sent_y_ref = refs[4:8]
    image_ref, cy_ref, ty_ref, rows_ref, columns_ref = refs[8:]
    run = ends[0].shape[2] - 2
    stencil = Stencil(run, counts)
    layers = stencil.layers
    inner = cy_middle_ref.shape[0]
    half = inner + 2 * REACH
    many_y = image_ref.shape[1]
    for old, new in ((cy_ends_ref, cy_ref), (ty_ends_ref, ty_ref)):
        new[:REACH], new[half - REACH :] = old[:REACH], old[REACH:]
    for old, new in ((cy_middle_ref, cy_ref), (ty_middle_ref, ty_ref)):
        new[REACH : half - REACH] = old[...]
    tiles = []
    for j in range(many_y):
        for k in range(half):
            if REACH <= k < half - REACH:
                tiles.append(stencil.features(*middle, k - REACH + 1, j))
            else:
                side, k = (0, k + 1) if k < REACH else (1, k - half + REACH + 1)
                fields = [ref.at[side] for ref in ends]
                tiles.append(stencil.features(*fields, k, run - many_y + j))
    rays = [(cy_ref.at[k], ty_ref.at[k]) for k in range(half)]
    march_planes(stencil, steps, tiles, many_y, (win_ref, wout_ref), rays, None, image_ref)
    parts_of(image_ref, kept_ref, sent_ref, lax.axis_index("bx") & 1)
    for k in range(half):
        image = column_image(cy_ref[k], ty_ref[k])
        for kind in range(2):
            rows_ref[kind, k * SUB : (k + 1) * SUB] = image[kind]
    for kind in range(2):
        turned = rows_ref[kind].T
        for part in range(2):
            columns_ref[kind, part] = turned[part * layers : (part + 1) * layers]
    parts_of(columns_ref, kept_y_ref, sent_y_ref, lax.axis_index("by") & 1)


def column_image(colours, clears):
    colours, clears = colours.T, clears.T
    colour, clear = colours[:SUB], clears[:SUB]
    for c in range(1, CHUNKS):
        at = slice(c * SUB, (c + 1) * SUB)
        colour = colour + clear * colours[at]
        clear = clear * clears[at]
    return colour, clear


def merge_kernel(level, kept_ref, received_ref, *refs):
    me = lax.axis_index("by") >> (level - 1)
    later = (me & 1) == 1
    kept, received = kept_ref[...], received_ref[...]
    front = jnp.where(later, received, kept)
    back = jnp.where(later, kept, received)
    many = kept.shape[0]
    colour = front[:, 0] + front[:, 1] * back[:, 0]
    clear = front[:, 1] * back[:, 1]
    if many == 1:
        refs[0][0] = colour[0]
        refs[0][1] = clear[0]
        return
    out_kept_ref, out_sent_ref = refs
    bit = ((me >> 1) & 1) == 1
    for r in range(many // 2):
        for kind, value in enumerate((colour, clear)):
            even, odd = value[2 * r], value[2 * r + 1]
            out_kept_ref[r, kind] = jnp.where(bit, odd, even)
            out_sent_ref[r, kind] = jnp.where(bit, even, odd)


def merge_x_kernel(*refs):
    many = refs[0].shape[0]
    ins, outs = refs[:4], refs[-many:]
    at = lax.axis_index("bx")
    later = (at & 1) == 1
    first = 0
    for kept_ref, received_ref in (ins[:2], ins[2:]):
        last = first + kept_ref.shape[2]
        for t in range(many):
            r = lax.rem((at >> 1) + t, many)
            kept, received = kept_ref[r], received_ref[r]
            front = jnp.where(later, received, kept)
            back = jnp.where(later, kept, received)
            outs[t][0, first:last] = front[0] + front[1] * back[0]
            outs[t][1, first:last] = front[1] * back[1]
        first = last


def fold_x_kernel(*refs):
    pieces, out_ref = refs[:-1], refs[-1]
    _, run, share, _ = pieces[0].shape
    lane = iota((share, LANES), 1)
    me = lax.axis_index("bx") >> 1
    kinds = [[], []]
    for y in range(run):
        behind = colour, clear = jnp.zeros((share, LANES), F32), jnp.ones((share, LANES), F32)
        for s in reversed(range(len(pieces))):
            start = me == s
            behind = jnp.where(start, colour, behind[0]), jnp.where(start, clear, behind[1])
            colour, clear = jnp.where(start, 0.0, colour), jnp.where(start, 1.0, clear)
            colour = colour + clear * pieces[s][0, y]
            clear = clear * pieces[s][1, y]
        kinds[0].append(colour + clear * behind[0])
        kinds[1].append(clear * behind[1])
    for kind, values in enumerate(kinds):
        for s in (1, 2, 4):
            for i in range(run):
                if not i & s:
                    a, b = values[i], values[i | s]
                    odd = (lane & s) != 0
                    values[i] = jnp.where(odd, pltpu.roll(b, s, axis=1), a)
                    values[i | s] = jnp.where(odd, b, pltpu.roll(a, LANES - s, axis=1))
        for band, value in enumerate(values):
            out_ref[kind, band] = value


def exchange(last, first, axis):
    peers = lax.axis_size(axis)
    up = [(i, (i + 1) % peers) for i in range(peers)]
    down = [(j, i) for i, j in up]
    return lax.ppermute(last, axis, up), lax.ppermute(first, axis, down)


def swap(value, axis, bit):
    return lax.ppermute(value, axis, [(i, i ^ bit) for i in range(lax.axis_size(axis))])


def body(scalar_field, transfer_in, transfer_out):
    layers, local_x, local_y = scalar_field.shape
    units, feats = transfer_in.shape
    channels = transfer_out.shape[0]
    bands = channels // 2
    count_x, count_y = lax.axis_size("bx"), lax.axis_size("by")
    steps = (2.0 / (local_x * count_x), 2.0 / (local_y * count_y))
    half, run, rows = local_x // 2, local_y // CHUNKS, rows_of(local_y)
    sds = lambda *shape: jax.ShapeDtypeStruct(shape, F32)
    weights = [
        jax.ShapeDtypeStruct((feats * CHUNKS, units * CHUNKS), BF16),
        jax.ShapeDtypeStruct((units * CHUNKS, channels * CHUNKS), BF16),
    ]

    edge = sds(REACH, half, LANES)
    turned, first, last = call(turn_kernel, "turn", [sds(half, rows, LANES), edge, edge], 1)(
        scalar_field
    )
    before, after = exchange(last, first, "by")
    inner = half - 2 * REACH
    counts = (count_x, count_y)
    plane = lambda *lead: sds(*lead, CHUNKS, LANES)
    order, *early = call(
        functools.partial(early_kernel, counts),
        "early",
        [sds(SUB, LANES), plane(inner + 4, run - 2)] + [plane(inner + 2, run - 4)] * 3,
        1,
        [pltpu.VMEM((inner + 4, run + 4, CHUNKS, LANES), F32)]
        + [pltpu.VMEM((inner + 2, run + 2, CHUNKS, LANES), F32)] * 3,
    )(turned)
    edge = sds(REACH, rows // 2, LANES)
    wide, first, last = call(
        functools.partial(sides_kernel, local_y, count_y), "sides", [sds(half, rows, LANES), edge, edge], 4
    )(turned, before, after, order)
    before, after = exchange(last, first, "bx")
    inner = half - 2 * REACH
    counts = (count_x, count_y)
    plane = lambda *lead: sds(*lead, CHUNKS, LANES)
    ahead = run - run // 4
    later = run - ahead
    win, wout, once, twice, ridge, slope, colour_x, clear_x, colour_y, clear_y, *fields = call(
        functools.partial(middle_kernel, counts, steps),
        "middle",
        weights
        + [plane(2, 4, run + 4)]
        + [plane(2, 2, run + 2)] * 3
        + [sds(ahead, LANES, LANES)] * 2
        + [sds(inner, LANES, LANES)] * 2
        + [plane(inner + 2, later + 2)] * 3,
        7,
        [
            pltpu.VMEM((inner + 4, run + 4, CHUNKS, LANES), F32),
            pltpu.VMEM((inner + 2, run + 2, CHUNKS, LANES), F32),
            pltpu.VMEM((inner + 2, run + 2, CHUNKS, LANES), F32),
            pltpu.VMEM((inner + 2, run + 2, CHUNKS, LANES), F32),
        ],
    )(wide, transfer_in, transfer_out, *early)
    share = layers // count_x
    share_y = layers // count_y
    parts = lambda many: [sds(count_x // 2, 2, many, share, LANES)] * 2
    parts_y = sds(count_y // 2, 2, 2, share_y, LANES)
    image = lambda many: pltpu.VMEM((2, many, layers, LANES), F32)
    field = plane(2, 5, run + 2)
    twice, ridge, slope, colour_ends, clear_ends, kept, sent = call(
        functools.partial(ends_first_kernel, counts, steps),
        "ends_first",
        [field] * 3 + [sds(2 * REACH, LANES, LANES)] * 2 + parts(ahead),
        11,
        [
            image(ahead),
            pltpu.VMEM((2, 5, rows, LANES), F32),
            pltpu.VMEM((2, 7, run + 4, CHUNKS, LANES), F32),
        ],
    )(wide, before, after, win, wout, once, twice, ridge, slope, colour_x, clear_x)
    halves = [(kept, swap(sent, "bx", 1))]
    ray = pltpu.VMEM((half, LANES, LANES), F32)
    kept, sent, kept_y, sent_y = call(
        functools.partial(last_kernel, counts, steps),
        "last",
        parts(later) + [parts_y] * 2,
        12,
        [
            image(later),
            ray,
            ray,
            pltpu.VMEM((2, LANES, LANES), F32),
            pltpu.VMEM((2, 2, layers, LANES), F32),
        ],
    )(win, wout, twice, ridge, slope, *fields, colour_ends, clear_ends, colour_y, clear_y)
    halves += [(kept, swap(sent, "bx", 1))]

    level, many = 1, count_y // 2
    while many:
        received = swap(sent_y, "by", level)
        merge = functools.partial(merge_kernel, level.bit_length())
        if many > 1:
            half_parts = sds(many // 2, 2, 2, share_y, LANES)
            kept_y, sent_y = call(merge, "merge", [half_parts] * 2, 2)(kept_y, received)
        else:
            view_y = call(merge, "merge", sds(2, 2, share_y, LANES), 2)(kept_y, received)
        level, many = 2 * level, many // 2
    many = count_x // 2
    piece = sds(2, run, share, LANES)
    operands = [*halves[0], *halves[1], received]
    pieces = list(call(merge_x_kernel, "merge_x", [piece] * many, len(operands))(*operands))
    for t in range(1, many):
        pairs = [(i, (i + 2 * t) % count_x) for i in range(count_x)]
        pieces[t] = lax.ppermute(pieces[t], "bx", pairs)
    view_x = call(fold_x_kernel, "fold_x", sds(2, bands, share, local_y), many)(*pieces)
    view_y = view_y.reshape(2, 2, share_y, half, bands)
    view_y = jnp.transpose(view_y, (0, 4, 2, 1, 3)).reshape(2, bands, share_y, local_x)
    return (view_x, view_y)


def solution(mesh):
    return jax.shard_map(
        body,
        mesh=mesh,
        in_specs=(P(None, "bx", "by"), P(), P()),
        out_specs=(P(None, None, "bx", "by"), P(None, None, "by", "bx")),
        check_vma=False,
    )
```

```python
import functools

import jax
import jax.numpy as jnp
from jax import lax
from jax.experimental import pallas as pl
from jax.experimental.pallas import tpu as pltpu
from jax.sharding import PartitionSpec as P

F32 = jnp.float32
BF16 = jnp.bfloat16
LOG2E = 1.4426950408889634
SUB = 8
LANES = 128
CHUNKS = 16
REACH = 3
VMEM = pl.BlockSpec(memory_space=pltpu.VMEM)
PARAMS = pltpu.CompilerParams(vmem_limit_bytes=36 * 1024 * 1024)


def call(kernel, name, outs, count, scratch=()):
    return pl.pallas_call(
        kernel,
        out_shape=outs,
        in_specs=[VMEM] * count,
        out_specs=jax.tree.map(lambda _: VMEM, outs),
        scratch_shapes=scratch,
        compiler_params=PARAMS,
        name=name,
    )


def rows_of(width):
    return -(-(width + 2 * REACH) // 16) * 16


def iota(shape, dim):
    return lax.broadcasted_iota(jnp.int32, shape, dim)


def one_hot(mask):
    return jnp.where(mask, 1.0, 0.0).astype(BF16)


def spread(weights, left, right, mask):
    inner = lax.dot_general(
        left, weights, (((1,), (1,)), ((), ())), preferred_element_type=F32
    ).astype(BF16)
    return jnp.where(mask, jnp.dot(inner, right, preferred_element_type=F32), 0.0)


def inside_grid(axis, peers, before, after):
    at = lax.axis_index(axis)
    return jnp.where(at == 0, 0.0, before), jnp.where(at == peers - 1, 0.0, after)


def turn_kernel(field_ref, turned_ref, first_ref, last_ref):
    layers, length, width = field_ref.shape
    half = length // 2
    for k in range(half):
        turned = jnp.concatenate([field_ref[:, k, :], field_ref[:, k + half, :]], axis=0).T
        turned_ref[k, REACH : REACH + width] = turned
        for j in range(REACH):
            first_ref[j, k : k + 1] = turned[j : j + 1]
            last_ref[j, k : k + 1] = turned[width - REACH + j : width - REACH + j + 1]


def spread_weights(in_ref, out_ref, win_ref, wout_ref):
    units, feats = in_ref.shape
    channels = out_ref.shape[0]
    bands = channels // 2
    rows, cols = feats * CHUNKS, units * CHUNKS
    left = one_hot(iota((rows, feats), 0) // CHUNKS == iota((rows, feats), 1))
    right = one_hot(iota((units, cols), 1) // CHUNKS == iota((units, cols), 0))
    mask = iota((rows, cols), 0) % CHUNKS == iota((rows, cols), 1) % CHUNKS
    win_ref[...] = (0.5 * spread(in_ref[...], left, right, mask)).astype(BF16)
    rows, cols = cols, channels * CHUNKS
    left = one_hot(iota((rows, units), 0) // CHUNKS == iota((rows, units), 1))
    at = iota((channels, cols), 1)
    right = one_hot((at // LANES) * bands + at % bands == iota((channels, cols), 0))
    mask = iota((rows, cols), 0) % CHUNKS == (iota((rows, cols), 1) % LANES) // bands
    wout_ref[...] = spread(out_ref[...], left, right, mask).astype(BF16)


def sides_kernel(
    width, count_y, turned_ref, before_ref, after_ref, wide_ref, first_ref, last_ref
):
    half, rows, _ = turned_ref.shape
    layers = LANES // 2
    part = rows // 2
    front = iota((part, LANES), 1) < layers
    befores, afters = inside_grid("by", count_y, before_ref[...], after_ref[...])
    for k in range(half):
        wide_ref[k, REACH : REACH + width] = turned_ref[k, REACH : REACH + width]
        for j in range(REACH):
            at = REACH + width + j
            wide_ref[k, j : j + 1] = befores[j, k : k + 1]
            wide_ref[k, at : at + 1] = afters[j, k : k + 1]
        wide_ref[k, 2 * REACH + width :] = jnp.zeros((rows - 2 * REACH - width, LANES), F32)
    for j in range(REACH):
        top, low = wide_ref[j, :part], wide_ref[j, part:]
        first_ref[j] = jnp.where(front, top, pltpu.roll(low, layers, axis=1))
        k = half - REACH + j
        top, low = wide_ref[k, :part], wide_ref[k, part:]
        last_ref[j] = jnp.where(front, pltpu.roll(top, layers, axis=1), low)


class Stencil:
    def __init__(self, run, counts):
        self.run = run
        self.layers = layers = LANES // 2
        self.shape = (CHUNKS, LANES)
        lane, chunk = iota(self.shape, 1), iota(self.shape, 0)
        z = lane % layers
        self.near = (z > 0).astype(F32)
        self.far = (z < layers - 1).astype(F32)
        at_x, at_y = lax.axis_index("bx"), lax.axis_index("by")
        count_x, count_y = counts
        self.x_low = jnp.where((lane < layers) & (at_x == 0), 0.0, 1.0)
        self.x_high = jnp.where((lane >= layers) & (at_x == count_x - 1), 0.0, 1.0)
        self.y_low = jnp.where((chunk == 0) & (at_y == 0), 0.0, 1.0)
        self.y_high = jnp.where((chunk == CHUNKS - 1) & (at_y == count_y - 1), 0.0, 1.0)

    def z_sum(self, value):
        return roll(value, 1) * self.near + roll(value, -1) * self.far

    def inside(self, value, y, edge):
        if edge is not None:
            value = value * edge
        if y < 0:
            value = value * self.y_low
        if y >= self.run:
            value = value * self.y_high
        return value

    def smooth(self, centre, others):
        total = self.z_sum(centre)
        for other in others:
            total = total + other
        return 0.4 * centre + 0.1 * total

    def raw(self, ref, k, y):
        return ref[k, pl.ds(y + REACH, CHUNKS, stride=self.run), :]

    def once(self, raw, k, out, at, edge=None):
        column = [self.raw(raw, k, y) for y in range(-3, self.run + 3)]
        for i in range(1, len(column) - 1):
            y = i - 3
            sides = [self.raw(raw, k - 1, y), self.raw(raw, k + 1, y)]
            value = self.smooth(column[i], [column[i - 1], column[i + 1]] + sides)
            out[at, i - 1] = self.inside(value, y, edge)

    def twice(self, once, k, out, ridge, slope, at, edge=None):
        column = [once[k, i] for i in range(self.run + 4)]
        for i in range(1, len(column) - 1):
            sides = [once[k - 1, i], once[k + 1, i]]
            value = self.smooth(column[i], [column[i - 1], column[i + 1]] + sides)
            value = self.inside(value, i - 2, edge)
            out[at, i - 1] = value
            below, above = roll(value, 1) * self.near, roll(value, -1) * self.far
            ridge[at, i - 1] = 2.0 * value + (below + above)
            slope[at, i - 1] = above - below

    def features(self, twice, ridge, slope, k, y):
        p = lambda a, b: twice[k + a, y + 1 + b]
        r = lambda a, b: ridge[k + a, y + 1 + b]
        centre = p(0, 0)
        main, cross = p(1, 1) - p(-1, -1), p(1, -1) - p(-1, 1)
        third = 1.0 / 3.0
        gx = (main + cross + (r(1, 0) - r(-1, 0))) * third
        gy = (main - cross + (r(0, 1) - r(0, -1))) * third
        d = lambda a, b: slope[k + a, y + 1 + b]
        gz = (2.0 * d(0, 0) + ((d(1, 0) + d(-1, 0)) + (d(0, 1) + d(0, -1)))) * third
        square = 1.0 + gx * gx + gy * gy + gz * gz
        m = square * lax.rsqrt(square)
        parts = [centre, gx, gy, gz, m, centre * m, centre * centre]
        packed = [part.astype(BF16) for part in parts] + [jnp.ones(self.shape, BF16)]
        return jnp.concatenate(packed, axis=0).T


def roll(value, shift):
    return pltpu.roll(value, shift % LANES, axis=1)


def network(tiles, win_ref, wout_ref, step):
    cells = jnp.concatenate(tiles, axis=0)
    half_v = jnp.dot(cells, win_ref[...], preferred_element_type=F32)
    hidden = (half_v + half_v * jnp.tanh(half_v)).astype(BF16)
    v = jnp.dot(hidden, wout_ref[...], preferred_element_type=F32)
    soft = jnp.maximum(v, jnp.log(1.0 + jnp.exp2(jnp.minimum(v * LOG2E, 126.0))))
    return soft[:, :LANES], jnp.exp2(soft[:, LANES:] * (-LOG2E * step))


def clear_of_x(q, ratio):
    if ratio == 1.0:
        return q
    if ratio == 2.0:
        return q * q
    return jnp.exp2(jnp.log(q) * (LOG2E * ratio))


def step_ray(ray, clear, emission):
    colour, light = ray
    later = light * clear
    return colour + (light - later) * emission, later


def middle_kernel(
    counts,
    steps,
    wide_ref,
    in_ref,
    out_ref,
    win_ref,
    wout_ref,
    once_out_ref,
    twice_out_ref,
    ridge_out_ref,
    slope_out_ref,
    cx_ref,
    tx_ref,
    cy_ref,
    ty_ref,
    *refs,
):
    later_refs, (once_ref, twice_ref, ridge_ref, slope_ref) = refs[:3], refs[3:]
    half = wide_ref.shape[0]
    run, ahead = once_ref.shape[1] - 4, cx_ref.shape[0]
    stencil = Stencil(run, counts)
    inner = half - 2 * REACH
    spread_weights(in_ref, out_ref, win_ref, wout_ref)
    for k in range(ahead):
        tx_ref[k] = jnp.ones((LANES, LANES), F32)
        cx_ref[k] = jnp.zeros((LANES, LANES), F32)
    for k in range(inner):
        ty_ref[k] = jnp.ones((LANES, LANES), F32)
        cy_ref[k] = jnp.zeros((LANES, LANES), F32)
    ratio = steps[0] / steps[1]

    def block(x0, y0, many_x, many_y):
        tiles = [
            stencil.features(twice_ref, ridge_ref, slope_ref, x0 + i + 1, y0 + j)
            for j in range(many_y)
            for i in range(many_x)
        ]
        emission, clear = network(tiles, win_ref, wout_ref, steps[1])
        for g in range(LANES // SUB):
            at = pl.ds(g * SUB, SUB)
            rays_y = [(cy_ref[x0 + i, at], ty_ref[x0 + i, at]) for i in range(many_x)]
            for j in range(many_y):
                ray_x = cx_ref[y0 + j, at], tx_ref[y0 + j, at]
                for i in range(many_x):
                    start = (j * many_x + i) * LANES + g * SUB
                    e, q = emission[start : start + SUB], clear[start : start + SUB]
                    rays_y[i] = step_ray(rays_y[i], q, e)
                    ray_x = step_ray(ray_x, clear_of_x(q, ratio), e)
                cx_ref[y0 + j, at], tx_ref[y0 + j, at] = ray_x
            for i in range(many_x):
                cy_ref[x0 + i, at], ty_ref[x0 + i, at] = rays_y[i]

    many_y = 2 if ahead % 2 == 0 else 1
    for k in range(inner + 4):
        stencil.once(wide_ref, k + 1, once_ref, k)
    for k in range(inner + 2):
        stencil.twice(once_ref, k + 1, twice_ref, ridge_ref, slope_ref, k)
    for y0 in range(0, ahead, many_y):
        block(0, y0, inner, many_y)
    for k in range(4):
        once_out_ref[0, k] = once_ref[k]
        once_out_ref[1, k] = once_ref[inner + k]
    fields = (twice_ref, ridge_ref, slope_ref)
    outs = (twice_out_ref, ridge_out_ref, slope_out_ref)
    for out_ref, later_ref, ref in zip(outs, later_refs, fields):
        for k in range(2):
            out_ref[0, k] = ref[k]
            out_ref[1, k] = ref[inner + k]
        later_ref[...] = ref[:, ahead:]


def parts_of(image_ref, kept_ref, sent_ref, mine):
    many, share = kept_ref.shape[0], kept_ref.shape[3]
    for r in range(many):
        for out_ref, bit in ((kept_ref, mine), (sent_ref, 1 - mine)):
            start = pl.multiple_of((2 * r + bit) * share, share)
            out_ref[r] = image_ref[:, :, pl.ds(start, share), :]


def march_planes(stencil, steps, tiles, many_y, weights, rays, middle, image_ref):
    layers = stencil.layers
    ratio = steps[0] / steps[1]
    many_x = len(rays)
    emission, clear = network(tiles, *weights, steps[1])
    images = [[], []]
    for g in range(LANES // SUB):
        at = pl.ds(g * SUB, SUB)
        rays_y = [(cy_ref[at], ty_ref[at]) for cy_ref, ty_ref in rays]
        for j in range(many_y):
            ray_x = jnp.zeros((SUB, LANES), F32), jnp.ones((SUB, LANES), F32)
            for i in range(many_x):
                if i == REACH and middle is not None:
                    colour, light = ray_x
                    colour = colour + light * middle[0][j, at]
                    ray_x = colour, light * middle[1][j, at]
                start = (j * many_x + i) * LANES + g * SUB
                e, q = emission[start : start + SUB], clear[start : start + SUB]
                rays_y[i] = step_ray(rays_y[i], q, e)
                ray_x = step_ray(ray_x, clear_of_x(q, ratio), e)
            images[0].append(ray_x[0])
            images[1].append(ray_x[1])
        for (cy_ref, ty_ref), ray in zip(rays, rays_y):
            cy_ref[at], ty_ref[at] = ray
    for d in range(layers // SUB):
        for j in range(many_y):
            near, far = d * many_y + j, (d + layers // SUB) * many_y + j
            q = images[1][near]
            at = pl.ds(d * SUB, SUB)
            image_ref[0, j, at] = images[0][near] + q * images[0][far]
            image_ref[1, j, at] = q * images[1][far]


def ends_first_kernel(
    counts,
    steps,
    wide_ref,
    before_ref,
    after_ref,
    win_ref,
    wout_ref,
    once_in_ref,
    twice_in_ref,
    ridge_in_ref,
    slope_in_ref,
    cx_ref,
    tx_ref,
    twice_ref,
    ridge_ref,
    slope_ref,
    cy_ref,
    ty_ref,
    kept_ref,
    sent_ref,
    image_ref,
    raw_ref,
    once_ref,
):
    half, rows, _ = wide_ref.shape
    run = once_ref.shape[2] - 4
    layers = LANES // 2
    stencil = Stencil(run, counts)
    part = rows // 2
    front = iota((part, LANES), 1) < layers
    at_x = lax.axis_index("bx")
    for j in range(REACH):
        before, after = inside_grid("bx", counts[0], before_ref[j], after_ref[j])
        halo, own = before, wide_ref[half - REACH + j]
        raw_ref[0, j, :part] = jnp.where(front, halo, roll(own[:part], layers))
        raw_ref[0, j, part:] = jnp.where(front, roll(halo, layers), roll(own[part:], layers))
        halo, own = after, wide_ref[j]
        raw_ref[1, 2 + j, :part] = jnp.where(front, roll(own[:part], layers), roll(halo, layers))
        raw_ref[1, 2 + j, part:] = jnp.where(front, roll(own[part:], layers), halo)
    for j in range(2):
        raw_ref[0, REACH + j] = wide_ref[j]
        raw_ref[1, j] = wide_ref[half - 2 + j]
    for k in range(4):
        once_ref[0, 3 + k] = once_in_ref[0, k]
        once_ref[1, k] = once_in_ref[1, k]
    for k in range(2):
        twice_ref[0, 3 + k] = twice_in_ref[0, k]
        twice_ref[1, k] = twice_in_ref[1, k]
        ridge_ref[0, 3 + k] = ridge_in_ref[0, k]
        ridge_ref[1, k] = ridge_in_ref[1, k]
        slope_ref[0, 3 + k] = slope_in_ref[0, k]
        slope_ref[1, k] = slope_in_ref[1, k]
    for side, edge in enumerate((stencil.x_low, stencil.x_high)):
        outside = (0, 1) if side == 0 else (1, 2)
        for k in range(3):
            kept = edge if k in outside else None
            stencil.once(raw_ref.at[side], k + 1, once_ref.at[side], k + 4 * side, kept)
    for side, edge in enumerate((stencil.x_low, stencil.x_high)):
        for k in range(3):
            kept = edge if k == 2 * side else None
            at = k + 2 * side
            outs = [ref.at[side] for ref in (twice_ref, ridge_ref, slope_ref)]
            stencil.twice(once_ref.at[side], at + 1, *outs, at, kept)
    for k in range(2 * REACH):
        ty_ref[k] = jnp.ones((LANES, LANES), F32)
        cy_ref[k] = jnp.zeros((LANES, LANES), F32)
    fields = (twice_ref, ridge_ref, slope_ref)
    ahead = image_ref.shape[1]
    tiles = [
        stencil.features(*[ref.at[side] for ref in fields], k, y)
        for y in range(ahead)
        for side in range(2)
        for k in range(1, REACH + 1)
    ]
    rays = [(cy_ref.at[k], ty_ref.at[k]) for k in range(2 * REACH)]
    march_planes(
        stencil, steps, tiles, ahead, (win_ref, wout_ref), rays, (cx_ref, tx_ref), image_ref
    )
    parts_of(image_ref, kept_ref, sent_ref, at_x & 1)


def last_kernel(counts, steps, *refs):
    win_ref, wout_ref, *refs = refs
    ends, middle, refs = refs[:3], refs[3:6], refs[6:]
    cy_ends_ref, ty_ends_ref, cy_middle_ref, ty_middle_ref = refs[:4]
    kept_ref, sent_ref, kept_y_ref, sent_y_ref = refs[4:8]
    image_ref, cy_ref, ty_ref, rows_ref, columns_ref = refs[8:]
    run = ends[0].shape[2] - 2
    stencil = Stencil(run, counts)
    layers = stencil.layers
    inner = cy_middle_ref.shape[0]
    half = inner + 2 * REACH
    many_y = image_ref.shape[1]
    for old, new in ((cy_ends_ref, cy_ref), (ty_ends_ref, ty_ref)):
        new[:REACH], new[half - REACH :] = old[:REACH], old[REACH:]
    for old, new in ((cy_middle_ref, cy_ref), (ty_middle_ref, ty_ref)):
        new[REACH : half - REACH] = old[...]
    tiles = []
    for j in range(many_y):
        for k in range(half):
            if REACH <= k < half - REACH:
                tiles.append(stencil.features(*middle, k - REACH + 1, j))
            else:
                side, k = (0, k + 1) if k < REACH else (1, k - half + REACH + 1)
                fields = [ref.at[side] for ref in ends]
                tiles.append(stencil.features(*fields, k, run - many_y + j))
    rays = [(cy_ref.at[k], ty_ref.at[k]) for k in range(half)]
    march_planes(stencil, steps, tiles, many_y, (win_ref, wout_ref), rays, None, image_ref)
    parts_of(image_ref, kept_ref, sent_ref, lax.axis_index("bx") & 1)
    for k in range(half):
        image = column_image(cy_ref[k], ty_ref[k])
        for kind in range(2):
            rows_ref[kind, k * SUB : (k + 1) * SUB] = image[kind]
    for kind in range(2):
        turned = rows_ref[kind].T
        for part in range(2):
            columns_ref[kind, part] = turned[part * layers : (part + 1) * layers]
    parts_of(columns_ref, kept_y_ref, sent_y_ref, lax.axis_index("by") & 1)


def column_image(colours, clears):
    colours, clears = colours.T, clears.T
    colour, clear = colours[:SUB], clears[:SUB]
    for c in range(1, CHUNKS):
        at = slice(c * SUB, (c + 1) * SUB)
        colour = colour + clear * colours[at]
        clear = clear * clears[at]
    return colour, clear


def merge_kernel(level, kept_ref, received_ref, *refs):
    me = lax.axis_index("by") >> (level - 1)
    later = (me & 1) == 1
    kept, received = kept_ref[...], received_ref[...]
    front = jnp.where(later, received, kept)
    back = jnp.where(later, kept, received)
    many = kept.shape[0]
    colour = front[:, 0] + front[:, 1] * back[:, 0]
    clear = front[:, 1] * back[:, 1]
    if many == 1:
        refs[0][0] = colour[0]
        refs[0][1] = clear[0]
        return
    out_kept_ref, out_sent_ref = refs
    bit = ((me >> 1) & 1) == 1
    for r in range(many // 2):
        for kind, value in enumerate((colour, clear)):
            even, odd = value[2 * r], value[2 * r + 1]
            out_kept_ref[r, kind] = jnp.where(bit, odd, even)
            out_sent_ref[r, kind] = jnp.where(bit, even, odd)


def merge_x_kernel(*refs):
    many = refs[0].shape[0]
    ins, outs = refs[:4], refs[-many:]
    at = lax.axis_index("bx")
    later = (at & 1) == 1
    first = 0
    for kept_ref, received_ref in (ins[:2], ins[2:]):
        last = first + kept_ref.shape[2]
        for t in range(many):
            r = lax.rem((at >> 1) + t, many)
            kept, received = kept_ref[r], received_ref[r]
            front = jnp.where(later, received, kept)
            back = jnp.where(later, kept, received)
            outs[t][0, first:last] = front[0] + front[1] * back[0]
            outs[t][1, first:last] = front[1] * back[1]
        first = last


def fold_x_kernel(*refs):
    pieces, out_ref = refs[:-1], refs[-1]
    _, run, share, _ = pieces[0].shape
    lane = iota((share, LANES), 1)
    me = lax.axis_index("bx") >> 1
    kinds = [[], []]
    for y in range(run):
        behind = colour, clear = jnp.zeros((share, LANES), F32), jnp.ones((share, LANES), F32)
        for s in reversed(range(len(pieces))):
            start = me == s
            behind = jnp.where(start, colour, behind[0]), jnp.where(start, clear, behind[1])
            colour, clear = jnp.where(start, 0.0, colour), jnp.where(start, 1.0, clear)
            colour = colour + clear * pieces[s][0, y]
            clear = clear * pieces[s][1, y]
        kinds[0].append(colour + clear * behind[0])
        kinds[1].append(clear * behind[1])
    for kind, values in enumerate(kinds):
        for s in (1, 2, 4):
            for i in range(run):
                if not i & s:
                    a, b = values[i], values[i | s]
                    odd = (lane & s) != 0
                    values[i] = jnp.where(odd, pltpu.roll(b, s, axis=1), a)
                    values[i | s] = jnp.where(odd, b, pltpu.roll(a, LANES - s, axis=1))
        for band, value in enumerate(values):
            out_ref[kind, band] = value


def exchange(last, first, axis):
    peers = lax.axis_size(axis)
    up = [(i, (i + 1) % peers) for i in range(peers)]
    down = [(j, i) for i, j in up]
    return lax.ppermute(last, axis, up), lax.ppermute(first, axis, down)


def swap(value, axis, bit):
    return lax.ppermute(value, axis, [(i, i ^ bit) for i in range(lax.axis_size(axis))])


def body(scalar_field, transfer_in, transfer_out):
    layers, local_x, local_y = scalar_field.shape
    units, feats = transfer_in.shape
    channels = transfer_out.shape[0]
    bands = channels // 2
    count_x, count_y = lax.axis_size("bx"), lax.axis_size("by")
    steps = (2.0 / (local_x * count_x), 2.0 / (local_y * count_y))
    half, run, rows = local_x // 2, local_y // CHUNKS, rows_of(local_y)
    sds = lambda *shape: jax.ShapeDtypeStruct(shape, F32)
    weights = [
        jax.ShapeDtypeStruct((feats * CHUNKS, units * CHUNKS), BF16),
        jax.ShapeDtypeStruct((units * CHUNKS, channels * CHUNKS), BF16),
    ]

    edge = sds(REACH, half, LANES)
    turned, first, last = call(turn_kernel, "turn", [sds(half, rows, LANES), edge, edge], 1)(
        scalar_field
    )
    before, after = exchange(last, first, "by")
    edge = sds(REACH, rows // 2, LANES)
    wide, first, last = call(
        functools.partial(sides_kernel, local_y, count_y), "sides", [sds(half, rows, LANES), edge, edge], 3
    )(turned, before, after)
    before, after = exchange(last, first, "bx")
    inner = half - 2 * REACH
    counts = (count_x, count_y)
    plane = lambda *lead: sds(*lead, CHUNKS, LANES)
    ahead = run - run // 4
    later = run - ahead
    win, wout, once, twice, ridge, slope, colour_x, clear_x, colour_y, clear_y, *fields = call(
        functools.partial(middle_kernel, counts, steps),
        "middle",
        weights
        + [plane(2, 4, run + 4)]
        + [plane(2, 2, run + 2)] * 3
        + [sds(ahead, LANES, LANES)] * 2
        + [sds(inner, LANES, LANES)] * 2
        + [plane(inner + 2, later + 2)] * 3,
        3,
        [
            pltpu.VMEM((inner + 4, run + 4, CHUNKS, LANES), F32),
            pltpu.VMEM((inner + 2, run + 2, CHUNKS, LANES), F32),
            pltpu.VMEM((inner + 2, run + 2, CHUNKS, LANES), F32),
            pltpu.VMEM((inner + 2, run + 2, CHUNKS, LANES), F32),
        ],
    )(wide, transfer_in, transfer_out)
    share = layers // count_x
    share_y = layers // count_y
    parts = lambda many: [sds(count_x // 2, 2, many, share, LANES)] * 2
    parts_y = sds(count_y // 2, 2, 2, share_y, LANES)
    image = lambda many: pltpu.VMEM((2, many, layers, LANES), F32)
    field = plane(2, 5, run + 2)
    twice, ridge, slope, colour_ends, clear_ends, kept, sent = call(
        functools.partial(ends_first_kernel, counts, steps),
        "ends_first",
        [field] * 3 + [sds(2 * REACH, LANES, LANES)] * 2 + parts(ahead),
        11,
        [
            image(ahead),
            pltpu.VMEM((2, 5, rows, LANES), F32),
            pltpu.VMEM((2, 7, run + 4, CHUNKS, LANES), F32),
        ],
    )(wide, before, after, win, wout, once, twice, ridge, slope, colour_x, clear_x)
    halves = [(kept, swap(sent, "bx", 1))]
    ray = pltpu.VMEM((half, LANES, LANES), F32)
    kept, sent, kept_y, sent_y = call(
        functools.partial(last_kernel, counts, steps),
        "last",
        parts(later) + [parts_y] * 2,
        12,
        [
            image(later),
            ray,
            ray,
            pltpu.VMEM((2, LANES, LANES), F32),
            pltpu.VMEM((2, 2, layers, LANES), F32),
        ],
    )(win, wout, twice, ridge, slope, *fields, colour_ends, clear_ends, colour_y, clear_y)
    halves += [(kept, swap(sent, "bx", 1))]

    level, many = 1, count_y // 2
    while many:
        received = swap(sent_y, "by", level)
        merge = functools.partial(merge_kernel, level.bit_length())
        if many > 1:
            half_parts = sds(many // 2, 2, 2, share_y, LANES)
            kept_y, sent_y = call(merge, "merge", [half_parts] * 2, 2)(kept_y, received)
        else:
            view_y = call(merge, "merge", sds(2, 2, share_y, LANES), 2)(kept_y, received)
        level, many = 2 * level, many // 2
    many = count_x // 2
    piece = sds(2, run, share, LANES)
    operands = [*halves[0], *halves[1], sent_y]
    pieces = list(call(merge_x_kernel, "merge_x", [piece] * many, len(operands))(*operands))
    for t in range(1, many):
        pairs = [(i, (i + 2 * t) % count_x) for i in range(count_x)]
        pieces[t] = lax.ppermute(pieces[t], "bx", pairs)
    view_x = call(fold_x_kernel, "fold_x", sds(2, bands, share, local_y), many)(*pieces)
    view_y = view_y.reshape(2, 2, share_y, half, bands)
    view_y = jnp.transpose(view_y, (0, 4, 2, 1, 3)).reshape(2, bands, share_y, local_x)
    return (view_x, view_y)


def solution(mesh):
    return jax.shard_map(
        body,
        mesh=mesh,
        in_specs=(P(None, "bx", "by"), P(), P()),
        out_specs=(P(None, None, "bx", "by"), P(None, None, "by", "bx")),
        check_vma=False,
    )
```
